32 devices in a mesh: cols: 4 (over x, core), rows: 8 (over z, y).
Axes of the slice: x: 2, y: 2, z: 4, core: 2. Of those that a mesh axis runs over, the one named last changes fastest.
Arguments:
- snapshots: float32 [8192, 512], P('rows', 'cols')
- plan: int32 [3], replicated, may hold values from 1 to 3, as said below
Outputs:
- rotated: float32 [8192, 512], P('rows', 'cols')
The draws below stay inside these ranges and needn't reach their ends.
Inputs may be any that keep to these rules, and one draw needn't show every extreme that they name: `plan`: the 3 masks are distinct; among them are 3 and 2.
All inputs are finite; a program needn't handle non-finite values.
Results may differ from the reference program's by a relative error of at most 0.0003.
Values sent between devices are 32-bit elements; how exact they have to be, the bound alone decides.
A program may use at most 64 MiB of HBM per device.

```python
import jax
import jax.numpy as jnp
from jax import lax

BC = 128
ITERS = 3
NSI = 5
NBLK = 4
COLS = 512
M = 8192


def draw_snapshots(key, part):
    key_noise = jax.random.fold_in(key, 11)
    key_shared = jax.random.fold_in(key, 12)
    key_weight = jax.random.fold_in(key, 13)
    shared = jax.random.normal(key_shared, (M, 1), jnp.float32)
    weights = jax.random.uniform(key_weight, (1, COLS), jnp.float32, 0.5, 1.5)
    noise = jax.random.normal(key_noise, (M, COLS), jnp.float32)
    return noise + 0.3 * shared * weights


def draw_plan(key, part):
    key_perm = jax.random.fold_in(key, 21)
    key_order = jax.random.fold_in(key, 22)
    values = jnp.arange(1, NBLK, dtype=jnp.int32)
    scores = jax.random.permutation(key_perm, jnp.arange(NBLK - 1, dtype=jnp.int32))
    special = jnp.logical_or(values == NBLK - 1, values == NBLK // 2)
    scores = scores + jnp.where(special, NBLK, 0).astype(jnp.int32)
    top_scores, top_index = lax_top(scores)
    chosen = values[top_index]
    shuffle = jax.random.permutation(key_order, jnp.arange(ITERS, dtype=jnp.int32))
    return chosen[shuffle].astype(jnp.int32)


def lax_top(scores):
    return jax.lax.top_k(scores, ITERS)


def setup_inputs(seed: int = 0) -> dict:
    key_of = jax.random.split(jax.random.key(seed), 3)
    return {
        "snapshots": draw_snapshots(jax.random.fold_in(key_of[2], 71), 0),
        "plan": draw_plan(jax.random.fold_in(key_of[2], 71), 0),
    }


def rotation(gram, sign):
    half = gram.shape[0] // 2
    diag = jnp.diagonal(gram)
    cross = gram[:half, half:] / jnp.sqrt(jnp.outer(diag[:half] + 1e-06, diag[half:] + 1e-06))
    gen = sign * cross / jnp.sqrt(1.0 + jnp.sum(cross * cross))
    zero = jnp.zeros((half, half), jnp.float32)
    top = jnp.concatenate([zero, -gen], axis=1)
    bottom = jnp.concatenate([gen.T, zero], axis=1)
    eye = jnp.eye(2 * half, dtype=jnp.float32)
    ymat = (eye + jnp.concatenate([top, bottom], axis=0)) / jnp.sqrt(jnp.float32(2.0))
    for index in range(NSI):
        inner = jnp.dot(ymat.T, ymat, precision=lax.Precision.HIGHEST)
        ymat = 1.5 * ymat - 0.5 * jnp.dot(ymat, inner, precision=lax.Precision.HIGHEST)
    return ymat

def reference(snapshots, plan):
    blocks = snapshots.reshape(M, NBLK, BC)
    labels = jnp.arange(NBLK, dtype=jnp.int32)
    hi = lax.Precision.HIGHEST
    for step in range(ITERS):
        partner = jnp.bitwise_xor(labels, plan[step])
        sign = jnp.where(labels < partner, 1.0, -1.0).astype(jnp.float32)
        other = blocks[:, partner, :]
        own_own = jnp.einsum('mbi,mbj->bij', blocks, blocks, precision=hi)
        own_other = jnp.einsum('mbi,mbj->bij', blocks, other, precision=hi)
        other_own = jnp.einsum('mbi,mbj->bij', other, blocks, precision=hi)
        other_other = own_own[partner]
        gram = jnp.concatenate([jnp.concatenate([own_own, own_other], axis=2), jnp.concatenate([other_own, other_other], axis=2)], axis=1)
        rot = jax.vmap(rotation)(gram, sign)
        blocks = jnp.einsum('mbi,bij->mbj', blocks, rot[:, :BC, :BC], precision=hi) + jnp.einsum('mbi,bij->mbj', other, rot[:, BC:, :BC], precision=hi)
    return blocks.reshape(M, COLS)
```

```python
import functools

import jax
import jax.numpy as jnp
from jax import lax
from jax.experimental import pallas as pl
from jax.experimental.pallas import tpu as pltpu
from jax.sharding import PartitionSpec as P

NSI = 5
EPS = 1e-6
VMEM = pl.BlockSpec(memory_space=pltpu.VMEM)
MESH = pl.DeviceIdType.MESH
SMEM = pl.BlockSpec(memory_space=pltpu.SMEM)


def split(x):
    high = x.astype(jnp.bfloat16)
    return high, (x - high.astype(jnp.float32)).astype(jnp.bfloat16)


def dots(a, b, ca=1, cb=0):
    def one(x, y):
        return lax.dot_general(
            x, y, (((ca,), (cb,)), ((), ())), preferred_element_type=jnp.float32
        )

    return one(a[0], b[0]) + (one(a[0], b[1]) + one(a[1], b[0]))


def dot(a, b, ca=1, cb=0):
    return dots(split(a), split(b), ca, cb)


def columns(gens):
    width = gens[0].shape[0]
    row = lax.broadcasted_iota(jnp.int32, (width, width), 0)
    col = lax.broadcasted_iota(jnp.int32, (width, width), 1)
    eye = jnp.where(row == col, 1.0, 0.0).astype(jnp.float32)
    parts = [split(g) for g in gens]
    zs = [0.5 * (eye + dots(p, p, 1, 1)) for p in parts]
    qs = None
    for index in range(NSI):
        ts = [1.5 * eye - 0.5 * z for z in zs]
        tsp = [split(t) for t in ts]
        if qs is None:
            qs = [t * (0.5**0.5) for t in ts]
        else:
            qs = [dots(split(q), t) for q, t in zip(qs, tsp)]
        if index < NSI - 1:
            squares = [dots(t, t) for t in tsp]
            zs = [dot(z, s) for z, s in zip(zs, squares)]
    return [(q, dots(p, split(q), 0, 0)) for q, p in zip(qs, parts)]


def generator(cross, own, other, sign):
    width = cross.shape[0]
    row = lax.broadcasted_iota(jnp.int32, (width, width), 0)
    col = lax.broadcasted_iota(jnp.int32, (width, width), 1)
    diag = row == col
    dc = jnp.sum(jnp.where(diag, own, 0.0), axis=1, keepdims=True)
    dp = jnp.sum(jnp.where(diag, other, 0.0), axis=0, keepdims=True)
    dc = jnp.maximum(dc, 0.0) + EPS
    dp = jnp.maximum(dp, 0.0) + EPS
    cross = cross * (lax.rsqrt(dc) * lax.rsqrt(dp))
    total = jnp.sum(jnp.sum(cross * cross, axis=1, keepdims=True), axis=0, keepdims=True)
    return cross * (sign * lax.rsqrt(1.0 + total))


def rotate(nb, plan_ref, label, gram_ref, all_ref, out_ref):
    width = out_ref.shape[1]
    masks = [plan_ref[s] for s in range(3)]
    labels = []
    for slot in range(8):
        block = label
        for bit in range(3):
            if slot >> bit & 1:
                block = jnp.bitwise_xor(block, masks[bit])
        labels.append(block)

    def sign(i, j):
        return jnp.where(labels[i] < labels[j], 1.0, -1.0).astype(jnp.float32)

    loaded = {}

    def gram(i, j):
        if (i, j) not in loaded:
            loaded[i, j] = gram_ref[labels[j], labels[i]]
        return loaded[i, j]

    def stack(parts, axis):
        return jnp.concatenate(parts, axis=axis)

    outs = (0, 2, 4, 6)
    gens = [generator(gram(i, i + 1), gram(i, i), gram(i + 1, i + 1), sign(i, i + 1)) for i in outs]
    first = columns(gens)
    col = {i: split(stack(c, 0)) for i, c in zip(outs, first)}
    after = {}
    for i in outs:
        for j in outs:
            if j < i:
                continue
            wide = stack(
                [stack([gram(i + p, j), gram(i + p, j + 1)], 1) for p in (0, 1)], 0
            )
            half = dots(split(wide), col[j])
            after[i, j] = dots(col[i], split(half), 0, 0)

    gens = [generator(after[i, i + 2], after[i, i], after[i + 2, i + 2], sign(i, i + 2)) for i in (0, 4)]
    second = columns(gens)
    c0, c4 = [split(stack(c, 0)) for c in second]

    def block(i, j):
        return stack(
            [
                stack([after[i, j], after[i, j + 2]], 1),
                stack([after[i + 2, j] if i + 2 <= j else after[j, i + 2].T, after[i + 2, j + 2]], 1),
            ],
            0,
        )

    def update(ci, mat, cj):
        return dots(ci, split(dots(split(mat), cj)), 0, 0)

    g00 = update(c0, block(0, 0), c0)
    g04 = update(c0, block(0, 4), c4)
    g44 = update(c4, block(4, 4), c4)
    gens = [generator(g04, g00, g44, sign(0, 4))]
    (a, b), = columns(gens)
    top = dots(c0, split(a))
    bottom = dots(c4, split(b))
    weight = {0: top[:width], 2: top[width:], 4: bottom[:width], 6: bottom[width:]}
    coef = {}
    for i in outs:
        both = dots(col[i], split(weight[i]))
        coef[i], coef[i + 1] = both[:width], both[width:]
    coefs = [split(coef[k]) for k in range(8)]
    rows = out_ref.shape[0]
    tile = min(rows, 256)

    for at in range(0, rows, tile):
        total = jnp.zeros((tile, width), jnp.float32)
        for k in range(len(coefs)):
            total += dots(split(all_ref[labels[k], at : at + tile]), coefs[k])
        out_ref[at : at + tile, :] = total


def cat(parts, axis):
    return jnp.concatenate(parts, axis=axis)


def one(a, b, cb=0):
    return lax.dot_general(
        a, b, (((1,), (cb,)), ((), ())), preferred_element_type=jnp.float32
    )


def wide(a, b, cb=0):
    return one(cat([a[0], a[1], a[0]], 1), cat([b[0], b[0], b[1]], cb), cb)


def eyes(width):
    row = lax.broadcasted_iota(jnp.int32, (width, width), 0)
    col = lax.broadcasted_iota(jnp.int32, (width, width), 1)
    return row == col


def normal(cross, own, other, sign):
    diag = eyes(cross.shape[0])
    dc = jnp.sum(jnp.where(diag, own, 0.0), axis=1, keepdims=True)
    dp = jnp.sum(jnp.where(diag, other, 0.0), axis=0, keepdims=True)
    dc = jnp.maximum(dc, 0.0) + EPS
    dp = jnp.maximum(dp, 0.0) + EPS
    cross = cross * (lax.rsqrt(dc) * lax.rsqrt(dp))
    total = jnp.sum(jnp.sum(cross * cross, axis=0, keepdims=True), axis=1, keepdims=True)
    return cross, sign * lax.rsqrt(1.0 + total)


def rows_of_rotations(pairs):
    width = pairs[0][0].shape[0]
    eye = jnp.where(eyes(width), 1.0, 0.0).astype(jnp.float32)
    parts = [split(c) for c, _ in pairs]
    squares = [wide(p, p, 1) for p in parts]
    es = [0.5 * eye - (0.5 * a * a) * s for (_, a), s in zip(pairs, squares)]
    gs = [a * c for c, a in pairs]
    ep = [split(e) for e in es]
    boths = [wide(p, [cat([x, y], 1) for x, y in zip(p, split(g))]) for p, g in zip(ep, gs)]
    ys = [
        (0.5**0.5) * cat([eye + 0.5 * e, g + 0.5 * b[:, width:]], 1)
        for e, g, b in zip(es, gs, boths)
    ]
    fs = [b[:, :width] for b in boths]
    es = [0.75 * f + 0.25 * wide(split(f), p) for f, p in zip(fs, ep)]
    ep = [split(e) for e in es]
    boths = [wide(p, [cat([x, z], 1) for x, z in zip(p, split(y))]) for p, y in zip(ep, ys)]
    ys = [y + 0.5 * b[:, width:] for y, b in zip(ys, boths)]
    fs = [b[:, :width] for b in boths]
    es = [0.75 * f + 0.25 * one(f.astype(jnp.bfloat16), p[0]) for f, p in zip(fs, ep)]
    ep = [split(e) for e in es]
    fs = [one(p[0], p[0]) for p in ep]
    ys = [y + 0.5 * wide(p, split(y)) for y, p in zip(ys, ep)]
    es = [0.75 * f + 0.25 * one(f.astype(jnp.bfloat16), p[0]) for f, p in zip(fs, ep)]
    eh = [e.astype(jnp.bfloat16) for e in es]
    fs = [one(h, h) for h in eh]
    ys = [y + 0.5 * one(h, y.astype(jnp.bfloat16)) for y, h in zip(ys, eh)]
    last = [
        (0.5 * (0.75 * f + 0.25 * one(f.astype(jnp.bfloat16), h))).astype(jnp.bfloat16)
        for f, h in zip(fs, eh)
    ]
    return ys, last


def finish(x, last):
    return x + one(last, x.astype(jnp.bfloat16))


def rotate4(plan_ref, label, gram_ref, all_ref, out_ref):
    width = out_ref.shape[1]
    masks = [plan_ref[s] for s in range(2)]
    labels = [label, jnp.bitwise_xor(label, masks[0]), jnp.bitwise_xor(label, masks[1])]
    labels.append(jnp.bitwise_xor(labels[1], masks[1]))

    def sign(i, j):
        return jnp.where(labels[i] < labels[j], 1.0, -1.0).astype(jnp.float32)

    def grid(blocks):
        return cat([cat(line, 1) for line in blocks], 0)

    first = [[gram_ref[labels[j], labels[i]] for j in range(4)] for i in range(4)]
    pairs = [normal(first[i][i ^ 1], first[i][i], first[i ^ 1][i ^ 1], sign(i, i ^ 1)) for i in range(4)]
    ys, last = rows_of_rotations(pairs)
    ys = [cat([y[:, width:], y[:, :width]], 1) if i % 2 else y for i, y in enumerate(ys)]
    turned = []
    lines = []
    for p in range(2):
        slab = split(grid([first[2 * p], first[2 * p + 1]]))
        top = wide(split(cat(ys[2 * p : 2 * p + 2], 0)), slab)
        top = cat([finish(top[:width], last[2 * p]), finish(top[width:], last[2 * p + 1])], 0)
        lines.append(split(top))
        turned.append(split(cat([finish(ys[2 * p + c], last[2 * p + c]) for c in (0, 1)], 0)))
    after = [[None] * 4 for _ in range(4)]
    for p in range(2):
        for q in range(2):
            cut = slice(2 * q * width, 2 * (q + 1) * width)
            block = wide([x[:, cut] for x in lines[p]], turned[q], 1)
            for i in range(2):
                for j in range(2):
                    at = slice(i * width, (i + 1) * width), slice(j * width, (j + 1) * width)
                    after[2 * p + i][2 * q + j] = block[at]
    own, far = (0, 2), (3, 1)
    pairs = [normal(after[i][j], after[i][i], after[j][j], sign(i, j)) for i, j in (own, far)]
    ys, last = rows_of_rotations(pairs)
    slab = split(grid([[after[i][j] for j in own + far] for i in own]))
    line0 = split(finish(wide(split(ys[0]), slab), last[0]))
    slab = split(grid([[after[i][j] for j in far] for i in far]))
    line3 = split(finish(wide(split(ys[1]), slab), last[1]))
    c0, c3 = [split(finish(y, e)) for y, e in zip(ys, last)]
    g00 = wide([x[:, : 2 * width] for x in line0], c0, 1)
    g03 = wide([x[:, 2 * width :] for x in line0], c3, 1)
    g33 = wide(line3, c3, 1)
    ys, last = rows_of_rotations([normal(g03, g00, g33, sign(0, 3))])

    def row(slot):
        at = slice(slot % 2 * width, (slot % 2 + 1) * width)
        return [x[at] for x in turned[slot // 2]]

    def piece(c, half, slot):
        return wide([x[:, half * width : (half + 1) * width] for x in c], row(slot))

    mixed = split(
        grid([[piece(c0, 0, 0), piece(c0, 1, 2)], [piece(c3, 1, 1), piece(c3, 0, 3)]])
    )
    coef = split(finish(wide(split(ys[0]), mixed), last[0]))
    rows = out_ref.shape[0]
    tile = min(rows, 256)
    for at in range(0, rows, tile):
        line = split(cat([all_ref[labels[k], at : at + tile] for k in range(4)], 1))
        out_ref[at : at + tile, :] = wide(line, coef, 1)


def kernel(nb, nr, plan_ref, own_ref, out_ref, all_ref, gram_ref, part, land, *sems):
    a_send, a_recv, b_send, b_recv, c_send, c_recv, d_send, d_recv = sems
    me, row = lax.axis_index("cols"), lax.axis_index("rows")
    chips = nb // 2
    chip, core = me // 2, lax.rem(me, 2)
    sibling = chip * 2 + (1 - core)
    rows, width = own_ref.shape
    piece = 2 * width // nr
    far = range(1, chips)
    chunks = a_send.shape[2]
    size = rows // chunks

    def ahead(d):
        return lax.rem(chip + d, chips)

    def behind(d):
        return lax.rem(chip + 2 * chips - d, chips)

    def peer(k):
        return lax.rem(row + k, nr)

    barrier = pltpu.get_barrier_semaphore()
    targets = [{"cols": sibling}] + [{"cols": ahead(d) * 2 + core} for d in far]
    targets += [{"rows": peer(k)} for k in range(1, nr)]
    for target in targets:
        pl.semaphore_signal(barrier, inc=1, device_id=target, device_id_type=MESH)
    pl.semaphore_wait(barrier, len(targets))

    started = []

    def start(copy):
        copy.start()
        started.append(copy)

    def copies(ref, source, send, recv, at):
        def direct(d, n):
            return pltpu.make_async_remote_copy(
                source.at[at(0, n)], ref.at[me, at(0, n)], send.at[d, 0, n], recv.at[d, 0, n],
                device_id={"cols": ahead(d) * 2 + core}, device_id_type=MESH,
            )

        def relay(d, n):
            block = behind(d) * 2 + core
            return pltpu.make_async_remote_copy(
                source.at[at(0, n)] if d == 0 else ref.at[block, at(d, n)], ref.at[block, at(d, n)],
                send.at[d, 1, n], recv.at[d, 1, n],
                device_id={"cols": sibling}, device_id_type=MESH,
            )

        return direct, relay

    def group(d, n):
        return pl.ds(behind(d + n) * 2, 2)

    direct, relay = copies(all_ref, own_ref, a_send, a_recv, lambda d, n: pl.ds(n * size, size))
    far_panel, near_panel = copies(gram_ref, gram_ref.at[me], d_send, d_recv, group)

    def multiply(block, ch):
        at = pl.ds(ch * size, size)
        to = pl.ds(pl.multiple_of(block * width, width), width)
        product = dot(all_ref[block, at, :], own_ref[at, :], 0, 0)
        if ch == 0:
            part[to, :] = product
        else:
            part[to, :] += product

    def rows_of(g, r):
        return pl.ds(pl.multiple_of(behind(g) * (2 * width) + r * piece, piece), piece)

    def place(g):
        half = nr // 2
        at = pl.ds(pl.multiple_of(lax.rem(row, half) * piece, piece), piece)
        return gram_ref.at[me, behind(g) * 2 + row // half, at]

    def scatter(g, k):
        return pltpu.make_async_remote_copy(
            part.at[rows_of(g, peer(k))], land.at[g, k - 1],
            b_send.at[g, k - 1], b_recv.at[g, k - 1],
            device_id={"rows": peer(k)}, device_id_type=MESH,
        )

    def spread(g, k):
        return pltpu.make_async_remote_copy(
            place(g), place(g),
            c_send.at[g, k - 1], c_recv.at[g, k - 1],
            device_id={"rows": peer(k)}, device_id_type=MESH,
        )

    def send_group(g):
        for k in range(1, nr):
            start(scatter(g, k))

    def sum_group(g):
        total = part[rows_of(g, row), :]
        for k in range(1, nr):
            scatter(g, k).wait_recv()
            total += land[g, k - 1]
        place(g)[...] = total
        for k in range(1, nr):
            start(spread(g, k))

    def share_group(g):
        for k in range(1, nr):
            spread(g, k).wait_recv()
        for d in far:
            start(far_panel(d, g))
        start(near_panel(0, g))

    for ch in range(chunks):
        for d in far:
            start(direct(d, ch))
    for ch in range(chunks):
        start(relay(0, ch))
    all_ref[me] = own_ref[...]
    for ch in range(chunks):
        multiply(me, ch)
    for ch in range(chunks):
        relay(0, ch).wait_recv()
        multiply(sibling, ch)
    send_group(0)
    for ch in range(chunks + 1):
        for d in far:
            if ch < chunks:
                direct(d, ch).wait_recv()
                start(relay(d, ch))
                multiply(behind(d) * 2 + core, ch)
            if ch > 0:
                relay(d, ch - 1).wait_recv()
                multiply(behind(d) * 2 + 1 - core, ch - 1)
        if ch == chunks - 2:
            sum_group(0)
    for g in far:
        send_group(g)
    share_group(0)
    for g in far:
        sum_group(g)
    for g in far:
        share_group(g)
    for g in range(chips):
        for d in far:
            far_panel(d, g).wait_recv()
            start(near_panel(d, g))
    for g in range(chips):
        for d in range(chips):
            near_panel(d, g).wait_recv()
    if nb == 4:
        rotate4(plan_ref, me, gram_ref, all_ref, out_ref)
    else:
        rotate(nb, plan_ref, me, gram_ref, all_ref, out_ref)
    for copy in started:
        copy.wait_send()


def local(nb, nr, snapshots, plan):
    rows, width = snapshots.shape
    chips = nb // 2
    dma = pltpu.SemaphoreType.DMA
    return pl.pallas_call(
        functools.partial(kernel, nb, nr),
        out_shape=jax.ShapeDtypeStruct((rows, width), jnp.float32),
        in_specs=[SMEM, VMEM],
        out_specs=VMEM,
        scratch_shapes=[
            pltpu.VMEM((nb, rows, width), jnp.float32),
            pltpu.VMEM((nb, nb, width, width), jnp.float32),
            pltpu.VMEM((nb * width, width), jnp.float32),
            pltpu.VMEM((chips, nr - 1, 2 * width // nr, width), jnp.float32),
            dma((chips, 2, 4)), dma((chips, 2, 4)),
            dma((chips, nr - 1)), dma((chips, nr - 1)),
            dma((chips, nr - 1)), dma((chips, nr - 1)),
            dma((chips, 2, chips)), dma((chips, 2, chips)),
        ],
        compiler_params=pltpu.CompilerParams(
            collective_id=0, has_side_effects=True, vmem_limit_bytes=48 * 2**20
        ),
    )(plan, snapshots)


def solution(mesh):
    return jax.shard_map(
        functools.partial(local, mesh.shape["cols"], mesh.shape["rows"]),
        mesh=mesh,
        in_specs=(P("rows", "cols"), P()),
        out_specs=P("rows", "cols"),
        check_vma=False,
    )
```

```python
import functools

import jax
import jax.numpy as jnp
from jax import lax
from jax.experimental import pallas as pl
from jax.experimental.pallas import tpu as pltpu
from jax.sharding import PartitionSpec as P

NSI = 5
EPS = 1e-6
VMEM = pl.BlockSpec(memory_space=pltpu.VMEM)
MESH = pl.DeviceIdType.MESH
SMEM = pl.BlockSpec(memory_space=pltpu.SMEM)


def split(x):
    high = x.astype(jnp.bfloat16)
    return high, (x - high.astype(jnp.float32)).astype(jnp.bfloat16)


def dots(a, b, ca=1, cb=0):
    def one(x, y):
        return lax.dot_general(
            x, y, (((ca,), (cb,)), ((), ())), preferred_element_type=jnp.float32
        )

    return one(a[0], b[0]) + (one(a[0], b[1]) + one(a[1], b[0]))


def dot(a, b, ca=1, cb=0):
    return dots(split(a), split(b), ca, cb)


def columns(gens):
    width = gens[0].shape[0]
    row = lax.broadcasted_iota(jnp.int32, (width, width), 0)
    col = lax.broadcasted_iota(jnp.int32, (width, width), 1)
    eye = jnp.where(row == col, 1.0, 0.0).astype(jnp.float32)
    parts = [split(g) for g in gens]
    zs = [0.5 * (eye + dots(p, p, 1, 1)) for p in parts]
    qs = None
    for index in range(NSI):
        ts = [1.5 * eye - 0.5 * z for z in zs]
        tsp = [split(t) for t in ts]
        if qs is None:
            qs = [t * (0.5**0.5) for t in ts]
        else:
            qs = [dots(split(q), t) for q, t in zip(qs, tsp)]
        if index < NSI - 1:
            squares = [dots(t, t) for t in tsp]
            zs = [dot(z, s) for z, s in zip(zs, squares)]
    return [(q, dots(p, split(q), 0, 0)) for q, p in zip(qs, parts)]


def generator(cross, own, other, sign):
    width = cross.shape[0]
    row = lax.broadcasted_iota(jnp.int32, (width, width), 0)
    col = lax.broadcasted_iota(jnp.int32, (width, width), 1)
    diag = row == col
    dc = jnp.sum(jnp.where(diag, own, 0.0), axis=1, keepdims=True)
    dp = jnp.sum(jnp.where(diag, other, 0.0), axis=0, keepdims=True)
    dc = jnp.maximum(dc, 0.0) + EPS
    dp = jnp.maximum(dp, 0.0) + EPS
    cross = cross * (lax.rsqrt(dc) * lax.rsqrt(dp))
    total = jnp.sum(jnp.sum(cross * cross, axis=1, keepdims=True), axis=0, keepdims=True)
    return cross * (sign * lax.rsqrt(1.0 + total))


def rotate(nb, plan_ref, label, gram_ref, all_ref, out_ref):
    width = out_ref.shape[1]
    masks = [plan_ref[s] for s in range(3)]
    labels = []
    for slot in range(8):
        block = label
        for bit in range(3):
            if slot >> bit & 1:
                block = jnp.bitwise_xor(block, masks[bit])
        labels.append(block)

    def sign(i, j):
        return jnp.where(labels[i] < labels[j], 1.0, -1.0).astype(jnp.float32)

    loaded = {}

    def gram(i, j):
        if (i, j) not in loaded:
            loaded[i, j] = gram_ref[labels[j], labels[i]]
        return loaded[i, j]

    def stack(parts, axis):
        return jnp.concatenate(parts, axis=axis)

    outs = (0, 2, 4, 6)
    gens = [generator(gram(i, i + 1), gram(i, i), gram(i + 1, i + 1), sign(i, i + 1)) for i in outs]
    first = columns(gens)
    col = {i: split(stack(c, 0)) for i, c in zip(outs, first)}
    after = {}
    for i in outs:
        for j in outs:
            if j < i:
                continue
            wide = stack(
                [stack([gram(i + p, j), gram(i + p, j + 1)], 1) for p in (0, 1)], 0
            )
            half = dots(split(wide), col[j])
            after[i, j] = dots(col[i], split(half), 0, 0)

    gens = [generator(after[i, i + 2], after[i, i], after[i + 2, i + 2], sign(i, i + 2)) for i in (0, 4)]
    second = columns(gens)
    c0, c4 = [split(stack(c, 0)) for c in second]

    def block(i, j):
        return stack(
            [
                stack([after[i, j], after[i, j + 2]], 1),
                stack([after[i + 2, j] if i + 2 <= j else after[j, i + 2].T, after[i + 2, j + 2]], 1),
            ],
            0,
        )

    def update(ci, mat, cj):
        return dots(ci, split(dots(split(mat), cj)), 0, 0)

    g00 = update(c0, block(0, 0), c0)
    g04 = update(c0, block(0, 4), c4)
    g44 = update(c4, block(4, 4), c4)
    gens = [generator(g04, g00, g44, sign(0, 4))]
    (a, b), = columns(gens)
    top = dots(c0, split(a))
    bottom = dots(c4, split(b))
    weight = {0: top[:width], 2: top[width:], 4: bottom[:width], 6: bottom[width:]}
    coef = {}
    for i in outs:
        both = dots(col[i], split(weight[i]))
        coef[i], coef[i + 1] = both[:width], both[width:]
    coefs = [split(coef[k]) for k in range(8)]
    rows = out_ref.shape[0]
    tile = min(rows, 256)

    for at in range(0, rows, tile):
        total = jnp.zeros((tile, width), jnp.float32)
        for k in range(len(coefs)):
            total += dots(split(all_ref[labels[k], at : at + tile]), coefs[k])
        out_ref[at : at + tile, :] = total


def cat(parts, axis):
    return jnp.concatenate(parts, axis=axis)


def one(a, b, cb=0):
    return lax.dot_general(
        a, b, (((1,), (cb,)), ((), ())), preferred_element_type=jnp.float32
    )


def wide(a, b, cb=0):
    return one(cat([a[0], a[1], a[0]], 1), cat([b[0], b[0], b[1]], cb), cb)


def eyes(width):
    row = lax.broadcasted_iota(jnp.int32, (width, width), 0)
    col = lax.broadcasted_iota(jnp.int32, (width, width), 1)
    return row == col


def normal(cross, own, other, sign):
    diag = eyes(cross.shape[0])
    dc = jnp.sum(jnp.where(diag, own, 0.0), axis=1, keepdims=True)
    dp = jnp.sum(jnp.where(diag, other, 0.0), axis=0, keepdims=True)
    dc = jnp.maximum(dc, 0.0) + EPS
    dp = jnp.maximum(dp, 0.0) + EPS
    cross = cross * (lax.rsqrt(dc) * lax.rsqrt(dp))
    total = jnp.sum(jnp.sum(cross * cross, axis=0, keepdims=True), axis=1, keepdims=True)
    return cross, sign * lax.rsqrt(1.0 + total)


def rows_of_rotations(pairs):
    width = pairs[0][0].shape[0]
    eye = jnp.where(eyes(width), 1.0, 0.0).astype(jnp.float32)
    parts = [split(c) for c, _ in pairs]
    squares = [wide(p, p, 1) for p in parts]
    es = [0.5 * eye - (0.5 * a * a) * s for (_, a), s in zip(pairs, squares)]
    gs = [a * c for c, a in pairs]
    ep = [split(e) for e in es]
    boths = [wide(p, [cat([x, y], 1) for x, y in zip(p, split(g))]) for p, g in zip(ep, gs)]
    ys = [
        (0.5**0.5) * cat([eye + 0.5 * e, g + 0.5 * b[:, width:]], 1)
        for e, g, b in zip(es, gs, boths)
    ]
    fs = [b[:, :width] for b in boths]
    es = [0.75 * f + 0.25 * wide(split(f), p) for f, p in zip(fs, ep)]
    ep = [split(e) for e in es]
    boths = [wide(p, [cat([x, z], 1) for x, z in zip(p, split(y))]) for p, y in zip(ep, ys)]
    ys = [y + 0.5 * b[:, width:] for y, b in zip(ys, boths)]
    fs = [b[:, :width] for b in boths]
    es = [0.75 * f + 0.25 * one(f.astype(jnp.bfloat16), p[0]) for f, p in zip(fs, ep)]
    ep = [split(e) for e in es]
    fs = [one(p[0], p[0]) for p in ep]
    ys = [y + 0.5 * wide(p, split(y)) for y, p in zip(ys, ep)]
    es = [0.75 * f + 0.25 * one(f.astype(jnp.bfloat16), p[0]) for f, p in zip(fs, ep)]
    eh = [e.astype(jnp.bfloat16) for e in es]
    fs = [one(h, h) for h in eh]
    ys = [y + 0.5 * one(h, y.astype(jnp.bfloat16)) for y, h in zip(ys, eh)]
    last = [
        (0.5 * (0.75 * f + 0.25 * one(f.astype(jnp.bfloat16), h))).astype(jnp.bfloat16)
        for f, h in zip(fs, eh)
    ]
    return ys, last


def finish(x, last):
    return x + one(last, x.astype(jnp.bfloat16))


def rotate4(plan_ref, label, gram_ref, all_ref, out_ref, relay, ready):
    width = out_ref.shape[1]
    masks = [plan_ref[s] for s in range(2)]
    labels = [label, jnp.bitwise_xor(label, masks[0]), jnp.bitwise_xor(label, masks[1])]
    labels.append(jnp.bitwise_xor(labels[1], masks[1]))

    def sign(i, j):
        return jnp.where(labels[i] < labels[j], 1.0, -1.0).astype(jnp.float32)

    def grid(blocks):
        return cat([cat(line, 1) for line in blocks], 0)

    first = [[gram_ref[labels[j], labels[i]] for j in range(4)] for i in range(4)]
    pairs = [normal(first[i][i ^ 1], first[i][i], first[i ^ 1][i ^ 1], sign(i, i ^ 1)) for i in range(4)]
    ys, last = rows_of_rotations(pairs)
    ys = [cat([y[:, width:], y[:, :width]], 1) if i % 2 else y for i, y in enumerate(ys)]
    turned = []
    lines = []
    for p in range(2):
        slab = split(grid([first[2 * p], first[2 * p + 1]]))
        top = wide(split(cat(ys[2 * p : 2 * p + 2], 0)), slab)
        top = cat([finish(top[:width], last[2 * p]), finish(top[width:], last[2 * p + 1])], 0)
        lines.append(split(top))
        turned.append(split(cat([finish(ys[2 * p + c], last[2 * p + c]) for c in (0, 1)], 0)))
    after = [[None] * 4 for _ in range(4)]
    for p in range(2):
        for q in range(2):
            cut = slice(2 * q * width, 2 * (q + 1) * width)
            block = wide([x[:, cut] for x in lines[p]], turned[q], 1)
            for i in range(2):
                for j in range(2):
                    at = slice(i * width, (i + 1) * width), slice(j * width, (j + 1) * width)
                    after[2 * p + i][2 * q + j] = block[at]
    relay()
    own, far = (0, 2), (3, 1)
    pairs = [normal(after[i][j], after[i][i], after[j][j], sign(i, j)) for i, j in (own, far)]
    ys, last = rows_of_rotations(pairs)
    slab = split(grid([[after[i][j] for j in own + far] for i in own]))
    line0 = split(finish(wide(split(ys[0]), slab), last[0]))
    slab = split(grid([[after[i][j] for j in far] for i in far]))
    line3 = split(finish(wide(split(ys[1]), slab), last[1]))
    c0, c3 = [split(finish(y, e)) for y, e in zip(ys, last)]
    g00 = wide([x[:, : 2 * width] for x in line0], c0, 1)
    g03 = wide([x[:, 2 * width :] for x in line0], c3, 1)
    g33 = wide(line3, c3, 1)
    ys, last = rows_of_rotations([normal(g03, g00, g33, sign(0, 3))])

    def row(slot):
        at = slice(slot % 2 * width, (slot % 2 + 1) * width)
        return [x[at] for x in turned[slot // 2]]

    def piece(c, half, slot):
        return wide([x[:, half * width : (half + 1) * width] for x in c], row(slot))

    mixed = split(
        grid([[piece(c0, 0, 0), piece(c0, 1, 2)], [piece(c3, 1, 1), piece(c3, 0, 3)]])
    )
    coef = split(finish(wide(split(ys[0]), mixed), last[0]))
    ready()
    rows = out_ref.shape[0]
    tile = min(rows, 256)
    for at in range(0, rows, tile):
        line = split(cat([all_ref[labels[k], at : at + tile] for k in range(4)], 1))
        out_ref[at : at + tile, :] = wide(line, coef, 1)


def kernel(nb, nr, plan_ref, own_ref, out_ref, all_ref, gram_ref, part, land, *sems):
    a_send, a_recv, b_send, b_recv, c_send, c_recv, d_send, d_recv = sems
    me, row = lax.axis_index("cols"), lax.axis_index("rows")
    chips = nb // 2
    chip, core = me // 2, lax.rem(me, 2)
    sibling = chip * 2 + (1 - core)
    rows, width = own_ref.shape
    piece = 2 * width // nr
    far = range(1, chips)
    chunks = a_send.shape[2]
    size = rows // chunks

    def ahead(d):
        return lax.rem(chip + d, chips)

    def behind(d):
        return lax.rem(chip + 2 * chips - d, chips)

    def peer(k):
        return lax.rem(row + k, nr)

    barrier = pltpu.get_barrier_semaphore()
    targets = [{"cols": sibling}] + [{"cols": ahead(d) * 2 + core} for d in far]
    targets += [{"rows": peer(k)} for k in range(1, nr)]
    for target in targets:
        pl.semaphore_signal(barrier, inc=1, device_id=target, device_id_type=MESH)
    pl.semaphore_wait(barrier, len(targets))

    started = []

    def start(copy):
        copy.start()
        started.append(copy)

    def copies(ref, source, send, recv, at):
        def direct(d, n):
            return pltpu.make_async_remote_copy(
                source.at[at(0, n)], ref.at[me, at(0, n)], send.at[d, 0, n], recv.at[d, 0, n],
                device_id={"cols": ahead(d) * 2 + core}, device_id_type=MESH,
            )

        def relay(d, n):
            block = behind(d) * 2 + core
            return pltpu.make_async_remote_copy(
                source.at[at(0, n)] if d == 0 else ref.at[block, at(d, n)], ref.at[block, at(d, n)],
                send.at[d, 1, n], recv.at[d, 1, n],
                device_id={"cols": sibling}, device_id_type=MESH,
            )

        return direct, relay

    def group(d, n):
        return pl.ds(behind(d + n) * 2, 2)

    direct, relay = copies(all_ref, own_ref, a_send, a_recv, lambda d, n: pl.ds(n * size, size))
    far_panel, near_panel = copies(gram_ref, gram_ref.at[me], d_send, d_recv, group)

    def multiply(block, ch):
        at = pl.ds(ch * size, size)
        to = pl.ds(pl.multiple_of(block * width, width), width)
        product = dot(all_ref[block, at, :], own_ref[at, :], 0, 0)
        if ch == 0:
            part[to, :] = product
        else:
            part[to, :] += product

    def rows_of(g, r):
        return pl.ds(pl.multiple_of(behind(g) * (2 * width) + r * piece, piece), piece)

    def place(g):
        half = nr // 2
        at = pl.ds(pl.multiple_of(lax.rem(row, half) * piece, piece), piece)
        return gram_ref.at[me, behind(g) * 2 + row // half, at]

    def scatter(g, k):
        return pltpu.make_async_remote_copy(
            part.at[rows_of(g, peer(k))], land.at[g, k - 1],
            b_send.at[g, k - 1], b_recv.at[g, k - 1],
            device_id={"rows": peer(k)}, device_id_type=MESH,
        )

    def spread(g, k):
        return pltpu.make_async_remote_copy(
            place(g), place(g),
            c_send.at[g, k - 1], c_recv.at[g, k - 1],
            device_id={"rows": peer(k)}, device_id_type=MESH,
        )

    def send_group(g):
        for k in range(1, nr):
            start(scatter(g, k))

    def sum_group(g):
        total = part[rows_of(g, row), :]
        for k in range(1, nr):
            scatter(g, k).wait_recv()
            total += land[g, k - 1]
        place(g)[...] = total
        for k in range(1, nr):
            start(spread(g, k))

    def share_group(g):
        for k in range(1, nr):
            spread(g, k).wait_recv()
        for d in far:
            start(far_panel(d, g))
        start(near_panel(0, g))

    for ch in range(chunks):
        for d in far:
            start(direct(d, ch))
    for ch in range(chunks):
        start(relay(0, ch))
    all_ref[me] = own_ref[...]
    for ch in range(chunks):
        multiply(me, ch)
    for ch in range(chunks):
        relay(0, ch).wait_recv()
        multiply(sibling, ch)
    send_group(0)
    for ch in range(chunks + 1):
        for d in far:
            if ch < chunks:
                direct(d, ch).wait_recv()
                start(relay(d, ch))
                multiply(behind(d) * 2 + core, ch)
            if ch > 0:
                relay(d, ch - 1).wait_recv()
                multiply(behind(d) * 2 + 1 - core, ch - 1)
        if ch == chunks - 2:
            sum_group(0)
    for g in far:
        send_group(g)
    share_group(0)
    for g in far:
        sum_group(g)
    for g in far:
        share_group(g)
    for g in range(chips):
        for d in far:
            far_panel(d, g).wait_recv()
            start(near_panel(d, g))
    for g in range(chips):
        for d in range(chips):
            near_panel(d, g).wait_recv()
    rotate(nb, plan_ref, me, gram_ref, all_ref, out_ref)
    for copy in started:
        copy.wait_send()


CHUNKS = 4
LATE = 2


def tall(a, b):
    return lax.dot_general(
        cat([a[0], a[1], a[0]], 0), cat([b[0], b[0], b[1]], 0),
        (((0,), (0,)), ((), ())), preferred_element_type=jnp.float32,
    )


def kernel4(
    nr, plan_ref, own_ref, out_ref, all_ref, gram_ref, flat, cross, stage, early, near, land, *sems
):
    (swap_send, swap_recv, pair_send, pair_recv, relay_send, relay_recv, b_send, b_recv,
     c_send, c_recv, d_send, d_recv, e_send, e_recv, f_send, f_recv) = sems
    me, row = lax.axis_index("cols"), lax.axis_index("rows")
    chip, core = me // 2, lax.rem(me, 2)
    sibling = chip * 2 + 1 - core
    far = (1 - chip) * 2 + core
    away = (1 - chip) * 2 + 1 - core
    rows, width = own_ref.shape
    half = rows // 2
    fine = width // (2 * nr)

    def peer(k):
        return lax.rem(row + k, nr)

    def there(d):
        return chip if d == 0 else 1 - chip

    def remote(source, target, send, recv, **device):
        return pltpu.make_async_remote_copy(
            source, target, send, recv, device_id=device, device_id_type=MESH
        )

    barrier = pltpu.get_barrier_semaphore()
    for d in range(4):
        for k in range(nr):
            if d or k:
                pl.semaphore_signal(
                    barrier, inc=1, device_id_type=MESH,
                    device_id={"cols": lax.rem(me + d, 4), "rows": peer(k)},
                )
    pl.semaphore_wait(barrier, 4 * nr - 1)

    started = []

    def start(copy):
        copy.start()
        started.append(copy)

    sizes = [half // CHUNKS] * CHUNKS + [half // LATE] * LATE
    offsets = [n * (half // CHUNKS) for n in range(CHUNKS)] + [n * (half // LATE) for n in range(LATE)]

    def span(side, n):
        at = side * half + offsets[n]
        return pl.ds(pl.multiple_of(at, 8), sizes[n])

    def swap(n):
        at = span(1 - chip if n < CHUNKS else chip, n)
        return remote(
            own_ref.at[at], all_ref.at[me, at], swap_send.at[n], swap_recv.at[n], cols=far
        )

    def relay(n):
        at = span(chip if n < CHUNKS else 1 - chip, n)
        return remote(
            all_ref.at[far, at], all_ref.at[far, at], relay_send.at[n], relay_recv.at[n],
            cols=sibling,
        )

    def pair(n):
        at = pl.ds(n * half, half)
        return remote(
            own_ref.at[at], all_ref.at[me, at], pair_send.at[n], pair_recv.at[n], cols=sibling
        )

    def scatter(k):
        return remote(
            stage.at[peer(k)], early.at[k - 1], b_send.at[k - 1], b_recv.at[k - 1], rows=peer(k)
        )

    def spread(k):
        return remote(
            near.at[me, row], near.at[me, row], c_send.at[k - 1], c_recv.at[k - 1], rows=peer(k)
        )

    def forward(n):
        block = far if n == 2 else me
        return remote(
            near.at[block], near.at[block], d_send.at[n], d_recv.at[n],
            cols=far if n == 0 else sibling,
        )

    def part(d, k):
        index = there(d) * nr + peer(k)
        return pl.ds(pl.multiple_of(index * fine, fine), fine)

    def side(b):
        return jnp.where(chip == 0, core, b)

    def slot(b):
        return jnp.where(chip == 0, b, core)

    def scatter_cross(b, d, k):
        return remote(
            cross.at[b, part(d, k)], land.at[slot(b), chip, k],
            e_send.at[b, d, k], e_recv.at[slot(b), chip, k],
            cols=there(d) * 2 + side(b), rows=peer(k),
        )

    def arrive_cross(i, source, k):
        return remote(
            cross.at[i, part(0, 0)], land.at[i, source, k],
            e_send.at[i, 0, k], e_recv.at[i, source, k], cols=sibling,
        )

    def spread_cross(d, k):
        at = gram_ref.at[2 + core, pl.ds(0, 2), part(0, 0)]
        return remote(
            at, at, f_send.at[d, k], f_recv.at[d, k], cols=there(d) * 2 + core, rows=peer(k)
        )

    def pass_cross():
        at = gram_ref.at[2 + core, pl.ds(0, 2)]
        return remote(at, at, d_send.at[3], d_recv.at[3], cols=sibling)

    for n in range(CHUNKS):
        start(swap(n))
    for n in range(2):
        start(pair(n))
    all_ref[me] = own_ref[...]

    step = rows // 4
    total = None
    for n in range(4):
        x = split(own_ref[n * step : (n + 1) * step])
        product = tall(x, x)
        total = product if total is None else total + product
    flat[0] = total
    total = None
    for n in range(4):
        if n % 2 == 0:
            pair(n // 2).wait_recv()
        at = pl.ds(n * step, step)
        product = tall(split(all_ref[chip * 2, at]), split(all_ref[chip * 2 + 1, at]))
        total = product if total is None else total + product
    flat[1] = total
    for k in range(nr):
        stage[k, : 2 * fine] = flat[0, 2 * fine * k : 2 * fine * (k + 1)]
        at = pl.multiple_of(core * (width // 2) + k * fine, fine)
        stage[k, 2 * fine :] = flat[1, pl.ds(at, fine)]
    for k in range(1, nr):
        start(scatter(k))

    totals = [None, None]
    for n in range(CHUNKS):
        swap(n).wait_recv()
        at = span(chip, n)
        for b in range(2):
            left = all_ref[jnp.where(chip == 0, b, far), at]
            right = all_ref[jnp.where(chip == 0, far, 2 + b), at]
            product = tall(split(left), split(right))
            totals[b] = product if n == 0 else totals[b] + product
    for b in range(2):
        cross[b] = totals[b]
    for k in range(nr - 1, -1, -1):
        for d in (1, 0):
            for b in range(2):
                if d or k:
                    start(scatter_cross(b, d, k))
    for b in range(2):
        same = side(b) == core

        @pl.when(same)
        def _():
            land[slot(b), chip, 0] = cross[b, part(0, 0)]

        @pl.when(jnp.logical_not(same))
        def _():
            scatter_cross(b, 0, 0).start()

    sums = stage[row]
    for k in range(1, nr):
        scatter(k).wait_recv()
        sums += early[k - 1]
    near[me, row] = sums
    for k in range(1, nr):
        start(spread(k))
    for n in range(CHUNKS):
        start(relay(n))

    for i in range(2):
        mine = jnp.logical_or(chip == 0, core == i)

        @pl.when(jnp.logical_not(mine))
        def _():
            arrive_cross(i, chip, 0).wait_recv()

        arrive_cross(i, 1 - chip, 0).wait_recv()
        for source in range(2):
            for k in range(1, nr):
                arrive_cross(i, source, k).wait_recv()
        sums = land[i, 0, 0]
        for source in range(2):
            for k in range(nr):
                if source or k:
                    sums += land[i, source, k]
        gram_ref[2 + core, i, part(0, 0)] = sums
    for k in range(nr - 1, -1, -1):
        for d in (1, 0):
            if d or k:
                start(spread_cross(d, k))

    for k in range(1, nr):
        spread(k).wait_recv()
    start(forward(0))
    start(forward(1))
    for n in range(CHUNKS, CHUNKS + LATE):
        start(swap(n))
    forward(0).wait_recv()
    start(forward(2))
    forward(1).wait_recv()
    forward(2).wait_recv()
    for block in range(4):
        gram_ref[block, block] = near[block, :, : 2 * fine].reshape(width, width)
    for c in range(2):
        both = [near[2 * c + i, :, 2 * fine :].reshape(width // 2, width) for i in range(2)]
        both = cat(both, 0)
        gram_ref[2 * c + 1, 2 * c] = both
        gram_ref[2 * c, 2 * c + 1] = both.T

    for k in range(nr):
        for d in range(2):
            if d or k:
                spread_cross(d, k).wait_recv()
    start(pass_cross())
    pass_cross().wait_recv()
    for i in range(2):
        for j in range(2):
            gram_ref[i, 2 + j] = gram_ref[2 + j, i].T

    def late():
        for n in range(CHUNKS, CHUNKS + LATE):
            swap(n).wait_recv()
            start(relay(n))

    def ready():
        for n in range(CHUNKS + LATE):
            relay(n).wait_recv()

    rotate4(plan_ref, me, gram_ref, all_ref, out_ref, late, ready)
    for copy in started:
        copy.wait_send()
    for b in range(2):

        @pl.when(jnp.logical_not(side(b) == core))
        def _():
            scatter_cross(b, 0, 0).wait_send()


def local4(nr, snapshots, plan):
    rows, width = snapshots.shape
    fine = width // (2 * nr)
    dma = pltpu.SemaphoreType.DMA
    return pl.pallas_call(
        functools.partial(kernel4, nr),
        out_shape=jax.ShapeDtypeStruct((rows, width), jnp.float32),
        in_specs=[SMEM, VMEM],
        out_specs=VMEM,
        scratch_shapes=[
            pltpu.VMEM((4, rows, width), jnp.float32),
            pltpu.VMEM((4, 4, width, width), jnp.float32),
            pltpu.VMEM((2, width, width), jnp.float32),
            pltpu.VMEM((2, width, width), jnp.float32),
            pltpu.VMEM((nr, 3 * fine, width), jnp.float32),
            pltpu.VMEM((nr - 1, 3 * fine, width), jnp.float32),
            pltpu.VMEM((4, nr, 3 * fine, width), jnp.float32),
            pltpu.VMEM((2, 2, nr, fine, width), jnp.float32),
            dma((CHUNKS + LATE,)), dma((CHUNKS + LATE,)),
            dma((2,)), dma((2,)),
            dma((CHUNKS + LATE,)), dma((CHUNKS + LATE,)),
            dma((nr - 1,)), dma((nr - 1,)),
            dma((nr - 1,)), dma((nr - 1,)),
            dma((4,)), dma((4,)),
            dma((2, 2, nr)), dma((2, 2, nr)),
            dma((2, nr)), dma((2, nr)),
        ],
        compiler_params=pltpu.CompilerParams(
            collective_id=0, has_side_effects=True, vmem_limit_bytes=40 * 2**20
        ),
    )(plan, snapshots)


def local(nb, nr, snapshots, plan):
    rows, width = snapshots.shape
    chips = nb // 2
    dma = pltpu.SemaphoreType.DMA
    return pl.pallas_call(
        functools.partial(kernel, nb, nr),
        out_shape=jax.ShapeDtypeStruct((rows, width), jnp.float32),
        in_specs=[SMEM, VMEM],
        out_specs=VMEM,
        scratch_shapes=[
            pltpu.VMEM((nb, rows, width), jnp.float32),
            pltpu.VMEM((nb, nb, width, width), jnp.float32),
            pltpu.VMEM((nb * width, width), jnp.float32),
            pltpu.VMEM((chips, nr - 1, 2 * width // nr, width), jnp.float32),
            dma((chips, 2, 4)), dma((chips, 2, 4)),
            dma((chips, nr - 1)), dma((chips, nr - 1)),
            dma((chips, nr - 1)), dma((chips, nr - 1)),
            dma((chips, 2, chips)), dma((chips, 2, chips)),
        ],
        compiler_params=pltpu.CompilerParams(
            collective_id=0, has_side_effects=True, vmem_limit_bytes=48 * 2**20
        ),
    )(plan, snapshots)


def solution(mesh):
    nb, nr = mesh.shape["cols"], mesh.shape["rows"]
    body = functools.partial(local4, nr) if nb == 4 else functools.partial(local, nb, nr)
    return jax.shard_map(
        body,
        mesh=mesh,
        in_specs=(P("rows", "cols"), P()),
        out_specs=P("rows", "cols"),
        check_vma=False,
    )
```

```python
import functools

import jax
import jax.numpy as jnp
from jax import lax
from jax.experimental import pallas as pl
from jax.experimental.pallas import tpu as pltpu
from jax.sharding import PartitionSpec as P

NSI = 5
EPS = 1e-6
VMEM = pl.BlockSpec(memory_space=pltpu.VMEM)
MESH = pl.DeviceIdType.MESH
SMEM = pl.BlockSpec(memory_space=pltpu.SMEM)
HBM = pl.BlockSpec(memory_space=pltpu.HBM)


def split(x):
    high = x.astype(jnp.bfloat16)
    return high, (x - high.astype(jnp.float32)).astype(jnp.bfloat16)


def dots(a, b, ca=1, cb=0):
    def one(x, y):
        return lax.dot_general(
            x, y, (((ca,), (cb,)), ((), ())), preferred_element_type=jnp.float32
        )

    return one(a[0], b[0]) + (one(a[0], b[1]) + one(a[1], b[0]))


def dot(a, b, ca=1, cb=0):
    return dots(split(a), split(b), ca, cb)


def columns(gens):
    width = gens[0].shape[0]
    row = lax.broadcasted_iota(jnp.int32, (width, width), 0)
    col = lax.broadcasted_iota(jnp.int32, (width, width), 1)
    eye = jnp.where(row == col, 1.0, 0.0).astype(jnp.float32)
    parts = [split(g) for g in gens]
    zs = [0.5 * (eye + dots(p, p, 1, 1)) for p in parts]
    qs = None
    for index in range(NSI):
        ts = [1.5 * eye - 0.5 * z for z in zs]
        tsp = [split(t) for t in ts]
        if qs is None:
            qs = [t * (0.5**0.5) for t in ts]
        else:
            qs = [dots(split(q), t) for q, t in zip(qs, tsp)]
        if index < NSI - 1:
            squares = [dots(t, t) for t in tsp]
            zs = [dot(z, s) for z, s in zip(zs, squares)]
    return [(q, dots(p, split(q), 0, 0)) for q, p in zip(qs, parts)]


def generator(cross, own, other, sign):
    width = cross.shape[0]
    row = lax.broadcasted_iota(jnp.int32, (width, width), 0)
    col = lax.broadcasted_iota(jnp.int32, (width, width), 1)
    diag = row == col
    dc = jnp.sum(jnp.where(diag, own, 0.0), axis=1, keepdims=True)
    dp = jnp.sum(jnp.where(diag, other, 0.0), axis=0, keepdims=True)
    dc = jnp.maximum(dc, 0.0) + EPS
    dp = jnp.maximum(dp, 0.0) + EPS
    cross = cross * (lax.rsqrt(dc) * lax.rsqrt(dp))
    total = jnp.sum(jnp.sum(cross * cross, axis=1, keepdims=True), axis=0, keepdims=True)
    return cross * (sign * lax.rsqrt(1.0 + total))


def rotate(nb, plan_ref, label, gram_ref, all_ref, out_ref):
    width = out_ref.shape[1]
    masks = [plan_ref[s] for s in range(3)]
    labels = []
    for slot in range(8):
        block = label
        for bit in range(3):
            if slot >> bit & 1:
                block = jnp.bitwise_xor(block, masks[bit])
        labels.append(block)

    def sign(i, j):
        return jnp.where(labels[i] < labels[j], 1.0, -1.0).astype(jnp.float32)

    loaded = {}

    def gram(i, j):
        if (i, j) not in loaded:
            loaded[i, j] = gram_ref[labels[j], labels[i]]
        return loaded[i, j]

    def stack(parts, axis):
        return jnp.concatenate(parts, axis=axis)

    outs = (0, 2, 4, 6)
    gens = [generator(gram(i, i + 1), gram(i, i), gram(i + 1, i + 1), sign(i, i + 1)) for i in outs]
    first = columns(gens)
    col = {i: split(stack(c, 0)) for i, c in zip(outs, first)}
    after = {}
    for i in outs:
        for j in outs:
            if j < i:
                continue
            wide = stack(
                [stack([gram(i + p, j), gram(i + p, j + 1)], 1) for p in (0, 1)], 0
            )
            half = dots(split(wide), col[j])
            after[i, j] = dots(col[i], split(half), 0, 0)

    gens = [generator(after[i, i + 2], after[i, i], after[i + 2, i + 2], sign(i, i + 2)) for i in (0, 4)]
    second = columns(gens)
    c0, c4 = [split(stack(c, 0)) for c in second]

    def block(i, j):
        return stack(
            [
                stack([after[i, j], after[i, j + 2]], 1),
                stack([after[i + 2, j] if i + 2 <= j else after[j, i + 2].T, after[i + 2, j + 2]], 1),
            ],
            0,
        )

    def update(ci, mat, cj):
        return dots(ci, split(dots(split(mat), cj)), 0, 0)

    g00 = update(c0, block(0, 0), c0)
    g04 = update(c0, block(0, 4), c4)
    g44 = update(c4, block(4, 4), c4)
    gens = [generator(g04, g00, g44, sign(0, 4))]
    (a, b), = columns(gens)
    top = dots(c0, split(a))
    bottom = dots(c4, split(b))
    weight = {0: top[:width], 2: top[width:], 4: bottom[:width], 6: bottom[width:]}
    coef = {}
    for i in outs:
        both = dots(col[i], split(weight[i]))
        coef[i], coef[i + 1] = both[:width], both[width:]
    coefs = [split(coef[k]) for k in range(8)]
    rows = out_ref.shape[0]
    tile = min(rows, 256)

    for at in range(0, rows, tile):
        total = jnp.zeros((tile, width), jnp.float32)
        for k in range(len(coefs)):
            total += dots(split(all_ref[labels[k], at : at + tile]), coefs[k])
        out_ref[at : at + tile, :] = total


def cat(parts, axis):
    return jnp.concatenate(parts, axis=axis)


def one(a, b, cb=0):
    return lax.dot_general(
        a, b, (((1,), (cb,)), ((), ())), preferred_element_type=jnp.float32
    )


def wide(a, b, cb=0):
    return one(cat([a[0], a[1], a[0]], 1), cat([b[0], b[0], b[1]], cb), cb)


def eyes(width):
    row = lax.broadcasted_iota(jnp.int32, (width, width), 0)
    col = lax.broadcasted_iota(jnp.int32, (width, width), 1)
    return row == col


def normal(cross, own, other, sign):
    diag = eyes(cross.shape[0])
    dc = jnp.sum(jnp.where(diag, own, 0.0), axis=1, keepdims=True)
    dp = jnp.sum(jnp.where(diag, other, 0.0), axis=0, keepdims=True)
    dc = jnp.maximum(dc, 0.0) + EPS
    dp = jnp.maximum(dp, 0.0) + EPS
    cross = cross * (lax.rsqrt(dc) * lax.rsqrt(dp))
    total = jnp.sum(jnp.sum(cross * cross, axis=0, keepdims=True), axis=1, keepdims=True)
    return cross, sign * lax.rsqrt(1.0 + total)


def rows_of_rotations(pairs):
    width = pairs[0][0].shape[0]
    eye = jnp.where(eyes(width), 1.0, 0.0).astype(jnp.float32)
    parts = [split(c) for c, _ in pairs]
    squares = [wide(p, p, 1) for p in parts]
    es = [0.5 * eye - (0.5 * a * a) * s for (_, a), s in zip(pairs, squares)]
    gs = [a * c for c, a in pairs]
    ep = [split(e) for e in es]
    boths = [wide(p, [cat([x, y], 1) for x, y in zip(p, split(g))]) for p, g in zip(ep, gs)]
    ys = [
        (0.5**0.5) * cat([eye + 0.5 * e, g + 0.5 * b[:, width:]], 1)
        for e, g, b in zip(es, gs, boths)
    ]
    fs = [b[:, :width] for b in boths]
    es = [0.75 * f + 0.25 * wide(split(f), p) for f, p in zip(fs, ep)]
    ep = [split(e) for e in es]
    boths = [wide(p, [cat([x, z], 1) for x, z in zip(p, split(y))]) for p, y in zip(ep, ys)]
    ys = [y + 0.5 * b[:, width:] for y, b in zip(ys, boths)]
    fs = [b[:, :width] for b in boths]
    es = [0.75 * f + 0.25 * one(f.astype(jnp.bfloat16), p[0]) for f, p in zip(fs, ep)]
    ep = [split(e) for e in es]
    fs = [one(p[0], p[0]) for p in ep]
    ys = [y + 0.5 * wide(p, split(y)) for y, p in zip(ys, ep)]
    es = [0.75 * f + 0.25 * one(f.astype(jnp.bfloat16), p[0]) for f, p in zip(fs, ep)]
    eh = [e.astype(jnp.bfloat16) for e in es]
    fs = [one(h, h) for h in eh]
    ys = [y + 0.5 * one(h, y.astype(jnp.bfloat16)) for y, h in zip(ys, eh)]
    last = [
        (0.5 * (0.75 * f + 0.25 * one(f.astype(jnp.bfloat16), h))).astype(jnp.bfloat16)
        for f, h in zip(fs, eh)
    ]
    return ys, last


def finish(x, last):
    return x + one(last, x.astype(jnp.bfloat16))


def rotate4(plan_ref, label, gram_ref, all_ref, out_ref, relay, ready):
    width = out_ref.shape[1]
    masks = [plan_ref[s] for s in range(2)]
    labels = [label, jnp.bitwise_xor(label, masks[0]), jnp.bitwise_xor(label, masks[1])]
    labels.append(jnp.bitwise_xor(labels[1], masks[1]))

    def sign(i, j):
        return jnp.where(labels[i] < labels[j], 1.0, -1.0).astype(jnp.float32)

    def grid(blocks):
        return cat([cat(line, 1) for line in blocks], 0)

    first = [[gram_ref[labels[j], labels[i]] for j in range(4)] for i in range(4)]
    pairs = [normal(first[i][i ^ 1], first[i][i], first[i ^ 1][i ^ 1], sign(i, i ^ 1)) for i in range(4)]
    ys, last = rows_of_rotations(pairs)
    ys = [cat([y[:, width:], y[:, :width]], 1) if i % 2 else y for i, y in enumerate(ys)]
    turned = []
    lines = []
    for p in range(2):
        slab = split(grid([first[2 * p], first[2 * p + 1]]))
        top = wide(split(cat(ys[2 * p : 2 * p + 2], 0)), slab)
        top = cat([finish(top[:width], last[2 * p]), finish(top[width:], last[2 * p + 1])], 0)
        lines.append(split(top))
        turned.append(split(cat([finish(ys[2 * p + c], last[2 * p + c]) for c in (0, 1)], 0)))
    after = [[None] * 4 for _ in range(4)]
    for p in range(2):
        for q in range(2):
            cut = slice(2 * q * width, 2 * (q + 1) * width)
            block = wide([x[:, cut] for x in lines[p]], turned[q], 1)
            for i in range(2):
                for j in range(2):
                    at = slice(i * width, (i + 1) * width), slice(j * width, (j + 1) * width)
                    after[2 * p + i][2 * q + j] = block[at]
    relay()
    own, far = (0, 2), (3, 1)
    pairs = [normal(after[i][j], after[i][i], after[j][j], sign(i, j)) for i, j in (own, far)]
    ys, last = rows_of_rotations(pairs)
    slab = split(grid([[after[i][j] for j in own + far] for i in own]))
    line0 = split(finish(wide(split(ys[0]), slab), last[0]))
    slab = split(grid([[after[i][j] for j in far] for i in far]))
    line3 = split(finish(wide(split(ys[1]), slab), last[1]))
    c0, c3 = [split(finish(y, e)) for y, e in zip(ys, last)]
    g00 = wide([x[:, : 2 * width] for x in line0], c0, 1)
    g03 = wide([x[:, 2 * width :] for x in line0], c3, 1)
    g33 = wide(line3, c3, 1)
    ys, last = rows_of_rotations([normal(g03, g00, g33, sign(0, 3))])

    def row(slot):
        at = slice(slot % 2 * width, (slot % 2 + 1) * width)
        return [x[at] for x in turned[slot // 2]]

    def piece(c, half, slot):
        return wide([x[:, half * width : (half + 1) * width] for x in c], row(slot))

    mixed = split(
        grid([[piece(c0, 0, 0), piece(c0, 1, 2)], [piece(c3, 1, 1), piece(c3, 0, 3)]])
    )
    coef = split(finish(wide(split(ys[0]), mixed), last[0]))
    ready()
    rows = out_ref.shape[0]
    tile = min(rows, 256)
    for at in range(0, rows, tile):
        line = split(cat([all_ref[labels[k], at : at + tile] for k in range(4)], 1))
        out_ref[at : at + tile, :] = wide(line, coef, 1)


def kernel(nb, nr, plan_ref, own_ref, out_ref, all_ref, gram_ref, part, land, *sems):
    a_send, a_recv, b_send, b_recv, c_send, c_recv, d_send, d_recv = sems
    me, row = lax.axis_index("cols"), lax.axis_index("rows")
    chips = nb // 2
    chip, core = me // 2, lax.rem(me, 2)
    sibling = chip * 2 + (1 - core)
    rows, width = own_ref.shape
    piece = 2 * width // nr
    far = range(1, chips)
    chunks = a_send.shape[2]
    size = rows // chunks

    def ahead(d):
        return lax.rem(chip + d, chips)

    def behind(d):
        return lax.rem(chip + 2 * chips - d, chips)

    def peer(k):
        return lax.rem(row + k, nr)

    barrier = pltpu.get_barrier_semaphore()
    targets = [{"cols": sibling}] + [{"cols": ahead(d) * 2 + core} for d in far]
    targets += [{"rows": peer(k)} for k in range(1, nr)]
    for target in targets:
        pl.semaphore_signal(barrier, inc=1, device_id=target, device_id_type=MESH)
    pl.semaphore_wait(barrier, len(targets))

    started = []

    def start(copy):
        copy.start()
        started.append(copy)

    def copies(ref, source, send, recv, at):
        def direct(d, n):
            return pltpu.make_async_remote_copy(
                source.at[at(0, n)], ref.at[me, at(0, n)], send.at[d, 0, n], recv.at[d, 0, n],
                device_id={"cols": ahead(d) * 2 + core}, device_id_type=MESH,
            )

        def relay(d, n):
            block = behind(d) * 2 + core
            return pltpu.make_async_remote_copy(
                source.at[at(0, n)] if d == 0 else ref.at[block, at(d, n)], ref.at[block, at(d, n)],
                send.at[d, 1, n], recv.at[d, 1, n],
                device_id={"cols": sibling}, device_id_type=MESH,
            )

        return direct, relay

    def group(d, n):
        return pl.ds(behind(d + n) * 2, 2)

    direct, relay = copies(all_ref, own_ref, a_send, a_recv, lambda d, n: pl.ds(n * size, size))
    far_panel, near_panel = copies(gram_ref, gram_ref.at[me], d_send, d_recv, group)

    def multiply(block, ch):
        at = pl.ds(ch * size, size)
        to = pl.ds(pl.multiple_of(block * width, width), width)
        product = dot(all_ref[block, at, :], own_ref[at, :], 0, 0)
        if ch == 0:
            part[to, :] = product
        else:
            part[to, :] += product

    def rows_of(g, r):
        return pl.ds(pl.multiple_of(behind(g) * (2 * width) + r * piece, piece), piece)

    def place(g):
        half = nr // 2
        at = pl.ds(pl.multiple_of(lax.rem(row, half) * piece, piece), piece)
        return gram_ref.at[me, behind(g) * 2 + row // half, at]

    def scatter(g, k):
        return pltpu.make_async_remote_copy(
            part.at[rows_of(g, peer(k))], land.at[g, k - 1],
            b_send.at[g, k - 1], b_recv.at[g, k - 1],
            device_id={"rows": peer(k)}, device_id_type=MESH,
        )

    def spread(g, k):
        return pltpu.make_async_remote_copy(
            place(g), place(g),
            c_send.at[g, k - 1], c_recv.at[g, k - 1],
            device_id={"rows": peer(k)}, device_id_type=MESH,
        )

    def send_group(g):
        for k in range(1, nr):
            start(scatter(g, k))

    def sum_group(g):
        total = part[rows_of(g, row), :]
        for k in range(1, nr):
            scatter(g, k).wait_recv()
            total += land[g, k - 1]
        place(g)[...] = total
        for k in range(1, nr):
            start(spread(g, k))

    def share_group(g):
        for k in range(1, nr):
            spread(g, k).wait_recv()
        for d in far:
            start(far_panel(d, g))
        start(near_panel(0, g))

    for ch in range(chunks):
        for d in far:
            start(direct(d, ch))
    for ch in range(chunks):
        start(relay(0, ch))
    all_ref[me] = own_ref[...]
    for ch in range(chunks):
        multiply(me, ch)
    for ch in range(chunks):
        relay(0, ch).wait_recv()
        multiply(sibling, ch)
    send_group(0)
    for ch in range(chunks + 1):
        for d in far:
            if ch < chunks:
                direct(d, ch).wait_recv()
                start(relay(d, ch))
                multiply(behind(d) * 2 + core, ch)
            if ch > 0:
                relay(d, ch - 1).wait_recv()
                multiply(behind(d) * 2 + 1 - core, ch - 1)
        if ch == chunks - 2:
            sum_group(0)
    for g in far:
        send_group(g)
    share_group(0)
    for g in far:
        sum_group(g)
    for g in far:
        share_group(g)
    for g in range(chips):
        for d in far:
            far_panel(d, g).wait_recv()
            start(near_panel(d, g))
    for g in range(chips):
        for d in range(chips):
            near_panel(d, g).wait_recv()
    rotate(nb, plan_ref, me, gram_ref, all_ref, out_ref)
    for copy in started:
        copy.wait_send()


CHUNKS = 4
LATE = 2


def tall(a, b):
    return lax.dot_general(
        cat([a[0], a[1], a[0]], 0), cat([b[0], b[0], b[1]], 0),
        (((0,), (0,)), ((), ())), preferred_element_type=jnp.float32,
    )


def kernel4(
    nr, plan_ref, own_ref, out_ref, all_ref, gram_ref, flat, cross, stage, early, near, land, masks_ref,
    local_sem, hop, *sems
):
    (swap_send, swap_recv, pair_send, pair_recv, relay_send, relay_recv, b_send, b_recv,
     c_send, c_recv, d_send, d_recv, e_send, e_recv, f_send, f_recv) = sems
    me, row = lax.axis_index("cols"), lax.axis_index("rows")
    chip, core = me // 2, lax.rem(me, 2)
    sibling = chip * 2 + 1 - core
    far = (1 - chip) * 2 + core
    away = (1 - chip) * 2 + 1 - core
    rows, width = own_ref.shape
    half = rows // 2
    fine = width // (2 * nr)

    def peer(k):
        return lax.rem(row + k, nr)

    def there(d):
        return chip if d == 0 else 1 - chip

    def remote(source, target, send, recv, **device):
        return pltpu.make_async_remote_copy(
            source, target, send, recv, device_id=device, device_id_type=MESH
        )

    bits = [1 << n for n in range(nr.bit_length() - 1)]
    ways = [{"rows": jnp.bitwise_xor(row, bit)} for bit in bits[:-1]]
    ways += [{"cols": sibling}, {"cols": far}]
    first = ways + [{"rows": jnp.bitwise_xor(row, bits[-1])}]
    barrier = pltpu.get_barrier_semaphore()
    for way in first:
        pl.semaphore_signal(barrier, inc=1, device_id=way, device_id_type=MESH)
    plan_copy = pltpu.make_async_copy(plan_ref, masks_ref, local_sem.at[0])
    plan_copy.start()
    own_copy = pltpu.make_async_copy(own_ref, all_ref.at[me], local_sem.at[1])
    own_copy.start()
    own_copy.wait()
    pl.semaphore_wait(barrier, len(first))

    def tell(n):
        pl.semaphore_signal(hop.at[n], inc=1, device_id=ways[n], device_id_type=MESH)

    def hear(n):
        pl.semaphore_wait(hop.at[n], 1)

    started = []

    def start(copy):
        copy.start()
        started.append(copy)

    sizes = [half // CHUNKS] * CHUNKS + [half // LATE] * LATE
    offsets = [n * (half // CHUNKS) for n in range(CHUNKS)] + [n * (half // LATE) for n in range(LATE)]

    def span(side, n):
        at = side * half + offsets[n]
        return pl.ds(pl.multiple_of(at, 8), sizes[n])

    def swap(n):
        at = span(1 - chip if n < CHUNKS else chip, n)
        return remote(
            all_ref.at[me, at], all_ref.at[me, at], swap_send.at[n], swap_recv.at[n], cols=far
        )

    def relay(n):
        at = span(chip if n < CHUNKS else 1 - chip, n)
        return remote(
            all_ref.at[far, at], all_ref.at[far, at], relay_send.at[n], relay_recv.at[n],
            cols=sibling,
        )

    def pair(n):
        at = pl.ds(n * half, half)
        return remote(
            all_ref.at[me, at], all_ref.at[me, at], pair_send.at[n], pair_recv.at[n], cols=sibling
        )

    def scatter(k):
        return remote(
            stage.at[peer(k)], early.at[k - 1], b_send.at[k - 1], b_recv.at[k - 1], rows=peer(k)
        )

    def spread(k):
        return remote(
            near.at[me, row], near.at[me, row], c_send.at[k - 1], c_recv.at[k - 1], rows=peer(k)
        )

    def forward(n):
        block = far if n == 2 else me
        return remote(
            near.at[block], near.at[block], d_send.at[n], d_recv.at[n],
            cols=far if n == 0 else sibling,
        )

    def part(d, k):
        index = there(d) * nr + peer(k)
        return pl.ds(pl.multiple_of(index * fine, fine), fine)

    def side(b):
        return jnp.where(chip == 0, core, b)

    def slot(b):
        return jnp.where(chip == 0, b, core)

    def scatter_cross(b, d, k):
        return remote(
            cross.at[b, part(d, k)], land.at[slot(b), chip, k],
            e_send.at[b, d, k], e_recv.at[slot(b), chip, k],
            cols=there(d) * 2 + side(b), rows=peer(k),
        )

    def arrive_cross(i, source, k):
        return remote(
            cross.at[i, part(0, 0)], land.at[i, source, k],
            e_send.at[i, 0, k], e_recv.at[i, source, k], cols=sibling,
        )

    def spread_cross(d, k):
        at = gram_ref.at[2 + core, pl.ds(0, 2), part(0, 0)]
        return remote(
            at, at, f_send.at[d, k], f_recv.at[d, k], cols=there(d) * 2 + core, rows=peer(k)
        )

    def pass_cross():
        at = gram_ref.at[2 + core, pl.ds(0, 2)]
        return remote(at, at, d_send.at[3], d_recv.at[3], cols=sibling)

    for n in range(CHUNKS):
        start(swap(n))
    for n in range(2):
        start(pair(n))
    tell(0)

    step = rows // 4
    total = None
    for n in range(4):
        x = split(all_ref[me, pl.ds(n * step, step)])
        product = tall(x, x)
        total = product if total is None else total + product
    flat[0] = total
    inner = len(bits) - 1
    for n in range(inner):
        hear(n)
        tell(n + 1)
    total = None
    for n in range(4):
        if n % 2 == 0:
            pair(n // 2).wait_recv()
        at = pl.ds(n * step, step)
        product = tall(split(all_ref[chip * 2, at]), split(all_ref[chip * 2 + 1, at]))
        total = product if total is None else total + product
    flat[1] = total
    for k in range(nr):
        stage[k, : 2 * fine] = flat[0, 2 * fine * k : 2 * fine * (k + 1)]
        at = pl.multiple_of(core * (width // 2) + k * fine, fine)
        stage[k, 2 * fine :] = flat[1, pl.ds(at, fine)]
    for k in range(1, nr):
        start(scatter(k))
    hear(inner)
    tell(inner + 1)
    hear(inner + 1)

    totals = [None, None]
    for n in range(CHUNKS):
        swap(n).wait_recv()
        at = span(chip, n)
        for b in range(2):
            left = all_ref[jnp.where(chip == 0, b, far), at]
            right = all_ref[jnp.where(chip == 0, far, 2 + b), at]
            product = tall(split(left), split(right))
            totals[b] = product if n == 0 else totals[b] + product
    for b in range(2):
        cross[b] = totals[b]
    for k in range(nr - 1, -1, -1):
        for d in (1, 0):
            for b in range(2):
                if d or k:
                    start(scatter_cross(b, d, k))
    for b in range(2):
        same = side(b) == core

        @pl.when(same)
        def _():
            land[slot(b), chip, 0] = cross[b, part(0, 0)]

        @pl.when(jnp.logical_not(same))
        def _():
            scatter_cross(b, 0, 0).start()

    sums = stage[row]
    for k in range(1, nr):
        scatter(k).wait_recv()
        sums += early[k - 1]
    near[me, row] = sums
    for k in range(1, nr):
        start(spread(k))
    for n in range(CHUNKS):
        start(relay(n))

    for i in range(2):
        mine = jnp.logical_or(chip == 0, core == i)

        @pl.when(jnp.logical_not(mine))
        def _():
            arrive_cross(i, chip, 0).wait_recv()

        arrive_cross(i, 1 - chip, 0).wait_recv()
        for source in range(2):
            for k in range(1, nr):
                arrive_cross(i, source, k).wait_recv()
        sums = land[i, 0, 0]
        for source in range(2):
            for k in range(nr):
                if source or k:
                    sums += land[i, source, k]
        gram_ref[2 + core, i, part(0, 0)] = sums
    for k in range(nr - 1, -1, -1):
        for d in (1, 0):
            if d or k:
                start(spread_cross(d, k))

    for k in range(1, nr):
        spread(k).wait_recv()
    start(forward(0))
    start(forward(1))
    for n in range(CHUNKS, CHUNKS + LATE):
        start(swap(n))
    forward(0).wait_recv()
    start(forward(2))
    forward(1).wait_recv()
    forward(2).wait_recv()
    for block in range(4):
        gram_ref[block, block] = near[block, :, : 2 * fine].reshape(width, width)
    for c in range(2):
        both = [near[2 * c + i, :, 2 * fine :].reshape(width // 2, width) for i in range(2)]
        both = cat(both, 0)
        gram_ref[2 * c + 1, 2 * c] = both
        gram_ref[2 * c, 2 * c + 1] = both.T

    for k in range(nr):
        for d in range(2):
            if d or k:
                spread_cross(d, k).wait_recv()
    start(pass_cross())
    pass_cross().wait_recv()
    for i in range(2):
        for j in range(2):
            gram_ref[i, 2 + j] = gram_ref[2 + j, i].T

    def late():
        for n in range(CHUNKS, CHUNKS + LATE):
            swap(n).wait_recv()
            start(relay(n))

    def ready():
        for n in range(CHUNKS + LATE):
            relay(n).wait_recv()

    plan_copy.wait()
    rotate4(masks_ref, me, gram_ref, all_ref, out_ref, late, ready)
    for copy in started:
        copy.wait_send()
    for b in range(2):

        @pl.when(jnp.logical_not(side(b) == core))
        def _():
            scatter_cross(b, 0, 0).wait_send()


def local4(nr, snapshots, plan):
    rows, width = snapshots.shape
    fine = width // (2 * nr)
    dma = pltpu.SemaphoreType.DMA
    return pl.pallas_call(
        functools.partial(kernel4, nr),
        out_shape=jax.ShapeDtypeStruct((rows, width), jnp.float32),
        in_specs=[HBM, HBM],
        out_specs=VMEM,
        scratch_shapes=[
            pltpu.VMEM((4, rows, width), jnp.float32),
            pltpu.VMEM((4, 4, width, width), jnp.float32),
            pltpu.VMEM((2, width, width), jnp.float32),
            pltpu.VMEM((2, width, width), jnp.float32),
            pltpu.VMEM((nr, 3 * fine, width), jnp.float32),
            pltpu.VMEM((nr - 1, 3 * fine, width), jnp.float32),
            pltpu.VMEM((4, nr, 3 * fine, width), jnp.float32),
            pltpu.VMEM((2, 2, nr, fine, width), jnp.float32),
            pltpu.SMEM(plan.shape, jnp.int32), dma((2,)),
            pltpu.SemaphoreType.REGULAR((nr.bit_length(),)),
            dma((CHUNKS + LATE,)), dma((CHUNKS + LATE,)),
            dma((2,)), dma((2,)),
            dma((CHUNKS + LATE,)), dma((CHUNKS + LATE,)),
            dma((nr - 1,)), dma((nr - 1,)),
            dma((nr - 1,)), dma((nr - 1,)),
            dma((4,)), dma((4,)),
            dma((2, 2, nr)), dma((2, 2, nr)),
            dma((2, nr)), dma((2, nr)),
        ],
        compiler_params=pltpu.CompilerParams(
            collective_id=0, has_side_effects=True, vmem_limit_bytes=53 * 2**20
        ),
    )(plan, snapshots)


def local(nb, nr, snapshots, plan):
    rows, width = snapshots.shape
    chips = nb // 2
    dma = pltpu.SemaphoreType.DMA
    return pl.pallas_call(
        functools.partial(kernel, nb, nr),
        out_shape=jax.ShapeDtypeStruct((rows, width), jnp.float32),
        in_specs=[SMEM, VMEM],
        out_specs=VMEM,
        scratch_shapes=[
            pltpu.VMEM((nb, rows, width), jnp.float32),
            pltpu.VMEM((nb, nb, width, width), jnp.float32),
            pltpu.VMEM((nb * width, width), jnp.float32),
            pltpu.VMEM((chips, nr - 1, 2 * width // nr, width), jnp.float32),
            dma((chips, 2, 4)), dma((chips, 2, 4)),
            dma((chips, nr - 1)), dma((chips, nr - 1)),
            dma((chips, nr - 1)), dma((chips, nr - 1)),
            dma((chips, 2, chips)), dma((chips, 2, chips)),
        ],
        compiler_params=pltpu.CompilerParams(
            collective_id=0, has_side_effects=True, vmem_limit_bytes=48 * 2**20
        ),
    )(plan, snapshots)


def solution(mesh):
    nb, nr = mesh.shape["cols"], mesh.shape["rows"]
    body = functools.partial(local4, nr) if nb == 4 else functools.partial(local, nb, nr)
    return jax.shard_map(
        body,
        mesh=mesh,
        in_specs=(P("rows", "cols"), P()),
        out_specs=P("rows", "cols"),
        check_vma=False,
    )
```

```python
import functools

import jax
import jax.numpy as jnp
from jax import lax
from jax.experimental import pallas as pl
from jax.experimental.pallas import tpu as pltpu
from jax.sharding import PartitionSpec as P

NSI = 5
EPS = 1e-6
VMEM = pl.BlockSpec(memory_space=pltpu.VMEM)
MESH = pl.DeviceIdType.MESH
SMEM = pl.BlockSpec(memory_space=pltpu.SMEM)
HBM = pl.BlockSpec(memory_space=pltpu.HBM)


def split(x):
    high = x.astype(jnp.bfloat16)
    return high, (x - high.astype(jnp.float32)).astype(jnp.bfloat16)


def dots(a, b, ca=1, cb=0):
    def one(x, y):
        return lax.dot_general(
            x, y, (((ca,), (cb,)), ((), ())), preferred_element_type=jnp.float32
        )

    return one(a[0], b[0]) + (one(a[0], b[1]) + one(a[1], b[0]))


def dot(a, b, ca=1, cb=0):
    return dots(split(a), split(b), ca, cb)


def columns(gens):
    width = gens[0].shape[0]
    row = lax.broadcasted_iota(jnp.int32, (width, width), 0)
    col = lax.broadcasted_iota(jnp.int32, (width, width), 1)
    eye = jnp.where(row == col, 1.0, 0.0).astype(jnp.float32)
    parts = [split(g) for g in gens]
    zs = [0.5 * (eye + dots(p, p, 1, 1)) for p in parts]
    qs = None
    for index in range(NSI):
        ts = [1.5 * eye - 0.5 * z for z in zs]
        tsp = [split(t) for t in ts]
        if qs is None:
            qs = [t * (0.5**0.5) for t in ts]
        else:
            qs = [dots(split(q), t) for q, t in zip(qs, tsp)]
        if index < NSI - 1:
            squares = [dots(t, t) for t in tsp]
            zs = [dot(z, s) for z, s in zip(zs, squares)]
    return [(q, dots(p, split(q), 0, 0)) for q, p in zip(qs, parts)]


def generator(cross, own, other, sign):
    width = cross.shape[0]
    row = lax.broadcasted_iota(jnp.int32, (width, width), 0)
    col = lax.broadcasted_iota(jnp.int32, (width, width), 1)
    diag = row == col
    dc = jnp.sum(jnp.where(diag, own, 0.0), axis=1, keepdims=True)
    dp = jnp.sum(jnp.where(diag, other, 0.0), axis=0, keepdims=True)
    dc = jnp.maximum(dc, 0.0) + EPS
    dp = jnp.maximum(dp, 0.0) + EPS
    cross = cross * (lax.rsqrt(dc) * lax.rsqrt(dp))
    total = jnp.sum(jnp.sum(cross * cross, axis=1, keepdims=True), axis=0, keepdims=True)
    return cross * (sign * lax.rsqrt(1.0 + total))


def rotate(nb, plan_ref, label, gram_ref, all_ref, out_ref):
    width = out_ref.shape[1]
    masks = [plan_ref[s] for s in range(3)]
    labels = []
    for slot in range(8):
        block = label
        for bit in range(3):
            if slot >> bit & 1:
                block = jnp.bitwise_xor(block, masks[bit])
        labels.append(block)

    def sign(i, j):
        return jnp.where(labels[i] < labels[j], 1.0, -1.0).astype(jnp.float32)

    loaded = {}

    def gram(i, j):
        if (i, j) not in loaded:
            loaded[i, j] = gram_ref[labels[j], labels[i]]
        return loaded[i, j]

    def stack(parts, axis):
        return jnp.concatenate(parts, axis=axis)

    outs = (0, 2, 4, 6)
    gens = [generator(gram(i, i + 1), gram(i, i), gram(i + 1, i + 1), sign(i, i + 1)) for i in outs]
    first = columns(gens)
    col = {i: split(stack(c, 0)) for i, c in zip(outs, first)}
    after = {}
    for i in outs:
        for j in outs:
            if j < i:
                continue
            wide = stack(
                [stack([gram(i + p, j), gram(i + p, j + 1)], 1) for p in (0, 1)], 0
            )
            half = dots(split(wide), col[j])
            after[i, j] = dots(col[i], split(half), 0, 0)

    gens = [generator(after[i, i + 2], after[i, i], after[i + 2, i + 2], sign(i, i + 2)) for i in (0, 4)]
    second = columns(gens)
    c0, c4 = [split(stack(c, 0)) for c in second]

    def block(i, j):
        return stack(
            [
                stack([after[i, j], after[i, j + 2]], 1),
                stack([after[i + 2, j] if i + 2 <= j else after[j, i + 2].T, after[i + 2, j + 2]], 1),
            ],
            0,
        )

    def update(ci, mat, cj):
        return dots(ci, split(dots(split(mat), cj)), 0, 0)

    g00 = update(c0, block(0, 0), c0)
    g04 = update(c0, block(0, 4), c4)
    g44 = update(c4, block(4, 4), c4)
    gens = [generator(g04, g00, g44, sign(0, 4))]
    (a, b), = columns(gens)
    top = dots(c0, split(a))
    bottom = dots(c4, split(b))
    weight = {0: top[:width], 2: top[width:], 4: bottom[:width], 6: bottom[width:]}
    coef = {}
    for i in outs:
        both = dots(col[i], split(weight[i]))
        coef[i], coef[i + 1] = both[:width], both[width:]
    coefs = [split(coef[k]) for k in range(8)]
    rows = out_ref.shape[0]
    tile = min(rows, 256)

    for at in range(0, rows, tile):
        total = jnp.zeros((tile, width), jnp.float32)
        for k in range(len(coefs)):
            total += dots(split(all_ref[labels[k], at : at + tile]), coefs[k])
        out_ref[at : at + tile, :] = total


def cat(parts, axis):
    return jnp.concatenate(parts, axis=axis)


def one(a, b, cb=0):
    return lax.dot_general(
        a, b, (((1,), (cb,)), ((), ())), preferred_element_type=jnp.float32
    )


def wide(a, b, cb=0):
    return one(cat([a[0], a[1], a[0]], 1), cat([b[0], b[0], b[1]], cb), cb)


def eyes(width):
    row = lax.broadcasted_iota(jnp.int32, (width, width), 0)
    col = lax.broadcasted_iota(jnp.int32, (width, width), 1)
    return row == col


def normal(cross, own, other, sign):
    diag = eyes(cross.shape[0])
    dc = jnp.sum(jnp.where(diag, own, 0.0), axis=1, keepdims=True)
    dp = jnp.sum(jnp.where(diag, other, 0.0), axis=0, keepdims=True)
    dc = jnp.maximum(dc, 0.0) + EPS
    dp = jnp.maximum(dp, 0.0) + EPS
    cross = cross * (lax.rsqrt(dc) * lax.rsqrt(dp))
    total = jnp.sum(jnp.sum(cross * cross, axis=0, keepdims=True), axis=1, keepdims=True)
    return cross, sign * lax.rsqrt(1.0 + total)


def rows_of_rotations(pairs):
    width = pairs[0][0].shape[0]
    eye = jnp.where(eyes(width), 1.0, 0.0).astype(jnp.float32)
    parts = [split(c) for c, _ in pairs]
    squares = [wide(p, p, 1) for p in parts]
    es = [0.5 * eye - (0.5 * a * a) * s for (_, a), s in zip(pairs, squares)]
    gs = [a * c for c, a in pairs]
    ep = [split(e) for e in es]
    boths = [wide(p, [cat([x, y], 1) for x, y in zip(p, split(g))]) for p, g in zip(ep, gs)]
    ys = [
        (0.5**0.5) * cat([eye + 0.5 * e, g + 0.5 * b[:, width:]], 1)
        for e, g, b in zip(es, gs, boths)
    ]
    fs = [b[:, :width] for b in boths]
    es = [0.75 * f + 0.25 * wide(split(f), p) for f, p in zip(fs, ep)]
    ep = [split(e) for e in es]
    boths = [wide(p, [cat([x, z], 1) for x, z in zip(p, split(y))]) for p, y in zip(ep, ys)]
    ys = [y + 0.5 * b[:, width:] for y, b in zip(ys, boths)]
    fs = [b[:, :width] for b in boths]
    es = [0.75 * f + 0.25 * one(f.astype(jnp.bfloat16), p[0]) for f, p in zip(fs, ep)]
    ep = [split(e) for e in es]
    fs = [one(p[0], p[0]) for p in ep]
    ys = [y + 0.5 * wide(p, split(y)) for y, p in zip(ys, ep)]
    es = [0.75 * f + 0.25 * one(f.astype(jnp.bfloat16), p[0]) for f, p in zip(fs, ep)]
    eh = [e.astype(jnp.bfloat16) for e in es]
    fs = [one(h, h) for h in eh]
    ys = [y + 0.5 * one(h, y.astype(jnp.bfloat16)) for y, h in zip(ys, eh)]
    last = [
        (0.5 * (0.75 * f + 0.25 * one(f.astype(jnp.bfloat16), h))).astype(jnp.bfloat16)
        for f, h in zip(fs, eh)
    ]
    return ys, last


def finish(x, last):
    return x + one(last, x.astype(jnp.bfloat16))


def rotate4(plan_ref, label, gram_ref, all_ref, out_ref, relay, ready):
    width = out_ref.shape[1]
    masks = [plan_ref[s] for s in range(2)]
    labels = [label, jnp.bitwise_xor(label, masks[0]), jnp.bitwise_xor(label, masks[1])]
    labels.append(jnp.bitwise_xor(labels[1], masks[1]))

    def sign(i, j):
        return jnp.where(labels[i] < labels[j], 1.0, -1.0).astype(jnp.float32)

    def grid(blocks):
        return cat([cat(line, 1) for line in blocks], 0)

    first = [[gram_ref[labels[j], labels[i]] for j in range(4)] for i in range(4)]
    pairs = [normal(first[i][i ^ 1], first[i][i], first[i ^ 1][i ^ 1], sign(i, i ^ 1)) for i in range(4)]
    ys, last = rows_of_rotations(pairs)
    ys = [cat([y[:, width:], y[:, :width]], 1) if i % 2 else y for i, y in enumerate(ys)]
    turned = []
    lines = []
    for p in range(2):
        slab = split(grid([first[2 * p], first[2 * p + 1]]))
        top = wide(split(cat(ys[2 * p : 2 * p + 2], 0)), slab)
        top = cat([finish(top[:width], last[2 * p]), finish(top[width:], last[2 * p + 1])], 0)
        lines.append(split(top))
        turned.append(split(cat([finish(ys[2 * p + c], last[2 * p + c]) for c in (0, 1)], 0)))
    after = [[None] * 4 for _ in range(4)]
    for p in range(2):
        for q in range(2):
            cut = slice(2 * q * width, 2 * (q + 1) * width)
            block = wide([x[:, cut] for x in lines[p]], turned[q], 1)
            for i in range(2):
                for j in range(2):
                    at = slice(i * width, (i + 1) * width), slice(j * width, (j + 1) * width)
                    after[2 * p + i][2 * q + j] = block[at]
    relay()
    own, far = (0, 2), (3, 1)
    pairs = [normal(after[i][j], after[i][i], after[j][j], sign(i, j)) for i, j in (own, far)]
    ys, last = rows_of_rotations(pairs)
    slab = split(grid([[after[i][j] for j in own + far] for i in own]))
    line0 = split(finish(wide(split(ys[0]), slab), last[0]))
    slab = split(grid([[after[i][j] for j in far] for i in far]))
    line3 = split(finish(wide(split(ys[1]), slab), last[1]))
    c0, c3 = [split(finish(y, e)) for y, e in zip(ys, last)]
    g00 = wide([x[:, : 2 * width] for x in line0], c0, 1)
    g03 = wide([x[:, 2 * width :] for x in line0], c3, 1)
    g33 = wide(line3, c3, 1)
    ys, last = rows_of_rotations([normal(g03, g00, g33, sign(0, 3))])

    def row(slot):
        at = slice(slot % 2 * width, (slot % 2 + 1) * width)
        return [x[at] for x in turned[slot // 2]]

    def piece(c, half, slot):
        return wide([x[:, half * width : (half + 1) * width] for x in c], row(slot))

    mixed = split(
        grid([[piece(c0, 0, 0), piece(c0, 1, 2)], [piece(c3, 1, 1), piece(c3, 0, 3)]])
    )
    coef = split(finish(wide(split(ys[0]), mixed), last[0]))
    ready()
    rows = out_ref.shape[0]
    tile = min(rows, 256)
    for at in range(0, rows, tile):
        line = split(cat([all_ref[labels[k], at : at + tile] for k in range(4)], 1))
        out_ref[at : at + tile, :] = wide(line, coef, 1)


def kernel(nb, nr, plan_ref, own_ref, out_ref, all_ref, gram_ref, part, land, *sems):
    a_send, a_recv, b_send, b_recv, c_send, c_recv, d_send, d_recv = sems
    me, row = lax.axis_index("cols"), lax.axis_index("rows")
    chips = nb // 2
    chip, core = me // 2, lax.rem(me, 2)
    sibling = chip * 2 + (1 - core)
    rows, width = own_ref.shape
    piece = 2 * width // nr
    far = range(1, chips)
    chunks = a_send.shape[2]
    size = rows // chunks

    def ahead(d):
        return lax.rem(chip + d, chips)

    def behind(d):
        return lax.rem(chip + 2 * chips - d, chips)

    def peer(k):
        return lax.rem(row + k, nr)

    barrier = pltpu.get_barrier_semaphore()
    targets = [{"cols": sibling}] + [{"cols": ahead(d) * 2 + core} for d in far]
    targets += [{"rows": peer(k)} for k in range(1, nr)]
    for target in targets:
        pl.semaphore_signal(barrier, inc=1, device_id=target, device_id_type=MESH)
    pl.semaphore_wait(barrier, len(targets))

    started = []

    def start(copy):
        copy.start()
        started.append(copy)

    def copies(ref, source, send, recv, at):
        def direct(d, n):
            return pltpu.make_async_remote_copy(
                source.at[at(0, n)], ref.at[me, at(0, n)], send.at[d, 0, n], recv.at[d, 0, n],
                device_id={"cols": ahead(d) * 2 + core}, device_id_type=MESH,
            )

        def relay(d, n):
            block = behind(d) * 2 + core
            return pltpu.make_async_remote_copy(
                source.at[at(0, n)] if d == 0 else ref.at[block, at(d, n)], ref.at[block, at(d, n)],
                send.at[d, 1, n], recv.at[d, 1, n],
                device_id={"cols": sibling}, device_id_type=MESH,
            )

        return direct, relay

    def group(d, n):
        return pl.ds(behind(d + n) * 2, 2)

    direct, relay = copies(all_ref, own_ref, a_send, a_recv, lambda d, n: pl.ds(n * size, size))
    far_panel, near_panel = copies(gram_ref, gram_ref.at[me], d_send, d_recv, group)

    def multiply(block, ch):
        at = pl.ds(ch * size, size)
        to = pl.ds(pl.multiple_of(block * width, width), width)
        product = dot(all_ref[block, at, :], own_ref[at, :], 0, 0)
        if ch == 0:
            part[to, :] = product
        else:
            part[to, :] += product

    def rows_of(g, r):
        return pl.ds(pl.multiple_of(behind(g) * (2 * width) + r * piece, piece), piece)

    def place(g):
        half = nr // 2
        at = pl.ds(pl.multiple_of(lax.rem(row, half) * piece, piece), piece)
        return gram_ref.at[me, behind(g) * 2 + row // half, at]

    def scatter(g, k):
        return pltpu.make_async_remote_copy(
            part.at[rows_of(g, peer(k))], land.at[g, k - 1],
            b_send.at[g, k - 1], b_recv.at[g, k - 1],
            device_id={"rows": peer(k)}, device_id_type=MESH,
        )

    def spread(g, k):
        return pltpu.make_async_remote_copy(
            place(g), place(g),
            c_send.at[g, k - 1], c_recv.at[g, k - 1],
            device_id={"rows": peer(k)}, device_id_type=MESH,
        )

    def send_group(g):
        for k in range(1, nr):
            start(scatter(g, k))

    def sum_group(g):
        total = part[rows_of(g, row), :]
        for k in range(1, nr):
            scatter(g, k).wait_recv()
            total += land[g, k - 1]
        place(g)[...] = total
        for k in range(1, nr):
            start(spread(g, k))

    def share_group(g):
        for k in range(1, nr):
            spread(g, k).wait_recv()
        for d in far:
            start(far_panel(d, g))
        start(near_panel(0, g))

    for ch in range(chunks):
        for d in far:
            start(direct(d, ch))
    for ch in range(chunks):
        start(relay(0, ch))
    all_ref[me] = own_ref[...]
    for ch in range(chunks):
        multiply(me, ch)
    for ch in range(chunks):
        relay(0, ch).wait_recv()
        multiply(sibling, ch)
    send_group(0)
    for ch in range(chunks + 1):
        for d in far:
            if ch < chunks:
                direct(d, ch).wait_recv()
                start(relay(d, ch))
                multiply(behind(d) * 2 + core, ch)
            if ch > 0:
                relay(d, ch - 1).wait_recv()
                multiply(behind(d) * 2 + 1 - core, ch - 1)
        if ch == chunks - 2:
            sum_group(0)
    for g in far:
        send_group(g)
    share_group(0)
    for g in far:
        sum_group(g)
    for g in far:
        share_group(g)
    for g in range(chips):
        for d in far:
            far_panel(d, g).wait_recv()
            start(near_panel(d, g))
    for g in range(chips):
        for d in range(chips):
            near_panel(d, g).wait_recv()
    rotate(nb, plan_ref, me, gram_ref, all_ref, out_ref)
    for copy in started:
        copy.wait_send()


CHUNKS = 4
LATE = 4
SOON = 2


def tall(a, b):
    return lax.dot_general(
        cat([a[0], a[1], a[0]], 0), cat([b[0], b[0], b[1]], 0),
        (((0,), (0,)), ((), ())), preferred_element_type=jnp.float32,
    )


def kernel4(
    nr, plan_ref, own_ref, out_ref, all_ref, gram_ref, flat, cross, stage, early, near, land, masks_ref,
    local_sem, hop, *sems
):
    (swap_send, swap_recv, pair_send, pair_recv, relay_send, relay_recv, b_send, b_recv,
     c_send, c_recv, d_send, d_recv, e_send, e_recv, f_send, f_recv) = sems
    me, row = lax.axis_index("cols"), lax.axis_index("rows")
    chip, core = me // 2, lax.rem(me, 2)
    sibling = chip * 2 + 1 - core
    far = (1 - chip) * 2 + core
    away = (1 - chip) * 2 + 1 - core
    rows, width = own_ref.shape
    half = rows // 2
    fine = width // (2 * nr)
    owners = nr // 2
    share = width // nr
    owner = jnp.logical_and(row >= nr // 4, row < nr // 4 + owners)

    def peer(k):
        return lax.rem(row + k, nr)

    def there(d):
        return chip if d == 0 else 1 - chip

    def remote(source, target, send, recv, **device):
        return pltpu.make_async_remote_copy(
            source, target, send, recv, device_id=device, device_id_type=MESH
        )

    bits = [1 << n for n in range(nr.bit_length() - 1)]
    ways = [{"rows": jnp.bitwise_xor(row, bit)} for bit in bits[:-1]]
    ways += [{"cols": sibling}, {"cols": far}]
    first = ways + [{"rows": jnp.bitwise_xor(row, bits[-1])}]
    barrier = pltpu.get_barrier_semaphore()
    for way in first:
        pl.semaphore_signal(barrier, inc=1, device_id=way, device_id_type=MESH)
    plan_copy = pltpu.make_async_copy(plan_ref, masks_ref, local_sem.at[0])
    plan_copy.start()
    own_copy = pltpu.make_async_copy(own_ref, all_ref.at[me], local_sem.at[1])
    own_copy.start()
    own_copy.wait()
    pl.semaphore_wait(barrier, len(first))

    def tell(n):
        pl.semaphore_signal(hop.at[n], inc=1, device_id=ways[n], device_id_type=MESH)

    def hear(n):
        pl.semaphore_wait(hop.at[n], 1)

    started = []

    def start(copy):
        copy.start()
        started.append(copy)

    sizes = [half // CHUNKS] * CHUNKS + [half // LATE] * LATE
    offsets = [n * (half // CHUNKS) for n in range(CHUNKS)] + [n * (half // LATE) for n in range(LATE)]

    def span(side, n):
        at = side * half + offsets[n]
        return pl.ds(pl.multiple_of(at, 8), sizes[n])

    def swap(n):
        at = span(1 - chip if n < CHUNKS else chip, n)
        return remote(
            all_ref.at[me, at], all_ref.at[me, at], swap_send.at[n], swap_recv.at[n], cols=far
        )

    def relay(n):
        at = span(chip if n < CHUNKS else 1 - chip, n)
        return remote(
            all_ref.at[far, at], all_ref.at[far, at], relay_send.at[n], relay_recv.at[n],
            cols=sibling,
        )

    def pair(n):
        at = pl.ds(n * half, half)
        return remote(
            all_ref.at[me, at], all_ref.at[me, at], pair_send.at[n], pair_recv.at[n], cols=sibling
        )

    def scatter(k):
        return remote(
            stage.at[peer(k)], early.at[k - 1], b_send.at[k - 1], b_recv.at[k - 1], rows=peer(k)
        )

    def spread(k):
        return remote(
            near.at[me, row], near.at[me, row], c_send.at[k - 1], c_recv.at[k - 1], rows=peer(k)
        )

    def forward(n):
        block = far if n == 2 else me
        return remote(
            near.at[block], near.at[block], d_send.at[n], d_recv.at[n],
            cols=far if n == 0 else sibling,
        )

    def target(o):
        return nr // 4 + lax.rem(o + row, owners)

    def piece(x, r):
        index = x * owners + r - nr // 4
        return pl.ds(pl.multiple_of(index * share, share), share)

    def side(b):
        return jnp.where(chip == 0, core, b)

    def slot(b):
        return jnp.where(chip == 0, b, core)

    def scatter_cross(b, d, o):
        return remote(
            cross.at[b, piece(there(d), target(o))], land.at[slot(b), chip, row],
            e_send.at[b, d, o], e_recv.at[slot(b), chip, row],
            cols=there(d) * 2 + side(b), rows=target(o),
        )

    def scatter_near(act):
        for o in range(owners):
            for b in range(2):
                same = jnp.logical_and(side(b) == core, target(o) == row)

                @pl.when(jnp.logical_not(same))
                def _():
                    act(scatter_cross(b, 0, o))

    def arrive_cross(i, x, r):
        return remote(
            cross.at[i, pl.ds(0, share)], land.at[i, x, r],
            e_send.at[i, 0, 0], e_recv.at[i, x, r], cols=sibling,
        )

    def spread_cross(d, k):
        at = gram_ref.at[2 + core, pl.ds(0, 2), piece(chip, row)]
        return remote(
            at, at, f_send.at[d, k], f_recv.at[chip, row - nr // 4],
            cols=there(d) * 2 + core, rows=peer(k),
        )

    def arrive_spread(x, o):
        at = gram_ref.at[2 + core, pl.ds(0, 2), piece(x, nr // 4 + o)]
        return remote(at, at, f_send.at[0, 0], f_recv.at[x, o], cols=sibling)

    def pass_cross():
        at = gram_ref.at[2 + core, pl.ds(0, 2)]
        return remote(at, at, d_send.at[3], d_recv.at[3], cols=sibling)

    for n in range(CHUNKS):
        start(swap(n))
    for n in range(2):
        start(pair(n))
    tell(0)

    step = rows // 4
    total = None
    for n in range(4):
        x = split(all_ref[me, pl.ds(n * step, step)])
        product = tall(x, x)
        total = product if total is None else total + product
    flat[0] = total
    inner = len(bits) - 1
    for n in range(inner):
        hear(n)
        tell(n + 1)
    total = None
    for n in range(4):
        if n % 2 == 0:
            pair(n // 2).wait_recv()
        at = pl.ds(n * step, step)
        product = tall(split(all_ref[chip * 2, at]), split(all_ref[chip * 2 + 1, at]))
        total = product if total is None else total + product
    flat[1] = total
    for k in range(nr):
        stage[k, : 2 * fine] = flat[0, 2 * fine * k : 2 * fine * (k + 1)]
        at = pl.multiple_of(core * (width // 2) + k * fine, fine)
        stage[k, 2 * fine :] = flat[1, pl.ds(at, fine)]
    for k in range(1, nr):
        start(scatter(k))
    hear(inner)
    tell(inner + 1)
    hear(inner + 1)

    totals = [None, None]
    for n in range(CHUNKS):
        swap(n).wait_recv()
        at = span(chip, n)
        for b in range(2):
            left = all_ref[jnp.where(chip == 0, b, far), at]
            right = all_ref[jnp.where(chip == 0, far, 2 + b), at]
            product = tall(split(left), split(right))
            totals[b] = product if n == 0 else totals[b] + product
    for b in range(2):
        cross[b] = totals[b]
    for o in range(owners):
        for b in range(2):
            start(scatter_cross(b, 1, o))
    scatter_near(lambda copy: copy.start())
    for n in range(CHUNKS, CHUNKS + SOON):
        start(swap(n))

    sums = stage[row]
    for k in range(1, nr):
        scatter(k).wait_recv()
        sums += early[k - 1]
    near[me, row] = sums
    for k in range(1, nr):
        start(spread(k))
    for n in range(CHUNKS):
        start(relay(n))

    for k in range(1, nr):
        spread(k).wait_recv()
    start(forward(0))
    start(forward(1))

    @pl.when(owner)
    def _():
        for b in range(2):

            @pl.when(side(b) == core)
            def _():
                land[slot(b), chip, row] = cross[b, piece(chip, row)]

        for i in range(2):
            sums = None
            for x in range(2):
                for r in range(nr):
                    same = jnp.logical_and(row == r, chip == x)
                    if x == 1:
                        same = jnp.logical_and(same, core == i)

                    @pl.when(jnp.logical_not(same))
                    def _():
                        arrive_cross(i, x, r).wait_recv()

            for x in range(2):
                for r in range(nr):
                    sums = land[i, x, r] if sums is None else sums + land[i, x, r]
            gram_ref[2 + core, i, piece(chip, row)] = sums
        for k in range(nr - 1, -1, -1):
            for d in (1, 0):
                if d or k:
                    spread_cross(d, k).start()

    for n in range(CHUNKS + SOON, CHUNKS + LATE):
        start(swap(n))
    forward(0).wait_recv()
    start(forward(2))
    for n in range(CHUNKS, CHUNKS + SOON):
        swap(n).wait_recv()
        start(relay(n))
    forward(1).wait_recv()
    forward(2).wait_recv()
    for block in range(4):
        gram_ref[block, block] = near[block, :, : 2 * fine].reshape(width, width)
    for c in range(2):
        both = [near[2 * c + i, :, 2 * fine :].reshape(width // 2, width) for i in range(2)]
        both = cat(both, 0)
        gram_ref[2 * c + 1, 2 * c] = both
        gram_ref[2 * c, 2 * c + 1] = both.T

    for x in range(2):
        for o in range(owners):

            @pl.when(jnp.logical_not(jnp.logical_and(chip == x, row == nr // 4 + o)))
            def _():
                arrive_spread(x, o).wait_recv()

    start(pass_cross())
    pass_cross().wait_recv()
    for i in range(2):
        for j in range(2):
            gram_ref[i, 2 + j] = gram_ref[2 + j, i].T

    def late():
        for n in range(CHUNKS + SOON, CHUNKS + LATE):
            swap(n).wait_recv()
            start(relay(n))

    def ready():
        for n in range(CHUNKS + LATE):
            relay(n).wait_recv()

    plan_copy.wait()
    rotate4(masks_ref, me, gram_ref, all_ref, out_ref, late, ready)
    for copy in started:
        copy.wait_send()
    scatter_near(lambda copy: copy.wait_send())

    @pl.when(owner)
    def _():
        for k in range(nr):
            for d in range(2):
                if d or k:
                    spread_cross(d, k).wait_send()


def local4(nr, snapshots, plan):
    rows, width = snapshots.shape
    fine = width // (2 * nr)
    dma = pltpu.SemaphoreType.DMA
    return pl.pallas_call(
        functools.partial(kernel4, nr),
        out_shape=jax.ShapeDtypeStruct((rows, width), jnp.float32),
        in_specs=[HBM, HBM],
        out_specs=VMEM,
        scratch_shapes=[
            pltpu.VMEM((4, rows, width), jnp.float32),
            pltpu.VMEM((4, 4, width, width), jnp.float32),
            pltpu.VMEM((2, width, width), jnp.float32),
            pltpu.VMEM((2, width, width), jnp.float32),
            pltpu.VMEM((nr, 3 * fine, width), jnp.float32),
            pltpu.VMEM((nr - 1, 3 * fine, width), jnp.float32),
            pltpu.VMEM((4, nr, 3 * fine, width), jnp.float32),
            pltpu.VMEM((2, 2, nr, width // nr, width), jnp.float32),
            pltpu.SMEM(plan.shape, jnp.int32), dma((2,)),
            pltpu.SemaphoreType.REGULAR((nr.bit_length(),)),
            dma((CHUNKS + LATE,)), dma((CHUNKS + LATE,)),
            dma((2,)), dma((2,)),
            dma((CHUNKS + LATE,)), dma((CHUNKS + LATE,)),
            dma((nr - 1,)), dma((nr - 1,)),
            dma((nr - 1,)), dma((nr - 1,)),
            dma((4,)), dma((4,)),
            dma((2, 2, nr // 2)), dma((2, 2, nr)),
            dma((2, nr)), dma((2, nr // 2)),
        ],
        compiler_params=pltpu.CompilerParams(
            collective_id=0, has_side_effects=True, vmem_limit_bytes=53 * 2**20
        ),
    )(plan, snapshots)


def local(nb, nr, snapshots, plan):
    rows, width = snapshots.shape
    chips = nb // 2
    dma = pltpu.SemaphoreType.DMA
    return pl.pallas_call(
        functools.partial(kernel, nb, nr),
        out_shape=jax.ShapeDtypeStruct((rows, width), jnp.float32),
        in_specs=[SMEM, VMEM],
        out_specs=VMEM,
        scratch_shapes=[
            pltpu.VMEM((nb, rows, width), jnp.float32),
            pltpu.VMEM((nb, nb, width, width), jnp.float32),
            pltpu.VMEM((nb * width, width), jnp.float32),
            pltpu.VMEM((chips, nr - 1, 2 * width // nr, width), jnp.float32),
            dma((chips, 2, 4)), dma((chips, 2, 4)),
            dma((chips, nr - 1)), dma((chips, nr - 1)),
            dma((chips, nr - 1)), dma((chips, nr - 1)),
            dma((chips, 2, chips)), dma((chips, 2, chips)),
        ],
        compiler_params=pltpu.CompilerParams(
            collective_id=0, has_side_effects=True, vmem_limit_bytes=48 * 2**20
        ),
    )(plan, snapshots)


def solution(mesh):
    nb, nr = mesh.shape["cols"], mesh.shape["rows"]
    four = nb == 4 and nr >= 4 and nr & (nr - 1) == 0
    body = functools.partial(local4, nr) if four else functools.partial(local, nb, nr)
    return jax.shard_map(
        body,
        mesh=mesh,
        in_specs=(P("rows", "cols"), P()),
        out_specs=P("rows", "cols"),
        check_vma=False,
    )
```

```python
import functools

import jax
import jax.numpy as jnp
from jax import lax
from jax.experimental import pallas as pl
from jax.experimental.pallas import tpu as pltpu
from jax.sharding import PartitionSpec as P

NSI = 5
EPS = 1e-6
VMEM = pl.BlockSpec(memory_space=pltpu.VMEM)
MESH = pl.DeviceIdType.MESH
SMEM = pl.BlockSpec(memory_space=pltpu.SMEM)
HBM = pl.BlockSpec(memory_space=pltpu.HBM)


def split(x):
    high = x.astype(jnp.bfloat16)
    return high, (x - high.astype(jnp.float32)).astype(jnp.bfloat16)


def dots(a, b, ca=1, cb=0):
    def one(x, y):
        return lax.dot_general(
            x, y, (((ca,), (cb,)), ((), ())), preferred_element_type=jnp.float32
        )

    return one(a[0], b[0]) + (one(a[0], b[1]) + one(a[1], b[0]))


def dot(a, b, ca=1, cb=0):
    return dots(split(a), split(b), ca, cb)


def columns(gens):
    width = gens[0].shape[0]
    row = lax.broadcasted_iota(jnp.int32, (width, width), 0)
    col = lax.broadcasted_iota(jnp.int32, (width, width), 1)
    eye = jnp.where(row == col, 1.0, 0.0).astype(jnp.float32)
    parts = [split(g) for g in gens]
    zs = [0.5 * (eye + dots(p, p, 1, 1)) for p in parts]
    qs = None
    for index in range(NSI):
        ts = [1.5 * eye - 0.5 * z for z in zs]
        tsp = [split(t) for t in ts]
        if qs is None:
            qs = [t * (0.5**0.5) for t in ts]
        else:
            qs = [dots(split(q), t) for q, t in zip(qs, tsp)]
        if index < NSI - 1:
            squares = [dots(t, t) for t in tsp]
            zs = [dot(z, s) for z, s in zip(zs, squares)]
    return [(q, dots(p, split(q), 0, 0)) for q, p in zip(qs, parts)]


def generator(cross, own, other, sign):
    width = cross.shape[0]
    row = lax.broadcasted_iota(jnp.int32, (width, width), 0)
    col = lax.broadcasted_iota(jnp.int32, (width, width), 1)
    diag = row == col
    dc = jnp.sum(jnp.where(diag, own, 0.0), axis=1, keepdims=True)
    dp = jnp.sum(jnp.where(diag, other, 0.0), axis=0, keepdims=True)
    dc = jnp.maximum(dc, 0.0) + EPS
    dp = jnp.maximum(dp, 0.0) + EPS
    cross = cross * (lax.rsqrt(dc) * lax.rsqrt(dp))
    total = jnp.sum(jnp.sum(cross * cross, axis=1, keepdims=True), axis=0, keepdims=True)
    return cross * (sign * lax.rsqrt(1.0 + total))


def rotate(nb, plan_ref, label, gram_ref, all_ref, out_ref):
    width = out_ref.shape[1]
    masks = [plan_ref[s] for s in range(3)]
    labels = []
    for slot in range(8):
        block = label
        for bit in range(3):
            if slot >> bit & 1:
                block = jnp.bitwise_xor(block, masks[bit])
        labels.append(block)

    def sign(i, j):
        return jnp.where(labels[i] < labels[j], 1.0, -1.0).astype(jnp.float32)

    loaded = {}

    def gram(i, j):
        if (i, j) not in loaded:
            loaded[i, j] = gram_ref[labels[j], labels[i]]
        return loaded[i, j]

    def stack(parts, axis):
        return jnp.concatenate(parts, axis=axis)

    outs = (0, 2, 4, 6)
    gens = [generator(gram(i, i + 1), gram(i, i), gram(i + 1, i + 1), sign(i, i + 1)) for i in outs]
    first = columns(gens)
    col = {i: split(stack(c, 0)) for i, c in zip(outs, first)}
    after = {}
    for i in outs:
        for j in outs:
            if j < i:
                continue
            wide = stack(
                [stack([gram(i + p, j), gram(i + p, j + 1)], 1) for p in (0, 1)], 0
            )
            half = dots(split(wide), col[j])
            after[i, j] = dots(col[i], split(half), 0, 0)

    gens = [generator(after[i, i + 2], after[i, i], after[i + 2, i + 2], sign(i, i + 2)) for i in (0, 4)]
    second = columns(gens)
    c0, c4 = [split(stack(c, 0)) for c in second]

    def block(i, j):
        return stack(
            [
                stack([after[i, j], after[i, j + 2]], 1),
                stack([after[i + 2, j] if i + 2 <= j else after[j, i + 2].T, after[i + 2, j + 2]], 1),
            ],
            0,
        )

    def update(ci, mat, cj):
        return dots(ci, split(dots(split(mat), cj)), 0, 0)

    g00 = update(c0, block(0, 0), c0)
    g04 = update(c0, block(0, 4), c4)
    g44 = update(c4, block(4, 4), c4)
    gens = [generator(g04, g00, g44, sign(0, 4))]
    (a, b), = columns(gens)
    top = dots(c0, split(a))
    bottom = dots(c4, split(b))
    weight = {0: top[:width], 2: top[width:], 4: bottom[:width], 6: bottom[width:]}
    coef = {}
    for i in outs:
        both = dots(col[i], split(weight[i]))
        coef[i], coef[i + 1] = both[:width], both[width:]
    coefs = [split(coef[k]) for k in range(8)]
    rows = out_ref.shape[0]
    tile = min(rows, 256)

    for at in range(0, rows, tile):
        total = jnp.zeros((tile, width), jnp.float32)
        for k in range(len(coefs)):
            total += dots(split(all_ref[labels[k], at : at + tile]), coefs[k])
        out_ref[at : at + tile, :] = total


def cat(parts, axis):
    return jnp.concatenate(parts, axis=axis)


def one(a, b, cb=0):
    return lax.dot_general(
        a, b, (((1,), (cb,)), ((), ())), preferred_element_type=jnp.float32
    )


def wide(a, b, cb=0):
    return one(cat([a[0], a[1], a[0]], 1), cat([b[0], b[0], b[1]], cb), cb)


def eyes(width):
    row = lax.broadcasted_iota(jnp.int32, (width, width), 0)
    col = lax.broadcasted_iota(jnp.int32, (width, width), 1)
    return row == col


def normal(cross, own, other, sign):
    diag = eyes(cross.shape[0])
    dc = jnp.sum(jnp.where(diag, own, 0.0), axis=1, keepdims=True)
    dp = jnp.sum(jnp.where(diag, other, 0.0), axis=0, keepdims=True)
    dc = jnp.maximum(dc, 0.0) + EPS
    dp = jnp.maximum(dp, 0.0) + EPS
    cross = cross * (lax.rsqrt(dc) * lax.rsqrt(dp))
    total = jnp.sum(jnp.sum(cross * cross, axis=0, keepdims=True), axis=1, keepdims=True)
    return cross, sign * lax.rsqrt(1.0 + total)


def rows_of_rotations(pairs):
    width = pairs[0][0].shape[0]
    eye = jnp.where(eyes(width), 1.0, 0.0).astype(jnp.float32)
    parts = [split(c) for c, _ in pairs]
    squares = [wide(p, p, 1) for p in parts]
    es = [0.5 * eye - (0.5 * a * a) * s for (_, a), s in zip(pairs, squares)]
    gs = [a * c for c, a in pairs]
    ep = [split(e) for e in es]
    boths = [wide(p, [cat([x, y], 1) for x, y in zip(p, split(g))]) for p, g in zip(ep, gs)]
    ys = [
        (0.5**0.5) * cat([eye + 0.5 * e, g + 0.5 * b[:, width:]], 1)
        for e, g, b in zip(es, gs, boths)
    ]
    fs = [b[:, :width] for b in boths]
    es = [0.75 * f + 0.25 * wide(split(f), p) for f, p in zip(fs, ep)]
    ep = [split(e) for e in es]
    boths = [wide(p, [cat([x, z], 1) for x, z in zip(p, split(y))]) for p, y in zip(ep, ys)]
    ys = [y + 0.5 * b[:, width:] for y, b in zip(ys, boths)]
    fs = [b[:, :width] for b in boths]
    es = [0.75 * f + 0.25 * one(f.astype(jnp.bfloat16), p[0]) for f, p in zip(fs, ep)]
    ep = [split(e) for e in es]
    fs = [one(p[0], p[0]) for p in ep]
    ys = [y + 0.5 * wide(p, split(y)) for y, p in zip(ys, ep)]
    es = [0.75 * f + 0.25 * one(f.astype(jnp.bfloat16), p[0]) for f, p in zip(fs, ep)]
    eh = [e.astype(jnp.bfloat16) for e in es]
    fs = [one(h, h) for h in eh]
    ys = [y + 0.5 * one(h, y.astype(jnp.bfloat16)) for y, h in zip(ys, eh)]
    last = [
        (0.5 * (0.75 * f + 0.25 * one(f.astype(jnp.bfloat16), h))).astype(jnp.bfloat16)
        for f, h in zip(fs, eh)
    ]
    return ys, last


def finish(x, last):
    return x + one(last, x.astype(jnp.bfloat16))


def rotate4(plan_ref, label, gram_ref, high_ref, low_ref, out_ref, relay, ready):
    width = out_ref.shape[1]
    masks = [plan_ref[s] for s in range(2)]
    labels = [label, jnp.bitwise_xor(label, masks[0]), jnp.bitwise_xor(label, masks[1])]
    labels.append(jnp.bitwise_xor(labels[1], masks[1]))

    def sign(i, j):
        return jnp.where(labels[i] < labels[j], 1.0, -1.0).astype(jnp.float32)

    def grid(blocks):
        return cat([cat(line, 1) for line in blocks], 0)

    first = [[gram_ref[labels[j], labels[i]] for j in range(4)] for i in range(4)]
    pairs = [normal(first[i][i ^ 1], first[i][i], first[i ^ 1][i ^ 1], sign(i, i ^ 1)) for i in range(4)]
    ys, last = rows_of_rotations(pairs)
    ys = [cat([y[:, width:], y[:, :width]], 1) if i % 2 else y for i, y in enumerate(ys)]
    turned = []
    lines = []
    for p in range(2):
        slab = split(grid([first[2 * p], first[2 * p + 1]]))
        top = wide(split(cat(ys[2 * p : 2 * p + 2], 0)), slab)
        top = cat([finish(top[:width], last[2 * p]), finish(top[width:], last[2 * p + 1])], 0)
        lines.append(split(top))
        turned.append(split(cat([finish(ys[2 * p + c], last[2 * p + c]) for c in (0, 1)], 0)))
    after = [[None] * 4 for _ in range(4)]
    for p in range(2):
        for q in range(2):
            cut = slice(2 * q * width, 2 * (q + 1) * width)
            block = wide([x[:, cut] for x in lines[p]], turned[q], 1)
            for i in range(2):
                for j in range(2):
                    at = slice(i * width, (i + 1) * width), slice(j * width, (j + 1) * width)
                    after[2 * p + i][2 * q + j] = block[at]
    relay()
    own, far = (0, 2), (3, 1)
    pairs = [normal(after[i][j], after[i][i], after[j][j], sign(i, j)) for i, j in (own, far)]
    ys, last = rows_of_rotations(pairs)
    slab = split(grid([[after[i][j] for j in own + far] for i in own]))
    line0 = split(finish(wide(split(ys[0]), slab), last[0]))
    slab = split(grid([[after[i][j] for j in far] for i in far]))
    line3 = split(finish(wide(split(ys[1]), slab), last[1]))
    c0, c3 = [split(finish(y, e)) for y, e in zip(ys, last)]
    g00 = wide([x[:, : 2 * width] for x in line0], c0, 1)
    g03 = wide([x[:, 2 * width :] for x in line0], c3, 1)
    g33 = wide(line3, c3, 1)
    ys, last = rows_of_rotations([normal(g03, g00, g33, sign(0, 3))])

    def row(slot):
        at = slice(slot % 2 * width, (slot % 2 + 1) * width)
        return [x[at] for x in turned[slot // 2]]

    def piece(c, half, slot):
        return wide([x[:, half * width : (half + 1) * width] for x in c], row(slot))

    mixed = split(
        grid([[piece(c0, 0, 0), piece(c0, 1, 2)], [piece(c3, 1, 1), piece(c3, 0, 3)]])
    )
    coef = split(finish(wide(split(ys[0]), mixed), last[0]))
    ready()
    rows = out_ref.shape[0]
    tile = min(rows, 256)
    for at in range(0, rows, tile):
        line = [
            cat([ref[labels[k], at : at + tile] for k in range(4)], 1) for ref in (high_ref, low_ref)
        ]
        both = one(line[0], cat(coef, 0), 1)
        out_ref[at : at + tile, :] = both[:, :width] + (both[:, width:] + one(line[1], coef[0], 1))


def kernel(nb, nr, plan_ref, own_ref, out_ref, all_ref, gram_ref, part, land, *sems):
    a_send, a_recv, b_send, b_recv, c_send, c_recv, d_send, d_recv = sems
    me, row = lax.axis_index("cols"), lax.axis_index("rows")
    chips = nb // 2
    chip, core = me // 2, lax.rem(me, 2)
    sibling = chip * 2 + (1 - core)
    rows, width = own_ref.shape
    piece = 2 * width // nr
    far = range(1, chips)
    chunks = a_send.shape[2]
    size = rows // chunks

    def ahead(d):
        return lax.rem(chip + d, chips)

    def behind(d):
        return lax.rem(chip + 2 * chips - d, chips)

    def peer(k):
        return lax.rem(row + k, nr)

    barrier = pltpu.get_barrier_semaphore()
    targets = [{"cols": sibling}] + [{"cols": ahead(d) * 2 + core} for d in far]
    targets += [{"rows": peer(k)} for k in range(1, nr)]
    for target in targets:
        pl.semaphore_signal(barrier, inc=1, device_id=target, device_id_type=MESH)
    pl.semaphore_wait(barrier, len(targets))

    started = []

    def start(copy):
        copy.start()
        started.append(copy)

    def copies(ref, source, send, recv, at):
        def direct(d, n):
            return pltpu.make_async_remote_copy(
                source.at[at(0, n)], ref.at[me, at(0, n)], send.at[d, 0, n], recv.at[d, 0, n],
                device_id={"cols": ahead(d) * 2 + core}, device_id_type=MESH,
            )

        def relay(d, n):
            block = behind(d) * 2 + core
            return pltpu.make_async_remote_copy(
                source.at[at(0, n)] if d == 0 else ref.at[block, at(d, n)], ref.at[block, at(d, n)],
                send.at[d, 1, n], recv.at[d, 1, n],
                device_id={"cols": sibling}, device_id_type=MESH,
            )

        return direct, relay

    def group(d, n):
        return pl.ds(behind(d + n) * 2, 2)

    direct, relay = copies(all_ref, own_ref, a_send, a_recv, lambda d, n: pl.ds(n * size, size))
    far_panel, near_panel = copies(gram_ref, gram_ref.at[me], d_send, d_recv, group)

    def multiply(block, ch):
        at = pl.ds(ch * size, size)
        to = pl.ds(pl.multiple_of(block * width, width), width)
        product = dot(all_ref[block, at, :], own_ref[at, :], 0, 0)
        if ch == 0:
            part[to, :] = product
        else:
            part[to, :] += product

    def rows_of(g, r):
        return pl.ds(pl.multiple_of(behind(g) * (2 * width) + r * piece, piece), piece)

    def place(g):
        half = nr // 2
        at = pl.ds(pl.multiple_of(lax.rem(row, half) * piece, piece), piece)
        return gram_ref.at[me, behind(g) * 2 + row // half, at]

    def scatter(g, k):
        return pltpu.make_async_remote_copy(
            part.at[rows_of(g, peer(k))], land.at[g, k - 1],
            b_send.at[g, k - 1], b_recv.at[g, k - 1],
            device_id={"rows": peer(k)}, device_id_type=MESH,
        )

    def spread(g, k):
        return pltpu.make_async_remote_copy(
            place(g), place(g),
            c_send.at[g, k - 1], c_recv.at[g, k - 1],
            device_id={"rows": peer(k)}, device_id_type=MESH,
        )

    def send_group(g):
        for k in range(1, nr):
            start(scatter(g, k))

    def sum_group(g):
        total = part[rows_of(g, row), :]
        for k in range(1, nr):
            scatter(g, k).wait_recv()
            total += land[g, k - 1]
        place(g)[...] = total
        for k in range(1, nr):
            start(spread(g, k))

    def share_group(g):
        for k in range(1, nr):
            spread(g, k).wait_recv()
        for d in far:
            start(far_panel(d, g))
        start(near_panel(0, g))

    for ch in range(chunks):
        for d in far:
            start(direct(d, ch))
    for ch in range(chunks):
        start(relay(0, ch))
    all_ref[me] = own_ref[...]
    for ch in range(chunks):
        multiply(me, ch)
    for ch in range(chunks):
        relay(0, ch).wait_recv()
        multiply(sibling, ch)
    send_group(0)
    for ch in range(chunks + 1):
        for d in far:
            if ch < chunks:
                direct(d, ch).wait_recv()
                start(relay(d, ch))
                multiply(behind(d) * 2 + core, ch)
            if ch > 0:
                relay(d, ch - 1).wait_recv()
                multiply(behind(d) * 2 + 1 - core, ch - 1)
        if ch == chunks - 2:
            sum_group(0)
    for g in far:
        send_group(g)
    share_group(0)
    for g in far:
        sum_group(g)
    for g in far:
        share_group(g)
    for g in range(chips):
        for d in far:
            far_panel(d, g).wait_recv()
            start(near_panel(d, g))
    for g in range(chips):
        for d in range(chips):
            near_panel(d, g).wait_recv()
    rotate(nb, plan_ref, me, gram_ref, all_ref, out_ref)
    for copy in started:
        copy.wait_send()


CHUNKS = 4
LATE = 4
SOON = 4


def tall(a, b):
    return lax.dot_general(
        cat([a[0], a[1], a[0]], 0), cat([b[0], b[0], b[1]], 0),
        (((0,), (0,)), ((), ())), preferred_element_type=jnp.float32,
    )


def kernel4(
    nr, plan_ref, own_ref, out_ref, all_ref, gram_ref, flat, cross, stage, early, near, land, high_ref, low_ref,
    masks_ref, local_sem, hop, *sems
):
    (swap_send, swap_recv, pair_send, pair_recv, relay_send, relay_recv, b_send, b_recv,
     c_send, c_recv, d_send, d_recv, e_send, e_recv, f_send, f_recv) = sems
    me, row = lax.axis_index("cols"), lax.axis_index("rows")
    chip, core = me // 2, lax.rem(me, 2)
    sibling = chip * 2 + 1 - core
    far = (1 - chip) * 2 + core
    away = (1 - chip) * 2 + 1 - core
    rows, width = own_ref.shape
    half = rows // 2
    fine = width // (2 * nr)
    owners = nr // 2
    share = width // nr
    owner = jnp.logical_and(row >= nr // 4, row < nr // 4 + owners)

    def peer(k):
        return lax.rem(row + k, nr)

    def there(d):
        return chip if d == 0 else 1 - chip

    def remote(source, target, send, recv, **device):
        return pltpu.make_async_remote_copy(
            source, target, send, recv, device_id=device, device_id_type=MESH
        )

    bits = [1 << n for n in range(nr.bit_length() - 1)]
    ways = [{"rows": jnp.bitwise_xor(row, bit)} for bit in bits[:-1]]
    ways += [{"cols": sibling}, {"cols": far}]
    first = ways + [{"rows": jnp.bitwise_xor(row, bits[-1])}]
    barrier = pltpu.get_barrier_semaphore()
    for way in first:
        pl.semaphore_signal(barrier, inc=1, device_id=way, device_id_type=MESH)
    plan_copy = pltpu.make_async_copy(plan_ref, masks_ref, local_sem.at[0])
    plan_copy.start()
    own_copy = pltpu.make_async_copy(own_ref, all_ref.at[me], local_sem.at[1])
    own_copy.start()
    own_copy.wait()
    pl.semaphore_wait(barrier, len(first))

    def tell(n):
        pl.semaphore_signal(hop.at[n], inc=1, device_id=ways[n], device_id_type=MESH)

    def hear(n):
        pl.semaphore_wait(hop.at[n], 1)

    started = []

    def start(copy):
        copy.start()
        started.append(copy)

    sizes = [half // CHUNKS] * CHUNKS + [half // LATE] * LATE
    offsets = [n * (half // CHUNKS) for n in range(CHUNKS)] + [n * (half // LATE) for n in range(LATE)]

    def span(side, n):
        at = side * half + offsets[n]
        return pl.ds(pl.multiple_of(at, 8), sizes[n])

    def swap(n):
        at = span(1 - chip if n < CHUNKS else chip, n)
        return remote(
            all_ref.at[me, at], all_ref.at[me, at], swap_send.at[n], swap_recv.at[n], cols=far
        )

    def relay(n):
        at = span(chip if n < CHUNKS else 1 - chip, n)
        return remote(
            all_ref.at[far, at], all_ref.at[far, at], relay_send.at[n], relay_recv.at[n],
            cols=sibling,
        )

    def pair(n):
        at = pl.ds(n * half, half)
        return remote(
            all_ref.at[me, at], all_ref.at[me, at], pair_send.at[n], pair_recv.at[n], cols=sibling
        )

    def scatter(k):
        return remote(
            stage.at[peer(k)], early.at[k - 1], b_send.at[k - 1], b_recv.at[k - 1], rows=peer(k)
        )

    def spread(k):
        return remote(
            near.at[me, row], near.at[me, row], c_send.at[k - 1], c_recv.at[k - 1], rows=peer(k)
        )

    def forward(n):
        block = far if n == 2 else me
        return remote(
            near.at[block], near.at[block], d_send.at[n], d_recv.at[n],
            cols=far if n == 0 else sibling,
        )

    def target(o):
        return nr // 4 + lax.rem(o + row, owners)

    def piece(x, r):
        index = x * owners + r - nr // 4
        return pl.ds(pl.multiple_of(index * share, share), share)

    def side(b):
        return jnp.where(chip == 0, core, b)

    def slot(b):
        return jnp.where(chip == 0, b, core)

    def scatter_cross(b, d, o):
        return remote(
            cross.at[b, piece(there(d), target(o))], land.at[slot(b), chip, row],
            e_send.at[b, d, o], e_recv.at[slot(b), chip, row],
            cols=there(d) * 2 + side(b), rows=target(o),
        )

    def scatter_near(act):
        for o in range(owners):
            for b in range(2):
                same = jnp.logical_and(side(b) == core, target(o) == row)

                @pl.when(jnp.logical_not(same))
                def _():
                    act(scatter_cross(b, 0, o))

    def arrive_cross(i, x, r):
        return remote(
            cross.at[i, pl.ds(0, share)], land.at[i, x, r],
            e_send.at[i, 0, 0], e_recv.at[i, x, r], cols=sibling,
        )

    def spread_cross(d, k):
        at = gram_ref.at[2 + core, pl.ds(0, 2), piece(chip, row)]
        return remote(
            at, at, f_send.at[d, k], f_recv.at[chip, row - nr // 4],
            cols=there(d) * 2 + core, rows=peer(k),
        )

    def arrive_spread(x, o):
        at = gram_ref.at[2 + core, pl.ds(0, 2), piece(x, nr // 4 + o)]
        return remote(at, at, f_send.at[0, 0], f_recv.at[x, o], cols=sibling)

    def pass_cross(x):
        at = gram_ref.at[2 + core, pl.ds(0, 2), pl.ds(x * (width // 2), width // 2)]
        return remote(at, at, d_send.at[3 + x], d_recv.at[3 + x], cols=sibling)

    tell(0)
    for n in range(CHUNKS):
        start(swap(n))
    for n in range(2):
        start(pair(n))

    step = rows // 4
    total = None
    for n in range(4):
        x = split(all_ref[me, pl.ds(n * step, step)])
        product = tall(x, x)
        total = product if total is None else total + product
    flat[0] = total
    inner = len(bits) - 1
    for n in range(inner):
        hear(n)
        tell(n + 1)
    total = None
    for n in range(4):
        if n % 2 == 0:
            pair(n // 2).wait_recv()
        at = pl.ds(n * step, step)
        product = tall(split(all_ref[chip * 2, at]), split(all_ref[chip * 2 + 1, at]))
        total = product if total is None else total + product
    flat[1] = total
    for k in range(nr):
        stage[k, : 2 * fine] = flat[0, 2 * fine * k : 2 * fine * (k + 1)]
        at = pl.multiple_of(core * (width // 2) + k * fine, fine)
        stage[k, 2 * fine :] = flat[1, pl.ds(at, fine)]
    for k in range(1, nr):
        start(scatter(k))
    hear(inner)
    tell(inner + 1)
    hear(inner + 1)

    totals = [None, None]
    def keep(block, at):
        high_ref[block, at], low_ref[block, at] = split(all_ref[block, at])

    for n in range(CHUNKS):
        swap(n).wait_recv()
        at = span(chip, n)
        for b in range(2):
            left = all_ref[jnp.where(chip == 0, b, far), at]
            right = all_ref[jnp.where(chip == 0, far, 2 + b), at]
            product = tall(split(left), split(right))
            totals[b] = product if n == 0 else totals[b] + product
    for b in range(2):
        cross[b] = totals[b]
    for o in range(owners):
        for b in range(2):
            start(scatter_cross(b, 1, o))
    scatter_near(lambda copy: copy.start())
    for n in range(CHUNKS, CHUNKS + SOON):
        start(swap(n))

    sums = stage[row]
    for k in range(1, nr):
        scatter(k).wait_recv()
        sums += early[k - 1]
    near[me, row] = sums
    for k in range(1, nr):
        start(spread(k))
    for n in range(CHUNKS):
        start(relay(n))
    for block in (me, sibling):
        keep(block, pl.ds(0, rows))
    for n in range(CHUNKS):
        keep(far, span(chip, n))

    @pl.when(owner)
    def _():
        for b in range(2):

            @pl.when(side(b) == core)
            def _():
                land[slot(b), chip, row] = cross[b, piece(chip, row)]

        for i in range(2):
            sums = None
            for x in range(2):
                for r in range(nr):
                    same = jnp.logical_and(row == r, chip == x)
                    if x == 1:
                        same = jnp.logical_and(same, core == i)

                    @pl.when(jnp.logical_not(same))
                    def _():
                        arrive_cross(i, x, r).wait_recv()

            for x in range(2):
                for r in range(nr):
                    sums = land[i, x, r] if sums is None else sums + land[i, x, r]
            gram_ref[2 + core, i, piece(chip, row)] = sums
        for k in range(nr - 1, -1, -1):
            for d in (1, 0):
                if d or k:
                    spread_cross(d, k).start()

    for k in range(1, nr):
        spread(k).wait_recv()
    start(forward(0))
    start(forward(1))

    for n in range(CHUNKS + SOON, CHUNKS + LATE):
        start(swap(n))
    forward(0).wait_recv()
    start(forward(2))
    for n in range(CHUNKS, CHUNKS + SOON):
        swap(n).wait_recv()
        start(relay(n))
    forward(1).wait_recv()
    forward(2).wait_recv()
    for n in range(CHUNKS):
        relay(n).wait_recv()
        keep(away, span(chip, n))
    for n in range(CHUNKS, CHUNKS + SOON):
        keep(far, span(1 - chip, n))
    for block in range(4):
        gram_ref[block, block] = near[block, :, : 2 * fine].reshape(width, width)
    for c in range(2):
        both = [near[2 * c + i, :, 2 * fine :].reshape(width // 2, width) for i in range(2)]
        both = cat(both, 0)
        gram_ref[2 * c + 1, 2 * c] = both
        gram_ref[2 * c, 2 * c + 1] = both.T

    for x in range(2):
        for o in range(owners):

            @pl.when(jnp.logical_not(jnp.logical_and(chip == x, row == nr // 4 + o)))
            def _():
                arrive_spread(x, o).wait_recv()

        start(pass_cross(x))
    for x in range(2):
        pass_cross(x).wait_recv()
    for i in range(2):
        for j in range(2):
            gram_ref[i, 2 + j] = gram_ref[2 + j, i].T

    def late():
        for n in range(CHUNKS + SOON, CHUNKS + LATE):
            swap(n).wait_recv()
            start(relay(n))

    def ready():
        for n in range(CHUNKS + SOON, CHUNKS + LATE):
            keep(far, span(1 - chip, n))
        for n in range(CHUNKS, CHUNKS + LATE):
            relay(n).wait_recv()
            keep(away, span(1 - chip, n))

    plan_copy.wait()
    rotate4(masks_ref, me, gram_ref, high_ref, low_ref, out_ref, late, ready)
    for copy in started:
        copy.wait_send()
    scatter_near(lambda copy: copy.wait_send())

    @pl.when(owner)
    def _():
        for k in range(nr):
            for d in range(2):
                if d or k:
                    spread_cross(d, k).wait_send()


def local4(nr, snapshots, plan):
    rows, width = snapshots.shape
    fine = width // (2 * nr)
    dma = pltpu.SemaphoreType.DMA
    return pl.pallas_call(
        functools.partial(kernel4, nr),
        out_shape=jax.ShapeDtypeStruct((rows, width), jnp.float32),
        in_specs=[HBM, HBM],
        out_specs=VMEM,
        scratch_shapes=[
            pltpu.VMEM((4, rows, width), jnp.float32),
            pltpu.VMEM((4, 4, width, width), jnp.float32),
            pltpu.VMEM((2, width, width), jnp.float32),
            pltpu.VMEM((2, width, width), jnp.float32),
            pltpu.VMEM((nr, 3 * fine, width), jnp.float32),
            pltpu.VMEM((nr - 1, 3 * fine, width), jnp.float32),
            pltpu.VMEM((4, nr, 3 * fine, width), jnp.float32),
            pltpu.VMEM((2, 2, nr, width // nr, width), jnp.float32),
            pltpu.VMEM((4, rows, width), jnp.bfloat16), pltpu.VMEM((4, rows, width), jnp.bfloat16),
            pltpu.SMEM(plan.shape, jnp.int32), dma((2,)),
            pltpu.SemaphoreType.REGULAR((nr.bit_length(),)),
            dma((CHUNKS + LATE,)), dma((CHUNKS + LATE,)),
            dma((2,)), dma((2,)),
            dma((CHUNKS + LATE,)), dma((CHUNKS + LATE,)),
            dma((nr - 1,)), dma((nr - 1,)),
            dma((nr - 1,)), dma((nr - 1,)),
            dma((5,)), dma((5,)),
            dma((2, 2, nr // 2)), dma((2, 2, nr)),
            dma((2, nr)), dma((2, nr // 2)),
        ],
        compiler_params=pltpu.CompilerParams(
            collective_id=0, has_side_effects=True, vmem_limit_bytes=53 * 2**20
        ),
    )(plan, snapshots)


def local(nb, nr, snapshots, plan):
    rows, width = snapshots.shape
    chips = nb // 2
    dma = pltpu.SemaphoreType.DMA
    return pl.pallas_call(
        functools.partial(kernel, nb, nr),
        out_shape=jax.ShapeDtypeStruct((rows, width), jnp.float32),
        in_specs=[SMEM, VMEM],
        out_specs=VMEM,
        scratch_shapes=[
            pltpu.VMEM((nb, rows, width), jnp.float32),
            pltpu.VMEM((nb, nb, width, width), jnp.float32),
            pltpu.VMEM((nb * width, width), jnp.float32),
            pltpu.VMEM((chips, nr - 1, 2 * width // nr, width), jnp.float32),
            dma((chips, 2, 4)), dma((chips, 2, 4)),
            dma((chips, nr - 1)), dma((chips, nr - 1)),
            dma((chips, nr - 1)), dma((chips, nr - 1)),
            dma((chips, 2, chips)), dma((chips, 2, chips)),
        ],
        compiler_params=pltpu.CompilerParams(
            collective_id=0, has_side_effects=True, vmem_limit_bytes=48 * 2**20
        ),
    )(plan, snapshots)


def solution(mesh):
    nb, nr = mesh.shape["cols"], mesh.shape["rows"]
    four = nb == 4 and nr >= 4 and nr & (nr - 1) == 0
    body = functools.partial(local4, nr) if four else functools.partial(local, nb, nr)
    return jax.shard_map(
        body,
        mesh=mesh,
        in_specs=(P("rows", "cols"), P()),
        out_specs=P("rows", "cols"),
        check_vma=False,
    )
```

```python
import functools

import jax
import jax.numpy as jnp
from jax import lax
from jax.experimental import pallas as pl
from jax.experimental.pallas import tpu as pltpu
from jax.sharding import PartitionSpec as P

NSI = 5
EPS = 1e-6
VMEM = pl.BlockSpec(memory_space=pltpu.VMEM)
MESH = pl.DeviceIdType.MESH
SMEM = pl.BlockSpec(memory_space=pltpu.SMEM)
HBM = pl.BlockSpec(memory_space=pltpu.HBM)


def split(x):
    high = x.astype(jnp.bfloat16)
    return high, (x - high.astype(jnp.float32)).astype(jnp.bfloat16)


def dots(a, b, ca=1, cb=0):
    def one(x, y):
        return lax.dot_general(
            x, y, (((ca,), (cb,)), ((), ())), preferred_element_type=jnp.float32
        )

    return one(a[0], b[0]) + (one(a[0], b[1]) + one(a[1], b[0]))


def dot(a, b, ca=1, cb=0):
    return dots(split(a), split(b), ca, cb)


def columns(gens):
    width = gens[0].shape[0]
    row = lax.broadcasted_iota(jnp.int32, (width, width), 0)
    col = lax.broadcasted_iota(jnp.int32, (width, width), 1)
    eye = jnp.where(row == col, 1.0, 0.0).astype(jnp.float32)
    parts = [split(g) for g in gens]
    zs = [0.5 * (eye + dots(p, p, 1, 1)) for p in parts]
    qs = None
    for index in range(NSI):
        ts = [1.5 * eye - 0.5 * z for z in zs]
        tsp = [split(t) for t in ts]
        if qs is None:
            qs = [t * (0.5**0.5) for t in ts]
        else:
            qs = [dots(split(q), t) for q, t in zip(qs, tsp)]
        if index < NSI - 1:
            squares = [dots(t, t) for t in tsp]
            zs = [dot(z, s) for z, s in zip(zs, squares)]
    return [(q, dots(p, split(q), 0, 0)) for q, p in zip(qs, parts)]


def generator(cross, own, other, sign):
    width = cross.shape[0]
    row = lax.broadcasted_iota(jnp.int32, (width, width), 0)
    col = lax.broadcasted_iota(jnp.int32, (width, width), 1)
    diag = row == col
    dc = jnp.sum(jnp.where(diag, own, 0.0), axis=1, keepdims=True)
    dp = jnp.sum(jnp.where(diag, other, 0.0), axis=0, keepdims=True)
    dc = jnp.maximum(dc, 0.0) + EPS
    dp = jnp.maximum(dp, 0.0) + EPS
    cross = cross * (lax.rsqrt(dc) * lax.rsqrt(dp))
    total = jnp.sum(jnp.sum(cross * cross, axis=1, keepdims=True), axis=0, keepdims=True)
    return cross * (sign * lax.rsqrt(1.0 + total))


def rotate(nb, plan_ref, label, gram_ref, all_ref, out_ref):
    width = out_ref.shape[1]
    masks = [plan_ref[s] for s in range(3)]
    labels = []
    for slot in range(8):
        block = label
        for bit in range(3):
            if slot >> bit & 1:
                block = jnp.bitwise_xor(block, masks[bit])
        labels.append(block)

    def sign(i, j):
        return jnp.where(labels[i] < labels[j], 1.0, -1.0).astype(jnp.float32)

    loaded = {}

    def gram(i, j):
        if (i, j) not in loaded:
            loaded[i, j] = gram_ref[labels[j], labels[i]]
        return loaded[i, j]

    def stack(parts, axis):
        return jnp.concatenate(parts, axis=axis)

    outs = (0, 2, 4, 6)
    gens = [generator(gram(i, i + 1), gram(i, i), gram(i + 1, i + 1), sign(i, i + 1)) for i in outs]
    first = columns(gens)
    col = {i: split(stack(c, 0)) for i, c in zip(outs, first)}
    after = {}
    for i in outs:
        for j in outs:
            if j < i:
                continue
            wide = stack(
                [stack([gram(i + p, j), gram(i + p, j + 1)], 1) for p in (0, 1)], 0
            )
            half = dots(split(wide), col[j])
            after[i, j] = dots(col[i], split(half), 0, 0)

    gens = [generator(after[i, i + 2], after[i, i], after[i + 2, i + 2], sign(i, i + 2)) for i in (0, 4)]
    second = columns(gens)
    c0, c4 = [split(stack(c, 0)) for c in second]

    def block(i, j):
        return stack(
            [
                stack([after[i, j], after[i, j + 2]], 1),
                stack([after[i + 2, j] if i + 2 <= j else after[j, i + 2].T, after[i + 2, j + 2]], 1),
            ],
            0,
        )

    def update(ci, mat, cj):
        return dots(ci, split(dots(split(mat), cj)), 0, 0)

    g00 = update(c0, block(0, 0), c0)
    g04 = update(c0, block(0, 4), c4)
    g44 = update(c4, block(4, 4), c4)
    gens = [generator(g04, g00, g44, sign(0, 4))]
    (a, b), = columns(gens)
    top = dots(c0, split(a))
    bottom = dots(c4, split(b))
    weight = {0: top[:width], 2: top[width:], 4: bottom[:width], 6: bottom[width:]}
    coef = {}
    for i in outs:
        both = dots(col[i], split(weight[i]))
        coef[i], coef[i + 1] = both[:width], both[width:]
    coefs = [split(coef[k]) for k in range(8)]
    rows = out_ref.shape[0]
    tile = min(rows, 256)

    for at in range(0, rows, tile):
        total = jnp.zeros((tile, width), jnp.float32)
        for k in range(len(coefs)):
            total += dots(split(all_ref[labels[k], at : at + tile]), coefs[k])
        out_ref[at : at + tile, :] = total


def cat(parts, axis):
    return jnp.concatenate(parts, axis=axis)


def one(a, b, cb=0):
    return lax.dot_general(
        a, b, (((1,), (cb,)), ((), ())), preferred_element_type=jnp.float32
    )


def wide(a, b, cb=0):
    return one(cat([a[0], a[1], a[0]], 1), cat([b[0], b[0], b[1]], cb), cb)


def eyes(width):
    row = lax.broadcasted_iota(jnp.int32, (width, width), 0)
    col = lax.broadcasted_iota(jnp.int32, (width, width), 1)
    return row == col


def normal(cross, own, other, sign):
    diag = eyes(cross.shape[0])
    dc = jnp.sum(jnp.where(diag, own, 0.0), axis=1, keepdims=True)
    dp = jnp.sum(jnp.where(diag, other, 0.0), axis=0, keepdims=True)
    dc = jnp.maximum(dc, 0.0) + EPS
    dp = jnp.maximum(dp, 0.0) + EPS
    cross = cross * (lax.rsqrt(dc) * lax.rsqrt(dp))
    total = jnp.sum(jnp.sum(cross * cross, axis=0, keepdims=True), axis=1, keepdims=True)
    return cross, sign * lax.rsqrt(1.0 + total)


def rows_of_rotations(pairs):
    width = pairs[0][0].shape[0]
    eye = jnp.where(eyes(width), 1.0, 0.0).astype(jnp.float32)
    parts = [split(c) for c, _ in pairs]
    squares = [wide(p, p, 1) for p in parts]
    es = [0.5 * eye - (0.5 * a * a) * s for (_, a), s in zip(pairs, squares)]
    gs = [a * c for c, a in pairs]
    ep = [split(e) for e in es]
    boths = [wide(p, [cat([x, y], 1) for x, y in zip(p, split(g))]) for p, g in zip(ep, gs)]
    ys = [
        (0.5**0.5) * cat([eye + 0.5 * e, g + 0.5 * b[:, width:]], 1)
        for e, g, b in zip(es, gs, boths)
    ]
    fs = [b[:, :width] for b in boths]
    es = [0.75 * f + 0.25 * wide(split(f), p) for f, p in zip(fs, ep)]
    ep = [split(e) for e in es]
    boths = [wide(p, [cat([x, z], 1) for x, z in zip(p, split(y))]) for p, y in zip(ep, ys)]
    ys = [y + 0.5 * b[:, width:] for y, b in zip(ys, boths)]
    fs = [b[:, :width] for b in boths]
    es = [0.75 * f + 0.25 * one(f.astype(jnp.bfloat16), p[0]) for f, p in zip(fs, ep)]
    ep = [split(e) for e in es]
    fs = [one(p[0], p[0]) for p in ep]
    ys = [y + 0.5 * wide(p, split(y)) for y, p in zip(ys, ep)]
    es = [0.75 * f + 0.25 * one(f.astype(jnp.bfloat16), p[0]) for f, p in zip(fs, ep)]
    eh = [e.astype(jnp.bfloat16) for e in es]
    fs = [one(h, h) for h in eh]
    ys = [y + 0.5 * one(h, y.astype(jnp.bfloat16)) for y, h in zip(ys, eh)]
    last = [
        (0.5 * (0.75 * f + 0.25 * one(f.astype(jnp.bfloat16), h))).astype(jnp.bfloat16)
        for f, h in zip(fs, eh)
    ]
    return ys, last


def finish(x, last):
    return x + one(last, x.astype(jnp.bfloat16))


def rotate4(plan_ref, label, gram_ref, high_ref, low_ref, out_ref):
    width = out_ref.shape[1]
    masks = [plan_ref[s] for s in range(2)]
    labels = [label, jnp.bitwise_xor(label, masks[0]), jnp.bitwise_xor(label, masks[1])]
    labels.append(jnp.bitwise_xor(labels[1], masks[1]))

    def sign(i, j):
        return jnp.where(labels[i] < labels[j], 1.0, -1.0).astype(jnp.float32)

    def grid(blocks):
        return cat([cat(line, 1) for line in blocks], 0)

    first = [[gram_ref[labels[j], labels[i]] for j in range(4)] for i in range(4)]
    pairs = [normal(first[i][i ^ 1], first[i][i], first[i ^ 1][i ^ 1], sign(i, i ^ 1)) for i in range(4)]
    ys, last = rows_of_rotations(pairs)
    ys = [cat([y[:, width:], y[:, :width]], 1) if i % 2 else y for i, y in enumerate(ys)]
    turned = []
    lines = []
    for p in range(2):
        slab = split(grid([first[2 * p], first[2 * p + 1]]))
        top = wide(split(cat(ys[2 * p : 2 * p + 2], 0)), slab)
        top = cat([finish(top[:width], last[2 * p]), finish(top[width:], last[2 * p + 1])], 0)
        lines.append(split(top))
        turned.append(split(cat([finish(ys[2 * p + c], last[2 * p + c]) for c in (0, 1)], 0)))
    after = [[None] * 4 for _ in range(4)]
    for p in range(2):
        for q in range(2):
            cut = slice(2 * q * width, 2 * (q + 1) * width)
            block = wide([x[:, cut] for x in lines[p]], turned[q], 1)
            for i in range(2):
                for j in range(2):
                    at = slice(i * width, (i + 1) * width), slice(j * width, (j + 1) * width)
                    after[2 * p + i][2 * q + j] = block[at]
    own, far = (0, 2), (3, 1)
    pairs = [normal(after[i][j], after[i][i], after[j][j], sign(i, j)) for i, j in (own, far)]
    ys, last = rows_of_rotations(pairs)
    slab = split(grid([[after[i][j] for j in own + far] for i in own]))
    line0 = split(finish(wide(split(ys[0]), slab), last[0]))
    slab = split(grid([[after[i][j] for j in far] for i in far]))
    line3 = split(finish(wide(split(ys[1]), slab), last[1]))
    c0, c3 = [split(finish(y, e)) for y, e in zip(ys, last)]
    g00 = wide([x[:, : 2 * width] for x in line0], c0, 1)
    g03 = wide([x[:, 2 * width :] for x in line0], c3, 1)
    g33 = wide(line3, c3, 1)
    ys, last = rows_of_rotations([normal(g03, g00, g33, sign(0, 3))])

    def row(slot):
        at = slice(slot % 2 * width, (slot % 2 + 1) * width)
        return [x[at] for x in turned[slot // 2]]

    def piece(c, half, slot):
        return wide([x[:, half * width : (half + 1) * width] for x in c], row(slot))

    mixed = split(
        grid([[piece(c0, 0, 0), piece(c0, 1, 2)], [piece(c3, 1, 1), piece(c3, 0, 3)]])
    )
    coef = split(finish(wide(split(ys[0]), mixed), last[0]))
    rows = out_ref.shape[0]
    tile = min(rows, 512)
    for at in range(0, rows, tile):
        line = [
            cat([ref[labels[k], at : at + tile] for k in range(4)], 1) for ref in (high_ref, low_ref)
        ]
        both = one(line[0], cat(coef, 0), 1)
        out_ref[at : at + tile, :] = both[:, :width] + (both[:, width:] + one(line[1], coef[0], 1))


def kernel(nb, nr, plan_ref, own_ref, out_ref, all_ref, gram_ref, part, land, *sems):
    a_send, a_recv, b_send, b_recv, c_send, c_recv, d_send, d_recv = sems
    me, row = lax.axis_index("cols"), lax.axis_index("rows")
    chips = nb // 2
    chip, core = me // 2, lax.rem(me, 2)
    sibling = chip * 2 + (1 - core)
    rows, width = own_ref.shape
    piece = 2 * width // nr
    far = range(1, chips)
    chunks = a_send.shape[2]
    size = rows // chunks

    def ahead(d):
        return lax.rem(chip + d, chips)

    def behind(d):
        return lax.rem(chip + 2 * chips - d, chips)

    def peer(k):
        return lax.rem(row + k, nr)

    barrier = pltpu.get_barrier_semaphore()
    targets = [{"cols": sibling}] + [{"cols": ahead(d) * 2 + core} for d in far]
    targets += [{"rows": peer(k)} for k in range(1, nr)]
    for target in targets:
        pl.semaphore_signal(barrier, inc=1, device_id=target, device_id_type=MESH)
    pl.semaphore_wait(barrier, len(targets))

    started = []

    def start(copy):
        copy.start()
        started.append(copy)

    def copies(ref, source, send, recv, at):
        def direct(d, n):
            return pltpu.make_async_remote_copy(
                source.at[at(0, n)], ref.at[me, at(0, n)], send.at[d, 0, n], recv.at[d, 0, n],
                device_id={"cols": ahead(d) * 2 + core}, device_id_type=MESH,
            )

        def relay(d, n):
            block = behind(d) * 2 + core
            return pltpu.make_async_remote_copy(
                source.at[at(0, n)] if d == 0 else ref.at[block, at(d, n)], ref.at[block, at(d, n)],
                send.at[d, 1, n], recv.at[d, 1, n],
                device_id={"cols": sibling}, device_id_type=MESH,
            )

        return direct, relay

    def group(d, n):
        return pl.ds(behind(d + n) * 2, 2)

    direct, relay = copies(all_ref, own_ref, a_send, a_recv, lambda d, n: pl.ds(n * size, size))
    far_panel, near_panel = copies(gram_ref, gram_ref.at[me], d_send, d_recv, group)

    def multiply(block, ch):
        at = pl.ds(ch * size, size)
        to = pl.ds(pl.multiple_of(block * width, width), width)
        product = dot(all_ref[block, at, :], own_ref[at, :], 0, 0)
        if ch == 0:
            part[to, :] = product
        else:
            part[to, :] += product

    def rows_of(g, r):
        return pl.ds(pl.multiple_of(behind(g) * (2 * width) + r * piece, piece), piece)

    def place(g):
        half = nr // 2
        at = pl.ds(pl.multiple_of(lax.rem(row, half) * piece, piece), piece)
        return gram_ref.at[me, behind(g) * 2 + row // half, at]

    def scatter(g, k):
        return pltpu.make_async_remote_copy(
            part.at[rows_of(g, peer(k))], land.at[g, k - 1],
            b_send.at[g, k - 1], b_recv.at[g, k - 1],
            device_id={"rows": peer(k)}, device_id_type=MESH,
        )

    def spread(g, k):
        return pltpu.make_async_remote_copy(
            place(g), place(g),
            c_send.at[g, k - 1], c_recv.at[g, k - 1],
            device_id={"rows": peer(k)}, device_id_type=MESH,
        )

    def send_group(g):
        for k in range(1, nr):
            start(scatter(g, k))

    def sum_group(g):
        total = part[rows_of(g, row), :]
        for k in range(1, nr):
            scatter(g, k).wait_recv()
            total += land[g, k - 1]
        place(g)[...] = total
        for k in range(1, nr):
            start(spread(g, k))

    def share_group(g):
        for k in range(1, nr):
            spread(g, k).wait_recv()
        for d in far:
            start(far_panel(d, g))
        start(near_panel(0, g))

    for ch in range(chunks):
        for d in far:
            start(direct(d, ch))
    for ch in range(chunks):
        start(relay(0, ch))
    all_ref[me] = own_ref[...]
    for ch in range(chunks):
        multiply(me, ch)
    for ch in range(chunks):
        relay(0, ch).wait_recv()
        multiply(sibling, ch)
    send_group(0)
    for ch in range(chunks + 1):
        for d in far:
            if ch < chunks:
                direct(d, ch).wait_recv()
                start(relay(d, ch))
                multiply(behind(d) * 2 + core, ch)
            if ch > 0:
                relay(d, ch - 1).wait_recv()
                multiply(behind(d) * 2 + 1 - core, ch - 1)
        if ch == chunks - 2:
            sum_group(0)
    for g in far:
        send_group(g)
    share_group(0)
    for g in far:
        sum_group(g)
    for g in far:
        share_group(g)
    for g in range(chips):
        for d in far:
            far_panel(d, g).wait_recv()
            start(near_panel(d, g))
    for g in range(chips):
        for d in range(chips):
            near_panel(d, g).wait_recv()
    rotate(nb, plan_ref, me, gram_ref, all_ref, out_ref)
    for copy in started:
        copy.wait_send()


CHUNKS = 4
LATE = 2


def tall(a, b):
    return lax.dot_general(
        cat([a[0], a[1], a[0]], 0), cat([b[0], b[0], b[1]], 0),
        (((0,), (0,)), ((), ())), preferred_element_type=jnp.float32,
    )


def kernel4(
    nr, plan_ref, own_ref, out_ref, all_ref, gram_ref, flat, cross, stage, early, near, land, high_ref, low_ref,
    masks_ref, local_sem, hop, *sems
):
    (swap_send, swap_recv, pair_send, pair_recv, relay_send, relay_recv, b_send, b_recv,
     c_send, c_recv, d_send, d_recv, g_send, g_recv, e_send, e_recv, f_send, f_recv) = sems
    me, row = lax.axis_index("cols"), lax.axis_index("rows")
    chip, core = me // 2, lax.rem(me, 2)
    sibling = chip * 2 + 1 - core
    far = (1 - chip) * 2 + core
    away = (1 - chip) * 2 + 1 - core
    rows, width = own_ref.shape
    half = rows // 2
    fine = width // (2 * nr)
    owners = nr // 2
    thick = width // nr
    owner = jnp.logical_and(row >= nr // 4, row < nr // 4 + owners)

    def peer(k):
        return lax.rem(row + k, nr)

    def there(d):
        return chip if d == 0 else 1 - chip

    def remote(source, target, send, recv, **device):
        return pltpu.make_async_remote_copy(
            source, target, send, recv, device_id=device, device_id_type=MESH
        )

    bits = [1 << n for n in range(nr.bit_length() - 1)]
    ways = [{"rows": jnp.bitwise_xor(row, bit)} for bit in bits[:-1]]
    ways += [{"cols": sibling}, {"cols": far}]
    first = ways + [{"rows": jnp.bitwise_xor(row, bits[-1])}]
    barrier = pltpu.get_barrier_semaphore()
    for way in first:
        pl.semaphore_signal(barrier, inc=1, device_id=way, device_id_type=MESH)
    plan_copy = pltpu.make_async_copy(plan_ref, masks_ref, local_sem.at[0])
    plan_copy.start()
    own_copy = pltpu.make_async_copy(own_ref, all_ref.at[me], local_sem.at[1])
    own_copy.start()
    own_copy.wait()
    pl.semaphore_wait(barrier, len(first))

    def tell(n):
        pl.semaphore_signal(hop.at[n], inc=1, device_id=ways[n], device_id_type=MESH)

    def hear(n):
        pl.semaphore_wait(hop.at[n], 1)

    started = []

    def start(copy):
        copy.start()
        started.append(copy)

    sizes = [half // CHUNKS] * CHUNKS + [half // LATE] * LATE
    offsets = [n * (half // CHUNKS) for n in range(CHUNKS)] + [n * (half // LATE) for n in range(LATE)]

    def span(side, n):
        at = side * half + offsets[n]
        return pl.ds(pl.multiple_of(at, 8), sizes[n])

    def swap(n):
        at = span(1 - chip if n < CHUNKS else chip, n)
        return remote(
            all_ref.at[me, at], all_ref.at[me, at], swap_send.at[n], swap_recv.at[n], cols=far
        )

    def relay(n):
        at = span(chip if n < CHUNKS else 1 - chip, n)
        return remote(
            all_ref.at[far, at], all_ref.at[far, at], relay_send.at[n], relay_recv.at[n],
            cols=sibling,
        )

    def pair(n):
        at = pl.ds(n * half, half)
        return remote(
            all_ref.at[me, at], all_ref.at[me, at], pair_send.at[n], pair_recv.at[n], cols=sibling
        )

    def scatter(k):
        return remote(
            stage.at[peer(k)], early.at[k - 1], b_send.at[k - 1], b_recv.at[k - 1], rows=peer(k)
        )

    def spread(k):
        return remote(
            near.at[me, row], near.at[me, row], c_send.at[k - 1], c_recv.at[k - 1], rows=peer(k)
        )

    def forward(k):
        at = near.at[me, lax.rem(row - k + nr, nr)]
        return remote(at, at, g_send.at[k], g_recv.at[k], cols=far)

    def share(n):
        at = near.at[me if n == 0 else far]
        return remote(at, at, d_send.at[n], d_recv.at[n], cols=sibling)

    def target(o):
        return nr // 4 + lax.rem(o + row, owners)

    def piece(x, r):
        index = x * owners + r - nr // 4
        return pl.ds(pl.multiple_of(index * thick, thick), thick)

    def side(b):
        return jnp.where(chip == 0, core, b)

    def slot(b):
        return jnp.where(chip == 0, b, core)

    def scatter_cross(b, d, o):
        return remote(
            cross.at[b, piece(there(d), target(o))], land.at[slot(b), chip, row],
            e_send.at[b, d, o], e_recv.at[slot(b), chip, row],
            cols=there(d) * 2 + side(b), rows=target(o),
        )

    def scatter_near(act):
        for o in range(owners):
            for b in range(2):
                same = jnp.logical_and(side(b) == core, target(o) == row)

                @pl.when(jnp.logical_not(same))
                def _():
                    act(scatter_cross(b, 0, o))

    def arrive_cross(i, x, r):
        return remote(
            cross.at[i, pl.ds(0, thick)], land.at[i, x, r],
            e_send.at[i, 0, 0], e_recv.at[i, x, r], cols=sibling,
        )

    def spread_cross(d, k):
        at = gram_ref.at[2 + core, pl.ds(0, 2), piece(chip, row)]
        return remote(
            at, at, f_send.at[d, k], f_recv.at[chip, row - nr // 4],
            cols=there(d) * 2 + core, rows=peer(k),
        )

    def arrive_spread(x, o):
        at = gram_ref.at[2 + core, pl.ds(0, 2), piece(x, nr // 4 + o)]
        return remote(at, at, f_send.at[0, 0], f_recv.at[x, o], cols=sibling)

    def pass_cross(x):
        at = gram_ref.at[2 + core, pl.ds(0, 2), pl.ds(x * (width // 2), width // 2)]
        return remote(at, at, d_send.at[2 + x], d_recv.at[2 + x], cols=sibling)

    tell(0)
    for n in range(CHUNKS):
        start(swap(n))
    for n in range(2):
        start(pair(n))

    step = rows // 4
    total = None
    for n in range(4):
        x = split(all_ref[me, pl.ds(n * step, step)])
        product = tall(x, x)
        total = product if total is None else total + product
    flat[0] = total
    inner = len(bits) - 1
    for n in range(inner):
        hear(n)
        tell(n + 1)
    total = None
    for n in range(4):
        if n % 2 == 0:
            pair(n // 2).wait_recv()
        at = pl.ds(n * step, step)
        product = tall(split(all_ref[chip * 2, at]), split(all_ref[chip * 2 + 1, at]))
        total = product if total is None else total + product
    flat[1] = total
    for k in range(nr):
        stage[k, : 2 * fine] = flat[0, 2 * fine * k : 2 * fine * (k + 1)]
        at = pl.multiple_of(core * (width // 2) + k * fine, fine)
        stage[k, 2 * fine :] = flat[1, pl.ds(at, fine)]
    for k in range(1, nr):
        start(scatter(k))
    hear(inner)
    tell(inner + 1)
    hear(inner + 1)

    totals = [None, None]

    def keep(block, at):
        high_ref[block, at], low_ref[block, at] = split(all_ref[block, at])

    for n in range(CHUNKS):
        swap(n).wait_recv()
        at = span(chip, n)
        for b in range(2):
            left = all_ref[jnp.where(chip == 0, b, far), at]
            right = all_ref[jnp.where(chip == 0, far, 2 + b), at]
            product = tall(split(left), split(right))
            totals[b] = product if n == 0 else totals[b] + product
    for b in range(2):
        cross[b] = totals[b]
    for o in range(owners):
        for b in range(2):
            start(scatter_cross(b, 1, o))
    scatter_near(lambda copy: copy.start())
    for n in range(CHUNKS, CHUNKS + LATE):
        start(swap(n))

    sums = stage[row]
    for k in range(1, nr):
        scatter(k).wait_recv()
        sums += early[k - 1]
    near[me, row] = sums
    for k in range(1, nr):
        start(spread(k))
    start(forward(0))
    for n in range(CHUNKS):
        start(relay(n))
    for block in (me, sibling):
        keep(block, pl.ds(0, rows))
    for n in range(CHUNKS):
        keep(far, span(chip, n))

    @pl.when(owner)
    def _():
        for b in range(2):

            @pl.when(side(b) == core)
            def _():
                land[slot(b), chip, row] = cross[b, piece(chip, row)]

        for i in range(2):
            sums = None
            for x in range(2):
                for r in range(nr):
                    same = jnp.logical_and(row == r, chip == x)
                    if x == 1:
                        same = jnp.logical_and(same, core == i)

                    @pl.when(jnp.logical_not(same))
                    def _():
                        arrive_cross(i, x, r).wait_recv()

            for x in range(2):
                for r in range(nr):
                    sums = land[i, x, r] if sums is None else sums + land[i, x, r]
            gram_ref[2 + core, i, piece(chip, row)] = sums
        for k in range(nr - 1, -1, -1):
            for d in (1, 0):
                if d or k:
                    spread_cross(d, k).start()

    for k in range(1, nr):
        spread(k).wait_recv()
        start(forward(k))
    start(share(0))

    for n in range(CHUNKS, CHUNKS + LATE):
        swap(n).wait_recv()
        start(relay(n))
    for k in range(nr):
        forward(k).wait_recv()
    start(share(1))
    for n in range(CHUNKS, CHUNKS + LATE):
        keep(far, span(1 - chip, n))
    for n in range(CHUNKS + LATE):
        relay(n).wait_recv()
        keep(away, span(chip if n < CHUNKS else 1 - chip, n))
    for x in range(2):
        for o in range(owners):

            @pl.when(jnp.logical_not(jnp.logical_and(chip == x, row == nr // 4 + o)))
            def _():
                arrive_spread(x, o).wait_recv()

        start(pass_cross(x))
    for n in range(2):
        share(n).wait_recv()
    for block in range(4):
        gram_ref[block, block] = near[block, :, : 2 * fine].reshape(width, width)
    for c in range(2):
        both = [near[2 * c + i, :, 2 * fine :].reshape(width // 2, width) for i in range(2)]
        both = cat(both, 0)
        gram_ref[2 * c + 1, 2 * c] = both
        gram_ref[2 * c, 2 * c + 1] = both.T

    for i in range(2):
        gram_ref[i, 2 + core] = gram_ref[2 + core, i].T
    for x in range(2):
        pass_cross(x).wait_recv()
    for i in range(2):
        gram_ref[i, 3 - core] = gram_ref[3 - core, i].T

    plan_copy.wait()
    rotate4(masks_ref, me, gram_ref, high_ref, low_ref, out_ref)
    for copy in started:
        copy.wait_send()
    scatter_near(lambda copy: copy.wait_send())

    @pl.when(owner)
    def _():
        for k in range(nr):
            for d in range(2):
                if d or k:
                    spread_cross(d, k).wait_send()


def local4(nr, snapshots, plan):
    rows, width = snapshots.shape
    fine = width // (2 * nr)
    dma = pltpu.SemaphoreType.DMA
    return pl.pallas_call(
        functools.partial(kernel4, nr),
        out_shape=jax.ShapeDtypeStruct((rows, width), jnp.float32),
        in_specs=[HBM, HBM],
        out_specs=VMEM,
        scratch_shapes=[
            pltpu.VMEM((4, rows, width), jnp.float32),
            pltpu.VMEM((4, 4, width, width), jnp.float32),
            pltpu.VMEM((2, width, width), jnp.float32),
            pltpu.VMEM((2, width, width), jnp.float32),
            pltpu.VMEM((nr, 3 * fine, width), jnp.float32),
            pltpu.VMEM((nr - 1, 3 * fine, width), jnp.float32),
            pltpu.VMEM((4, nr, 3 * fine, width), jnp.float32),
            pltpu.VMEM((2, 2, nr, width // nr, width), jnp.float32),
            pltpu.VMEM((4, rows, width), jnp.bfloat16), pltpu.VMEM((4, rows, width), jnp.bfloat16),
            pltpu.SMEM(plan.shape, jnp.int32), dma((2,)),
            pltpu.SemaphoreType.REGULAR((nr.bit_length(),)),
            dma((CHUNKS + LATE,)), dma((CHUNKS + LATE,)),
            dma((2,)), dma((2,)),
            dma((CHUNKS + LATE,)), dma((CHUNKS + LATE,)),
            dma((nr - 1,)), dma((nr - 1,)),
            dma((nr - 1,)), dma((nr - 1,)),
            dma((4,)), dma((4,)), dma((nr,)), dma((nr,)),
            dma((2, 2, nr // 2)), dma((2, 2, nr)),
            dma((2, nr)), dma((2, nr // 2)),
        ],
        compiler_params=pltpu.CompilerParams(
            collective_id=0, has_side_effects=True, vmem_limit_bytes=53 * 2**20
        ),
    )(plan, snapshots)


def local(nb, nr, snapshots, plan):
    rows, width = snapshots.shape
    chips = nb // 2
    dma = pltpu.SemaphoreType.DMA
    return pl.pallas_call(
        functools.partial(kernel, nb, nr),
        out_shape=jax.ShapeDtypeStruct((rows, width), jnp.float32),
        in_specs=[SMEM, VMEM],
        out_specs=VMEM,
        scratch_shapes=[
            pltpu.VMEM((nb, rows, width), jnp.float32),
            pltpu.VMEM((nb, nb, width, width), jnp.float32),
            pltpu.VMEM((nb * width, width), jnp.float32),
            pltpu.VMEM((chips, nr - 1, 2 * width // nr, width), jnp.float32),
            dma((chips, 2, 4)), dma((chips, 2, 4)),
            dma((chips, nr - 1)), dma((chips, nr - 1)),
            dma((chips, nr - 1)), dma((chips, nr - 1)),
            dma((chips, 2, chips)), dma((chips, 2, chips)),
        ],
        compiler_params=pltpu.CompilerParams(
            collective_id=0, has_side_effects=True, vmem_limit_bytes=48 * 2**20
        ),
    )(plan, snapshots)


def solution(mesh):
    nb, nr = mesh.shape["cols"], mesh.shape["rows"]
    four = nb == 4 and nr >= 4 and nr & (nr - 1) == 0
    body = functools.partial(local4, nr) if four else functools.partial(local, nb, nr)
    return jax.shard_map(
        body,
        mesh=mesh,
        in_specs=(P("rows", "cols"), P()),
        out_specs=P("rows", "cols"),
        check_vma=False,
    )
```

```python
import functools

import jax
import jax.numpy as jnp
from jax import lax
from jax.experimental import pallas as pl
from jax.experimental.pallas import tpu as pltpu
from jax.sharding import PartitionSpec as P

NSI = 5
EPS = 1e-6
VMEM = pl.BlockSpec(memory_space=pltpu.VMEM)
MESH = pl.DeviceIdType.MESH
SMEM = pl.BlockSpec(memory_space=pltpu.SMEM)
HBM = pl.BlockSpec(memory_space=pltpu.HBM)


def split(x):
    high = x.astype(jnp.bfloat16)
    return high, (x - high.astype(jnp.float32)).astype(jnp.bfloat16)


def dots(a, b, ca=1, cb=0):
    def one(x, y):
        return lax.dot_general(
            x, y, (((ca,), (cb,)), ((), ())), preferred_element_type=jnp.float32
        )

    return one(a[0], b[0]) + (one(a[0], b[1]) + one(a[1], b[0]))


def dot(a, b, ca=1, cb=0):
    return dots(split(a), split(b), ca, cb)


def columns(gens):
    width = gens[0].shape[0]
    row = lax.broadcasted_iota(jnp.int32, (width, width), 0)
    col = lax.broadcasted_iota(jnp.int32, (width, width), 1)
    eye = jnp.where(row == col, 1.0, 0.0).astype(jnp.float32)
    parts = [split(g) for g in gens]
    zs = [0.5 * (eye + dots(p, p, 1, 1)) for p in parts]
    qs = None
    for index in range(NSI):
        ts = [1.5 * eye - 0.5 * z for z in zs]
        tsp = [split(t) for t in ts]
        if qs is None:
            qs = [t * (0.5**0.5) for t in ts]
        else:
            qs = [dots(split(q), t) for q, t in zip(qs, tsp)]
        if index < NSI - 1:
            squares = [dots(t, t) for t in tsp]
            zs = [dot(z, s) for z, s in zip(zs, squares)]
    return [(q, dots(p, split(q), 0, 0)) for q, p in zip(qs, parts)]


def generator(cross, own, other, sign):
    width = cross.shape[0]
    row = lax.broadcasted_iota(jnp.int32, (width, width), 0)
    col = lax.broadcasted_iota(jnp.int32, (width, width), 1)
    diag = row == col
    dc = jnp.sum(jnp.where(diag, own, 0.0), axis=1, keepdims=True)
    dp = jnp.sum(jnp.where(diag, other, 0.0), axis=0, keepdims=True)
    dc = jnp.maximum(dc, 0.0) + EPS
    dp = jnp.maximum(dp, 0.0) + EPS
    cross = cross * (lax.rsqrt(dc) * lax.rsqrt(dp))
    total = jnp.sum(jnp.sum(cross * cross, axis=1, keepdims=True), axis=0, keepdims=True)
    return cross * (sign * lax.rsqrt(1.0 + total))


def rotate(nb, plan_ref, label, gram_ref, all_ref, out_ref):
    width = out_ref.shape[1]
    masks = [plan_ref[s] for s in range(3)]
    labels = []
    for slot in range(8):
        block = label
        for bit in range(3):
            if slot >> bit & 1:
                block = jnp.bitwise_xor(block, masks[bit])
        labels.append(block)

    def sign(i, j):
        return jnp.where(labels[i] < labels[j], 1.0, -1.0).astype(jnp.float32)

    loaded = {}

    def gram(i, j):
        if (i, j) not in loaded:
            loaded[i, j] = gram_ref[labels[j], labels[i]]
        return loaded[i, j]

    def stack(parts, axis):
        return jnp.concatenate(parts, axis=axis)

    outs = (0, 2, 4, 6)
    gens = [generator(gram(i, i + 1), gram(i, i), gram(i + 1, i + 1), sign(i, i + 1)) for i in outs]
    first = columns(gens)
    col = {i: split(stack(c, 0)) for i, c in zip(outs, first)}
    after = {}
    for i in outs:
        for j in outs:
            if j < i:
                continue
            wide = stack(
                [stack([gram(i + p, j), gram(i + p, j + 1)], 1) for p in (0, 1)], 0
            )
            half = dots(split(wide), col[j])
            after[i, j] = dots(col[i], split(half), 0, 0)

    gens = [generator(after[i, i + 2], after[i, i], after[i + 2, i + 2], sign(i, i + 2)) for i in (0, 4)]
    second = columns(gens)
    c0, c4 = [split(stack(c, 0)) for c in second]

    def block(i, j):
        return stack(
            [
                stack([after[i, j], after[i, j + 2]], 1),
                stack([after[i + 2, j] if i + 2 <= j else after[j, i + 2].T, after[i + 2, j + 2]], 1),
            ],
            0,
        )

    def update(ci, mat, cj):
        return dots(ci, split(dots(split(mat), cj)), 0, 0)

    g00 = update(c0, block(0, 0), c0)
    g04 = update(c0, block(0, 4), c4)
    g44 = update(c4, block(4, 4), c4)
    gens = [generator(g04, g00, g44, sign(0, 4))]
    (a, b), = columns(gens)
    top = dots(c0, split(a))
    bottom = dots(c4, split(b))
    weight = {0: top[:width], 2: top[width:], 4: bottom[:width], 6: bottom[width:]}
    coef = {}
    for i in outs:
        both = dots(col[i], split(weight[i]))
        coef[i], coef[i + 1] = both[:width], both[width:]
    coefs = [split(coef[k]) for k in range(8)]
    rows = out_ref.shape[0]
    tile = min(rows, 256)

    for at in range(0, rows, tile):
        total = jnp.zeros((tile, width), jnp.float32)
        for k in range(len(coefs)):
            total += dots(split(all_ref[labels[k], at : at + tile]), coefs[k])
        out_ref[at : at + tile, :] = total


def cat(parts, axis):
    return jnp.concatenate(parts, axis=axis)


def one(a, b, cb=0):
    return lax.dot_general(
        a, b, (((1,), (cb,)), ((), ())), preferred_element_type=jnp.float32
    )


def wide(a, b, cb=0):
    return one(cat([a[0], a[1], a[0]], 1), cat([b[0], b[0], b[1]], cb), cb)


def eyes(width):
    row = lax.broadcasted_iota(jnp.int32, (width, width), 0)
    col = lax.broadcasted_iota(jnp.int32, (width, width), 1)
    return row == col


def squares_of(turn, line):
    return jnp.sum(turn * line, axis=1, keepdims=True)


def strength(cross, sign):
    total = jnp.sum(jnp.sum(cross * cross, axis=0, keepdims=True), axis=1, keepdims=True)
    return sign * lax.rsqrt(1.0 + total)


def inverse(square):
    return lax.rsqrt(jnp.maximum(square, 0.0) + EPS)


def normal(cross, own, other, sign):
    dp = jnp.sum(jnp.where(eyes(cross.shape[0]), other, 0.0), axis=0, keepdims=True)
    cross = cross * (inverse(own) * inverse(dp))
    return cross, strength(cross, sign)


def rows_of_rotations(pairs):
    width = pairs[0][0].shape[0]
    eye = jnp.where(eyes(width), 1.0, 0.0).astype(jnp.float32)
    parts = [split(c) for c, _ in pairs]
    squares = [wide(p, p, 1) for p in parts]
    es = [0.5 * eye - (0.5 * a * a) * s for (_, a), s in zip(pairs, squares)]
    gs = [a * c for c, a in pairs]
    ep = [split(e) for e in es]
    boths = [wide(p, [cat([x, y], 1) for x, y in zip(p, split(g))]) for p, g in zip(ep, gs)]
    ys = [
        (0.5**0.5) * cat([eye + 0.5 * e, g + 0.5 * b[:, width:]], 1)
        for e, g, b in zip(es, gs, boths)
    ]
    fs = [b[:, :width] for b in boths]
    es = [0.75 * f + 0.25 * wide(split(f), p) for f, p in zip(fs, ep)]
    ep = [split(e) for e in es]
    boths = [wide(p, [cat([x, z], 1) for x, z in zip(p, split(y))]) for p, y in zip(ep, ys)]
    ys = [y + 0.5 * b[:, width:] for y, b in zip(ys, boths)]
    fs = [b[:, :width] for b in boths]
    es = [0.75 * f + 0.25 * one(f.astype(jnp.bfloat16), p[0]) for f, p in zip(fs, ep)]
    ep = [split(e) for e in es]
    fs = [one(p[0], p[0]) for p in ep]
    ys = [y + 0.5 * wide(p, split(y)) for y, p in zip(ys, ep)]
    es = [0.75 * f + 0.25 * one(f.astype(jnp.bfloat16), p[0]) for f, p in zip(fs, ep)]
    eh = [e.astype(jnp.bfloat16) for e in es]
    fs = [one(h, h) for h in eh]
    ys = [y + 0.5 * one(h, y.astype(jnp.bfloat16)) for y, h in zip(ys, eh)]
    last = [
        (0.5 * (0.75 * f + 0.25 * one(f.astype(jnp.bfloat16), h))).astype(jnp.bfloat16)
        for f, h in zip(fs, eh)
    ]
    return ys, last


def finish(x, last):
    return x + one(last, x.astype(jnp.bfloat16))


def rotate4(plan_ref, label, gram_ref, down_ref, across_ref, high_ref, low_ref, out_ref):
    width = out_ref.shape[1]
    masks = [plan_ref[s] for s in range(2)]
    labels = [label, jnp.bitwise_xor(label, masks[0]), jnp.bitwise_xor(label, masks[1])]
    labels.append(jnp.bitwise_xor(labels[1], masks[1]))

    def sign(i, j):
        return jnp.where(labels[i] < labels[j], 1.0, -1.0).astype(jnp.float32)

    def grid(blocks):
        return cat([cat(line, 1) for line in blocks], 0)

    first = [[gram_ref[labels[j], labels[i]] for j in range(4)] for i in range(4)]
    pairs = []
    for i in range(4):
        scale = down_ref[labels[i]] * across_ref[labels[i ^ 1], :1]
        pairs.append(first[i][i ^ 1] * scale)
    sizes = [strength(pairs[i], sign(i, i ^ 1)) for i in (0, 2)]
    pairs = list(zip(pairs, (sizes[0], -sizes[0], sizes[1], -sizes[1])))
    ys, last = rows_of_rotations(pairs)
    ys = [cat([y[:, width:], y[:, :width]], 1) if i % 2 else y for i, y in enumerate(ys)]
    turned = []
    lines = []
    norms = []
    for p in range(2):
        slab = split(grid([first[2 * p][2 * p :], first[2 * p + 1][2 * p :]]))
        top = wide(split(cat(ys[2 * p : 2 * p + 2], 0)), slab)
        top = cat([finish(top[:width], last[2 * p]), finish(top[width:], last[2 * p + 1])], 0)
        lines.append(split(top))
        turn = cat([finish(ys[2 * p + c], last[2 * p + c]) for c in (0, 1)], 0)
        turned.append(split(turn))
        sums = squares_of(turn, top[:, : 2 * width])
        norms += [sums[:width], sums[width:]]
    after = [[None] * 4 for _ in range(4)]
    for p in range(2):
        for q in range(p, 2):
            cut = slice(2 * (q - p) * width, 2 * (q - p + 1) * width)
            block = wide([x[:, cut] for x in lines[p]], turned[q], 1)
            for i in range(2):
                for j in range(2):
                    at = slice(i * width, (i + 1) * width), slice(j * width, (j + 1) * width)
                    after[2 * p + i][2 * q + j] = block[at]
    for i, j in ((2, 0), (2, 1), (3, 1)):
        after[i][j] = after[j][i].T
    own, far = (0, 2), (3, 1)
    pairs = [normal(after[i][j], norms[i], norms[j], sign(i, j)) for i, j in (own, far)]
    ys, last = rows_of_rotations(pairs)
    slab = split(grid([[after[i][j] for j in own + far] for i in own]))
    line0 = finish(wide(split(ys[0]), slab), last[0])
    slab = split(grid([[after[i][j] for j in far] for i in far]))
    line3 = finish(wide(split(ys[1]), slab), last[1])
    ys = [finish(y, e) for y, e in zip(ys, last)]
    c0, c3 = [split(y) for y in ys]
    g03 = wide(split(line0[:, 2 * width :]), c3, 1)
    g00 = squares_of(ys[0], line0[:, : 2 * width])
    g33 = squares_of(ys[1], line3)
    ys, last = rows_of_rotations([normal(g03, g00, g33, sign(0, 3))])

    def row(slot):
        at = slice(slot % 2 * width, (slot % 2 + 1) * width)
        return [x[at] for x in turned[slot // 2]]

    def piece(c, half, slot):
        return wide([x[:, half * width : (half + 1) * width] for x in c], row(slot))

    mixed = split(
        grid([[piece(c0, 0, 0), piece(c0, 1, 2)], [piece(c3, 1, 1), piece(c3, 0, 3)]])
    )
    coef = split(finish(wide(split(ys[0]), mixed), last[0]))
    rows = out_ref.shape[0]
    tile = min(rows, 512)
    for at in range(0, rows, tile):
        line = [
            cat([ref[labels[k], at : at + tile] for k in range(4)], 1) for ref in (high_ref, low_ref)
        ]
        both = one(line[0], cat(coef, 0), 1)
        out_ref[at : at + tile, :] = both[:, :width] + (both[:, width:] + one(line[1], coef[0], 1))


def kernel(nb, nr, plan_ref, own_ref, out_ref, all_ref, gram_ref, part, land, *sems):
    a_send, a_recv, b_send, b_recv, c_send, c_recv, d_send, d_recv = sems
    me, row = lax.axis_index("cols"), lax.axis_index("rows")
    chips = nb // 2
    chip, core = me // 2, lax.rem(me, 2)
    sibling = chip * 2 + (1 - core)
    rows, width = own_ref.shape
    piece = 2 * width // nr
    far = range(1, chips)
    chunks = a_send.shape[2]
    size = rows // chunks

    def ahead(d):
        return lax.rem(chip + d, chips)

    def behind(d):
        return lax.rem(chip + 2 * chips - d, chips)

    def peer(k):
        return lax.rem(row + k, nr)

    barrier = pltpu.get_barrier_semaphore()
    targets = [{"cols": sibling}] + [{"cols": ahead(d) * 2 + core} for d in far]
    targets += [{"rows": peer(k)} for k in range(1, nr)]
    for target in targets:
        pl.semaphore_signal(barrier, inc=1, device_id=target, device_id_type=MESH)
    pl.semaphore_wait(barrier, len(targets))

    started = []

    def start(copy):
        copy.start()
        started.append(copy)

    def copies(ref, source, send, recv, at):
        def direct(d, n):
            return pltpu.make_async_remote_copy(
                source.at[at(0, n)], ref.at[me, at(0, n)], send.at[d, 0, n], recv.at[d, 0, n],
                device_id={"cols": ahead(d) * 2 + core}, device_id_type=MESH,
            )

        def relay(d, n):
            block = behind(d) * 2 + core
            return pltpu.make_async_remote_copy(
                source.at[at(0, n)] if d == 0 else ref.at[block, at(d, n)], ref.at[block, at(d, n)],
                send.at[d, 1, n], recv.at[d, 1, n],
                device_id={"cols": sibling}, device_id_type=MESH,
            )

        return direct, relay

    def group(d, n):
        return pl.ds(behind(d + n) * 2, 2)

    direct, relay = copies(all_ref, own_ref, a_send, a_recv, lambda d, n: pl.ds(n * size, size))
    far_panel, near_panel = copies(gram_ref, gram_ref.at[me], d_send, d_recv, group)

    def multiply(block, ch):
        at = pl.ds(ch * size, size)
        to = pl.ds(pl.multiple_of(block * width, width), width)
        product = dot(all_ref[block, at, :], own_ref[at, :], 0, 0)
        if ch == 0:
            part[to, :] = product
        else:
            part[to, :] += product

    def rows_of(g, r):
        return pl.ds(pl.multiple_of(behind(g) * (2 * width) + r * piece, piece), piece)

    def place(g):
        half = nr // 2
        at = pl.ds(pl.multiple_of(lax.rem(row, half) * piece, piece), piece)
        return gram_ref.at[me, behind(g) * 2 + row // half, at]

    def scatter(g, k):
        return pltpu.make_async_remote_copy(
            part.at[rows_of(g, peer(k))], land.at[g, k - 1],
            b_send.at[g, k - 1], b_recv.at[g, k - 1],
            device_id={"rows": peer(k)}, device_id_type=MESH,
        )

    def spread(g, k):
        return pltpu.make_async_remote_copy(
            place(g), place(g),
            c_send.at[g, k - 1], c_recv.at[g, k - 1],
            device_id={"rows": peer(k)}, device_id_type=MESH,
        )

    def send_group(g):
        for k in range(1, nr):
            start(scatter(g, k))

    def sum_group(g):
        total = part[rows_of(g, row), :]
        for k in range(1, nr):
            scatter(g, k).wait_recv()
            total += land[g, k - 1]
        place(g)[...] = total
        for k in range(1, nr):
            start(spread(g, k))

    def share_group(g):
        for k in range(1, nr):
            spread(g, k).wait_recv()
        for d in far:
            start(far_panel(d, g))
        start(near_panel(0, g))

    for ch in range(chunks):
        for d in far:
            start(direct(d, ch))
    for ch in range(chunks):
        start(relay(0, ch))
    all_ref[me] = own_ref[...]
    for ch in range(chunks):
        multiply(me, ch)
    for ch in range(chunks):
        relay(0, ch).wait_recv()
        multiply(sibling, ch)
    send_group(0)
    for ch in range(chunks + 1):
        for d in far:
            if ch < chunks:
                direct(d, ch).wait_recv()
                start(relay(d, ch))
                multiply(behind(d) * 2 + core, ch)
            if ch > 0:
                relay(d, ch - 1).wait_recv()
                multiply(behind(d) * 2 + 1 - core, ch - 1)
        if ch == chunks - 2:
            sum_group(0)
    for g in far:
        send_group(g)
    share_group(0)
    for g in far:
        sum_group(g)
    for g in far:
        share_group(g)
    for g in range(chips):
        for d in far:
            far_panel(d, g).wait_recv()
            start(near_panel(d, g))
    for g in range(chips):
        for d in range(chips):
            near_panel(d, g).wait_recv()
    rotate(nb, plan_ref, me, gram_ref, all_ref, out_ref)
    for copy in started:
        copy.wait_send()


CHUNKS = 4
LATE = 2


def tall(a, b):
    return lax.dot_general(
        cat([a[0], a[1], a[0]], 0), cat([b[0], b[0], b[1]], 0),
        (((0,), (0,)), ((), ())), preferred_element_type=jnp.float32,
    )


def kernel4(
    nr, plan_ref, own_ref, out_ref, all_ref, gram_ref, flat, cross, stage, early, near, land, high_ref, low_ref,
    down_ref, across_ref,
    masks_ref, local_sem, hop, *sems
):
    (swap_send, swap_recv, pair_send, pair_recv, relay_send, relay_recv, b_send, b_recv,
     c_send, c_recv, d_send, d_recv, g_send, g_recv, e_send, e_recv, f_send, f_recv) = sems
    me, row = lax.axis_index("cols"), lax.axis_index("rows")
    chip, core = me // 2, lax.rem(me, 2)
    sibling = chip * 2 + 1 - core
    far = (1 - chip) * 2 + core
    away = (1 - chip) * 2 + 1 - core
    rows, width = own_ref.shape
    half = rows // 2
    fine = width // (2 * nr)
    owners = nr // 2
    thick = width // nr
    owner = jnp.logical_and(row >= nr // 4, row < nr // 4 + owners)

    def peer(k):
        return lax.rem(row + k, nr)

    def there(d):
        return chip if d == 0 else 1 - chip

    def remote(source, target, send, recv, **device):
        return pltpu.make_async_remote_copy(
            source, target, send, recv, device_id=device, device_id_type=MESH
        )

    bits = [1 << n for n in range(nr.bit_length() - 1)]
    ways = [{"rows": jnp.bitwise_xor(row, bit)} for bit in bits[:-1]]
    ways += [{"cols": sibling}, {"cols": far}]
    first = ways + [{"rows": jnp.bitwise_xor(row, bits[-1])}]
    barrier = pltpu.get_barrier_semaphore()
    for way in first:
        pl.semaphore_signal(barrier, inc=1, device_id=way, device_id_type=MESH)
    plan_copy = pltpu.make_async_copy(plan_ref, masks_ref, local_sem.at[0])
    plan_copy.start()
    own_copy = pltpu.make_async_copy(own_ref, all_ref.at[me], local_sem.at[1])
    own_copy.start()
    own_copy.wait()
    pl.semaphore_wait(barrier, len(first))

    def tell(n):
        pl.semaphore_signal(hop.at[n], inc=1, device_id=ways[n], device_id_type=MESH)

    def hear(n):
        pl.semaphore_wait(hop.at[n], 1)

    started = []

    def start(copy):
        copy.start()
        started.append(copy)

    sizes = [half // CHUNKS] * CHUNKS + [half // LATE] * LATE
    offsets = [n * (half // CHUNKS) for n in range(CHUNKS)] + [n * (half // LATE) for n in range(LATE)]

    def span(side, n):
        at = side * half + offsets[n]
        return pl.ds(pl.multiple_of(at, 8), sizes[n])

    def swap(n):
        at = span(1 - chip if n < CHUNKS else chip, n)
        return remote(
            all_ref.at[me, at], all_ref.at[me, at], swap_send.at[n], swap_recv.at[n], cols=far
        )

    def relay(n):
        at = span(chip if n < CHUNKS else 1 - chip, n)
        return remote(
            all_ref.at[far, at], all_ref.at[far, at], relay_send.at[n], relay_recv.at[n],
            cols=sibling,
        )

    def pair(n):
        at = pl.ds(n * half, half)
        return remote(
            all_ref.at[me, at], all_ref.at[me, at], pair_send.at[n], pair_recv.at[n], cols=sibling
        )

    def scatter(k):
        return remote(
            stage.at[peer(k)], early.at[k - 1], b_send.at[k - 1], b_recv.at[k - 1], rows=peer(k)
        )

    def spread(k):
        return remote(
            near.at[me, row], near.at[me, row], c_send.at[k - 1], c_recv.at[k - 1], rows=peer(k)
        )

    def forward(k):
        at = near.at[me, lax.rem(row - k + nr, nr)]
        return remote(at, at, g_send.at[k], g_recv.at[k], cols=far)

    def share(n):
        at = near.at[me if n == 0 else far]
        return remote(at, at, d_send.at[n], d_recv.at[n], cols=sibling)

    def target(o):
        upper = (row < nr // 2) == (o < owners // 2)
        return jnp.where(upper, nr // 2, nr // 4) + lax.rem(o + row, owners // 2)

    def piece(x, r):
        index = x * owners + r - nr // 4
        return pl.ds(pl.multiple_of(index * thick, thick), thick)

    def side(b):
        return jnp.where(chip == 0, core, b)

    def slot(b):
        return jnp.where(chip == 0, b, core)

    def scatter_cross(b, d, o):
        return remote(
            cross.at[b, piece(there(d), target(o))], land.at[slot(b), chip, row],
            e_send.at[b, d, o], e_recv.at[slot(b), chip, row],
            cols=there(d) * 2 + side(b), rows=target(o),
        )

    def scatter_near(act):
        for o in range(owners):
            for b in range(2):
                same = jnp.logical_and(side(b) == core, target(o) == row)

                @pl.when(jnp.logical_not(same))
                def _():
                    act(scatter_cross(b, 0, o))

    def arrive_cross(i, x, r):
        return remote(
            cross.at[i, pl.ds(0, thick)], land.at[i, x, r],
            e_send.at[i, 0, 0], e_recv.at[i, x, r], cols=sibling,
        )

    def spread_cross(d, k):
        at = gram_ref.at[2 + core, pl.ds(0, 2), piece(chip, row)]
        return remote(
            at, at, f_send.at[d, k], f_recv.at[chip, row - nr // 4],
            cols=there(d) * 2 + core, rows=peer(k),
        )

    def arrive_spread(x, o):
        at = gram_ref.at[2 + core, pl.ds(0, 2), piece(x, nr // 4 + o)]
        return remote(at, at, f_send.at[0, 0], f_recv.at[x, o], cols=sibling)

    def pass_cross(x):
        at = gram_ref.at[2 + core, pl.ds(0, 2), pl.ds(x * (width // 2), width // 2)]
        return remote(at, at, d_send.at[2 + x], d_recv.at[2 + x], cols=sibling)

    tell(0)
    for n in range(CHUNKS):
        start(swap(n))
    for n in range(2):
        start(pair(n))

    step = rows // 4
    total = None
    for n in range(4):
        x = split(all_ref[me, pl.ds(n * step, step)])
        product = tall(x, x)
        total = product if total is None else total + product
    flat[0] = total
    inner = len(bits) - 1
    for n in range(inner):
        hear(n)
        tell(n + 1)
    total = None
    for n in range(4):
        if n % 2 == 0:
            pair(n // 2).wait_recv()
        at = pl.ds(n * step, step)
        product = tall(split(all_ref[chip * 2, at]), split(all_ref[chip * 2 + 1, at]))
        total = product if total is None else total + product
    flat[1] = total
    for k in range(nr):
        stage[k, : 2 * fine] = flat[0, 2 * fine * k : 2 * fine * (k + 1)]
        at = pl.multiple_of(core * (width // 2) + k * fine, fine)
        stage[k, 2 * fine :] = flat[1, pl.ds(at, fine)]
    for k in range(1, nr):
        start(scatter(k))
    hear(inner)
    tell(inner + 1)
    hear(inner + 1)

    totals = [None, None]

    def keep(block, at):
        high_ref[block, at], low_ref[block, at] = split(all_ref[block, at])

    for n in range(CHUNKS):
        swap(n).wait_recv()
        at = span(chip, n)
        for b in range(2):
            left = all_ref[jnp.where(chip == 0, b, far), at]
            right = all_ref[jnp.where(chip == 0, far, 2 + b), at]
            product = tall(split(left), split(right))
            totals[b] = product if n == 0 else totals[b] + product
    for b in range(2):
        cross[b] = totals[b]
    for o in range(owners):
        for b in range(2):
            start(scatter_cross(b, 1, o))
    scatter_near(lambda copy: copy.start())
    for n in range(CHUNKS, CHUNKS + LATE):
        start(swap(n))

    sums = stage[row]
    for k in range(1, nr):
        scatter(k).wait_recv()
        sums += early[k - 1]
    near[me, row] = sums
    for k in range(1, nr):
        start(spread(k))
    start(forward(0))
    for n in range(CHUNKS):
        start(relay(n))
    for block in (me, sibling):
        keep(block, pl.ds(0, rows))
    for n in range(CHUNKS):
        keep(far, span(chip, n))

    @pl.when(owner)
    def _():
        for b in range(2):

            @pl.when(side(b) == core)
            def _():
                land[slot(b), chip, row] = cross[b, piece(chip, row)]

        for i in range(2):
            sums = None
            for x in range(2):
                for r in range(nr):
                    same = jnp.logical_and(row == r, chip == x)
                    if x == 1:
                        same = jnp.logical_and(same, core == i)

                    @pl.when(jnp.logical_not(same))
                    def _():
                        arrive_cross(i, x, r).wait_recv()

            for x in range(2):
                for r in range(nr):
                    sums = land[i, x, r] if sums is None else sums + land[i, x, r]
            gram_ref[2 + core, i, piece(chip, row)] = sums
        for d in (1, 0):
            for k in sorted(range(nr), key=lambda k: abs(2 * k - nr - 1)):
                if d or k:
                    spread_cross(d, k).start()

    for k in range(1, nr):
        spread(k).wait_recv()
        start(forward(k))
    start(share(0))

    for n in range(CHUNKS, CHUNKS + LATE):
        swap(n).wait_recv()
        start(relay(n))
    for k in range(nr):
        forward(k).wait_recv()
    start(share(1))
    for n in range(CHUNKS, CHUNKS + LATE):
        keep(far, span(1 - chip, n))
    for n in range(CHUNKS + LATE):
        relay(n).wait_recv()
        keep(away, span(chip if n < CHUNKS else 1 - chip, n))
    for x in range(2):
        for o in range(owners):

            @pl.when(jnp.logical_not(jnp.logical_and(chip == x, row == nr // 4 + o)))
            def _():
                arrive_spread(x, o).wait_recv()

        start(pass_cross(x))
    for n in range(2):
        share(n).wait_recv()
    for block in range(4):
        square = near[block, :, : 2 * fine].reshape(width, width)
        gram_ref[block, block] = square
        square = jnp.where(eyes(width), square, 0.0)
        down = inverse(jnp.sum(square, axis=1, keepdims=True))
        down_ref[block] = jnp.broadcast_to(down, (width, width))
        across = inverse(jnp.sum(square, axis=0, keepdims=True))
        across_ref[block] = jnp.broadcast_to(across, (8, width))
    for c in range(2):
        both = [near[2 * c + i, :, 2 * fine :].reshape(width // 2, width) for i in range(2)]
        both = cat(both, 0)
        gram_ref[2 * c + 1, 2 * c] = both
        gram_ref[2 * c, 2 * c + 1] = both.T

    for i in range(2):
        gram_ref[i, 2 + core] = gram_ref[2 + core, i].T
    for x in range(2):
        pass_cross(x).wait_recv()
    for i in range(2):
        gram_ref[i, 3 - core] = gram_ref[3 - core, i].T

    plan_copy.wait()
    rotate4(masks_ref, me, gram_ref, down_ref, across_ref, high_ref, low_ref, out_ref)
    for copy in started:
        copy.wait_send()
    scatter_near(lambda copy: copy.wait_send())

    @pl.when(owner)
    def _():
        for k in range(nr):
            for d in range(2):
                if d or k:
                    spread_cross(d, k).wait_send()


def local4(nr, snapshots, plan):
    rows, width = snapshots.shape
    fine = width // (2 * nr)
    dma = pltpu.SemaphoreType.DMA
    return pl.pallas_call(
        functools.partial(kernel4, nr),
        out_shape=jax.ShapeDtypeStruct((rows, width), jnp.float32),
        in_specs=[HBM, HBM],
        out_specs=VMEM,
        scratch_shapes=[
            pltpu.VMEM((4, rows, width), jnp.float32),
            pltpu.VMEM((4, 4, width, width), jnp.float32),
            pltpu.VMEM((2, width, width), jnp.float32),
            pltpu.VMEM((2, width, width), jnp.float32),
            pltpu.VMEM((nr, 3 * fine, width), jnp.float32),
            pltpu.VMEM((nr - 1, 3 * fine, width), jnp.float32),
            pltpu.VMEM((4, nr, 3 * fine, width), jnp.float32),
            pltpu.VMEM((2, 2, nr, width // nr, width), jnp.float32),
            pltpu.VMEM((4, rows, width), jnp.bfloat16), pltpu.VMEM((4, rows, width), jnp.bfloat16),
            pltpu.VMEM((4, width, width), jnp.float32), pltpu.VMEM((4, 8, width), jnp.float32),
            pltpu.SMEM(plan.shape, jnp.int32), dma((2,)),
            pltpu.SemaphoreType.REGULAR((nr.bit_length(),)),
            dma((CHUNKS + LATE,)), dma((CHUNKS + LATE,)),
            dma((2,)), dma((2,)),
            dma((CHUNKS + LATE,)), dma((CHUNKS + LATE,)),
            dma((nr - 1,)), dma((nr - 1,)),
            dma((nr - 1,)), dma((nr - 1,)),
            dma((4,)), dma((4,)), dma((nr,)), dma((nr,)),
            dma((2, 2, nr // 2)), dma((2, 2, nr)),
            dma((2, nr)), dma((2, nr // 2)),
        ],
        compiler_params=pltpu.CompilerParams(
            collective_id=0, has_side_effects=True, vmem_limit_bytes=53 * 2**20
        ),
    )(plan, snapshots)


def local(nb, nr, snapshots, plan):
    rows, width = snapshots.shape
    chips = nb // 2
    dma = pltpu.SemaphoreType.DMA
    return pl.pallas_call(
        functools.partial(kernel, nb, nr),
        out_shape=jax.ShapeDtypeStruct((rows, width), jnp.float32),
        in_specs=[SMEM, VMEM],
        out_specs=VMEM,
        scratch_shapes=[
            pltpu.VMEM((nb, rows, width), jnp.float32),
            pltpu.VMEM((nb, nb, width, width), jnp.float32),
            pltpu.VMEM((nb * width, width), jnp.float32),
            pltpu.VMEM((chips, nr - 1, 2 * width // nr, width), jnp.float32),
            dma((chips, 2, 4)), dma((chips, 2, 4)),
            dma((chips, nr - 1)), dma((chips, nr - 1)),
            dma((chips, nr - 1)), dma((chips, nr - 1)),
            dma((chips, 2, chips)), dma((chips, 2, chips)),
        ],
        compiler_params=pltpu.CompilerParams(
            collective_id=0, has_side_effects=True, vmem_limit_bytes=48 * 2**20
        ),
    )(plan, snapshots)


def solution(mesh):
    nb, nr = mesh.shape["cols"], mesh.shape["rows"]
    four = nb == 4 and nr >= 4 and nr & (nr - 1) == 0
    body = functools.partial(local4, nr) if four else functools.partial(local, nb, nr)
    return jax.shard_map(
        body,
        mesh=mesh,
        in_specs=(P("rows", "cols"), P()),
        out_specs=P("rows", "cols"),
        check_vma=False,
    )
```

```python
import functools

import jax
import jax.numpy as jnp
from jax import lax
from jax.experimental import pallas as pl
from jax.experimental.pallas import tpu as pltpu
from jax.sharding import PartitionSpec as P

NSI = 5
EPS = 1e-6
VMEM = pl.BlockSpec(memory_space=pltpu.VMEM)
MESH = pl.DeviceIdType.MESH
SMEM = pl.BlockSpec(memory_space=pltpu.SMEM)
HBM = pl.BlockSpec(memory_space=pltpu.HBM)


def split(x):
    high = x.astype(jnp.bfloat16)
    return high, (x - high.astype(jnp.float32)).astype(jnp.bfloat16)


def dots(a, b, ca=1, cb=0):
    def one(x, y):
        return lax.dot_general(
            x, y, (((ca,), (cb,)), ((), ())), preferred_element_type=jnp.float32
        )

    return one(a[0], b[0]) + (one(a[0], b[1]) + one(a[1], b[0]))


def dot(a, b, ca=1, cb=0):
    return dots(split(a), split(b), ca, cb)


def columns(gens):
    width = gens[0].shape[0]
    row = lax.broadcasted_iota(jnp.int32, (width, width), 0)
    col = lax.broadcasted_iota(jnp.int32, (width, width), 1)
    eye = jnp.where(row == col, 1.0, 0.0).astype(jnp.float32)
    parts = [split(g) for g in gens]
    zs = [0.5 * (eye + dots(p, p, 1, 1)) for p in parts]
    qs = None
    for index in range(NSI):
        ts = [1.5 * eye - 0.5 * z for z in zs]
        tsp = [split(t) for t in ts]
        if qs is None:
            qs = [t * (0.5**0.5) for t in ts]
        else:
            qs = [dots(split(q), t) for q, t in zip(qs, tsp)]
        if index < NSI - 1:
            squares = [dots(t, t) for t in tsp]
            zs = [dot(z, s) for z, s in zip(zs, squares)]
    return [(q, dots(p, split(q), 0, 0)) for q, p in zip(qs, parts)]


def generator(cross, own, other, sign):
    width = cross.shape[0]
    row = lax.broadcasted_iota(jnp.int32, (width, width), 0)
    col = lax.broadcasted_iota(jnp.int32, (width, width), 1)
    diag = row == col
    dc = jnp.sum(jnp.where(diag, own, 0.0), axis=1, keepdims=True)
    dp = jnp.sum(jnp.where(diag, other, 0.0), axis=0, keepdims=True)
    dc = jnp.maximum(dc, 0.0) + EPS
    dp = jnp.maximum(dp, 0.0) + EPS
    cross = cross * (lax.rsqrt(dc) * lax.rsqrt(dp))
    total = jnp.sum(jnp.sum(cross * cross, axis=1, keepdims=True), axis=0, keepdims=True)
    return cross * (sign * lax.rsqrt(1.0 + total))


def rotate(nb, plan_ref, label, gram_ref, all_ref, out_ref):
    width = out_ref.shape[1]
    masks = [plan_ref[s] for s in range(3)]
    labels = []
    for slot in range(8):
        block = label
        for bit in range(3):
            if slot >> bit & 1:
                block = jnp.bitwise_xor(block, masks[bit])
        labels.append(block)

    def sign(i, j):
        return jnp.where(labels[i] < labels[j], 1.0, -1.0).astype(jnp.float32)

    loaded = {}

    def gram(i, j):
        if (i, j) not in loaded:
            loaded[i, j] = gram_ref[labels[j], labels[i]]
        return loaded[i, j]

    def stack(parts, axis):
        return jnp.concatenate(parts, axis=axis)

    outs = (0, 2, 4, 6)
    gens = [generator(gram(i, i + 1), gram(i, i), gram(i + 1, i + 1), sign(i, i + 1)) for i in outs]
    first = columns(gens)
    col = {i: split(stack(c, 0)) for i, c in zip(outs, first)}
    after = {}
    for i in outs:
        for j in outs:
            if j < i:
                continue
            wide = stack(
                [stack([gram(i + p, j), gram(i + p, j + 1)], 1) for p in (0, 1)], 0
            )
            half = dots(split(wide), col[j])
            after[i, j] = dots(col[i], split(half), 0, 0)

    gens = [generator(after[i, i + 2], after[i, i], after[i + 2, i + 2], sign(i, i + 2)) for i in (0, 4)]
    second = columns(gens)
    c0, c4 = [split(stack(c, 0)) for c in second]

    def block(i, j):
        return stack(
            [
                stack([after[i, j], after[i, j + 2]], 1),
                stack([after[i + 2, j] if i + 2 <= j else after[j, i + 2].T, after[i + 2, j + 2]], 1),
            ],
            0,
        )

    def update(ci, mat, cj):
        return dots(ci, split(dots(split(mat), cj)), 0, 0)

    g00 = update(c0, block(0, 0), c0)
    g04 = update(c0, block(0, 4), c4)
    g44 = update(c4, block(4, 4), c4)
    gens = [generator(g04, g00, g44, sign(0, 4))]
    (a, b), = columns(gens)
    top = dots(c0, split(a))
    bottom = dots(c4, split(b))
    weight = {0: top[:width], 2: top[width:], 4: bottom[:width], 6: bottom[width:]}
    coef = {}
    for i in outs:
        both = dots(col[i], split(weight[i]))
        coef[i], coef[i + 1] = both[:width], both[width:]
    coefs = [split(coef[k]) for k in range(8)]
    rows = out_ref.shape[0]
    tile = min(rows, 256)

    for at in range(0, rows, tile):
        total = jnp.zeros((tile, width), jnp.float32)
        for k in range(len(coefs)):
            total += dots(split(all_ref[labels[k], at : at + tile]), coefs[k])
        out_ref[at : at + tile, :] = total


def cat(parts, axis):
    return jnp.concatenate(parts, axis=axis)


def one(a, b, cb=0):
    return lax.dot_general(
        a, b, (((1,), (cb,)), ((), ())), preferred_element_type=jnp.float32
    )


def wide(a, b, cb=0):
    return one(cat([a[0], a[1], a[0]], 1), cat([b[0], b[0], b[1]], cb), cb)


def eyes(width):
    row = lax.broadcasted_iota(jnp.int32, (width, width), 0)
    col = lax.broadcasted_iota(jnp.int32, (width, width), 1)
    return row == col


def squares_of(turn, line):
    return jnp.sum(turn * line, axis=1, keepdims=True)


def strength(cross, sign):
    total = jnp.sum(jnp.sum(cross * cross, axis=0, keepdims=True), axis=1, keepdims=True)
    return sign * lax.rsqrt(1.0 + total)


def inverse(square):
    return lax.rsqrt(jnp.maximum(square, 0.0) + EPS)


def normal(cross, own, other, sign):
    dp = jnp.sum(jnp.where(eyes(cross.shape[0]), other, 0.0), axis=0, keepdims=True)
    cross = cross * (inverse(own) * inverse(dp))
    return cross, strength(cross, sign)


def rows_of_rotations(pairs, thin=False):
    width = pairs[0][0].shape[0]
    eye = jnp.where(eyes(width), 1.0, 0.0).astype(jnp.float32)
    parts = [split(c) for c, _ in pairs]
    squares = [wide(p, p, 1) for p in parts]
    es = [0.5 * eye - (0.5 * a * a) * s for (_, a), s in zip(pairs, squares)]
    gs = [a * c for c, a in pairs]
    ep = [split(e) for e in es]
    boths = [
        wide(p, p if thin and n % 2 else [cat([x, y], 1) for x, y in zip(p, split(g))])
        for n, (p, g) in enumerate(zip(ep, gs))
    ]
    ys = [
        (0.5**0.5)
        * (eye + 0.5 * e if thin and n % 2 else cat([eye + 0.5 * e, g + 0.5 * b[:, width:]], 1))
        for n, (e, g, b) in enumerate(zip(es, gs, boths))
    ]
    fs = [b[:, :width] for b in boths]
    es = [0.75 * f + 0.25 * wide(split(f), p) for f, p in zip(fs, ep)]
    ep = [split(e) for e in es]
    boths = [wide(p, [cat([x, z], 1) for x, z in zip(p, split(y))]) for p, y in zip(ep, ys)]
    ys = [y + 0.5 * b[:, width:] for y, b in zip(ys, boths)]
    fs = [b[:, :width] for b in boths]
    es = [0.75 * f + 0.25 * one(f.astype(jnp.bfloat16), p[0]) for f, p in zip(fs, ep)]
    ep = [split(e) for e in es]
    fs = [one(p[0], p[0]) for p in ep]
    ys = [y + 0.5 * wide(p, split(y)) for y, p in zip(ys, ep)]
    es = [0.75 * f + 0.25 * one(f.astype(jnp.bfloat16), p[0]) for f, p in zip(fs, ep)]
    eh = [e.astype(jnp.bfloat16) for e in es]
    fs = [one(h, h) for h in eh]
    ys = [y + 0.5 * one(h, y.astype(jnp.bfloat16)) for y, h in zip(ys, eh)]
    last = [
        (0.5 * (0.75 * f + 0.25 * one(f.astype(jnp.bfloat16), h))).astype(jnp.bfloat16)
        for f, h in zip(fs, eh)
    ]
    return ys, last


def finish(x, last):
    return x + one(last, x.astype(jnp.bfloat16))


def rotate4(plan_ref, label, gram_ref, down_ref, across_ref, high_ref, low_ref, out_ref):
    width = out_ref.shape[1]
    masks = [plan_ref[s] for s in range(2)]
    labels = [label, jnp.bitwise_xor(label, masks[0]), jnp.bitwise_xor(label, masks[1])]
    labels.append(jnp.bitwise_xor(labels[1], masks[1]))

    def sign(i, j):
        return jnp.where(labels[i] < labels[j], 1.0, -1.0).astype(jnp.float32)

    def grid(blocks):
        return cat([cat(line, 1) for line in blocks], 0)

    first = [[gram_ref[labels[j], labels[i]] for j in range(4)] for i in range(4)]
    pairs = []
    for i in range(4):
        scale = down_ref[labels[i]] * across_ref[labels[i ^ 1], :1]
        pairs.append(first[i][i ^ 1] * scale)
    sizes = [strength(pairs[i], sign(i, i ^ 1)) for i in (0, 2)]
    pairs = list(zip(pairs, (sizes[0], -sizes[0], sizes[1], -sizes[1])))
    ys, last = rows_of_rotations(pairs, True)
    ys = [cat([-ys[i - 1][:, width:].T, y], 1) if i % 2 else y for i, y in enumerate(ys)]
    turned = []
    lines = []
    norms = []
    for p in range(2):
        slab = split(grid([first[2 * p][2 * p :], first[2 * p + 1][2 * p :]]))
        top = wide(split(cat(ys[2 * p : 2 * p + 2], 0)), slab)
        top = cat([finish(top[:width], last[2 * p]), finish(top[width:], last[2 * p + 1])], 0)
        lines.append(split(top))
        turn = cat([finish(ys[2 * p + c], last[2 * p + c]) for c in (0, 1)], 0)
        turned.append(split(turn))
        sums = squares_of(turn, top[:, : 2 * width])
        norms += [sums[:width], sums[width:]]
    after = [[None] * 4 for _ in range(4)]
    for p in range(2):
        for q in range(p, 2):
            cut = slice(2 * (q - p) * width, 2 * (q - p + 1) * width)
            block = wide([x[:, cut] for x in lines[p]], turned[q], 1)
            for i in range(2):
                for j in range(2):
                    at = slice(i * width, (i + 1) * width), slice(j * width, (j + 1) * width)
                    after[2 * p + i][2 * q + j] = block[at]
    for i, j in ((2, 0), (2, 1), (3, 1)):
        after[i][j] = after[j][i].T
    own, far = (0, 2), (3, 1)
    pairs = [normal(after[i][j], norms[i], norms[j], sign(i, j)) for i, j in (own, far)]
    ys, last = rows_of_rotations(pairs)
    slab = split(grid([[after[i][j] for j in own + far] for i in own]))
    line0 = finish(wide(split(ys[0]), slab), last[0])
    slab = split(grid([[after[i][j] for j in far] for i in far]))
    line3 = finish(wide(split(ys[1]), slab), last[1])
    ys = [finish(y, e) for y, e in zip(ys, last)]
    c0, c3 = [split(y) for y in ys]
    g03 = wide(split(line0[:, 2 * width :]), c3, 1)
    g00 = squares_of(ys[0], line0[:, : 2 * width])
    g33 = squares_of(ys[1], line3)
    ys, last = rows_of_rotations([normal(g03, g00, g33, sign(0, 3))])

    def row(slot):
        at = slice(slot % 2 * width, (slot % 2 + 1) * width)
        return [x[at] for x in turned[slot // 2]]

    def piece(c, half, slot):
        return wide([x[:, half * width : (half + 1) * width] for x in c], row(slot))

    mixed = split(
        grid([[piece(c0, 0, 0), piece(c0, 1, 2)], [piece(c3, 1, 1), piece(c3, 0, 3)]])
    )
    coef = split(finish(wide(split(ys[0]), mixed), last[0]))
    rows = out_ref.shape[0]
    tile = min(rows, 512)
    for at in range(0, rows, tile):
        line = [
            cat([ref[labels[k], at : at + tile] for k in range(4)], 1) for ref in (high_ref, low_ref)
        ]
        both = one(line[0], cat(coef, 0), 1)
        out_ref[at : at + tile, :] = both[:, :width] + (both[:, width:] + one(line[1], coef[0], 1))


def kernel(nb, nr, plan_ref, own_ref, out_ref, all_ref, gram_ref, part, land, *sems):
    a_send, a_recv, b_send, b_recv, c_send, c_recv, d_send, d_recv = sems
    me, row = lax.axis_index("cols"), lax.axis_index("rows")
    chips = nb // 2
    chip, core = me // 2, lax.rem(me, 2)
    sibling = chip * 2 + (1 - core)
    rows, width = own_ref.shape
    piece = 2 * width // nr
    far = range(1, chips)
    chunks = a_send.shape[2]
    size = rows // chunks

    def ahead(d):
        return lax.rem(chip + d, chips)

    def behind(d):
        return lax.rem(chip + 2 * chips - d, chips)

    def peer(k):
        return lax.rem(row + k, nr)

    barrier = pltpu.get_barrier_semaphore()
    targets = [{"cols": sibling}] + [{"cols": ahead(d) * 2 + core} for d in far]
    targets += [{"rows": peer(k)} for k in range(1, nr)]
    for target in targets:
        pl.semaphore_signal(barrier, inc=1, device_id=target, device_id_type=MESH)
    pl.semaphore_wait(barrier, len(targets))

    started = []

    def start(copy):
        copy.start()
        started.append(copy)

    def copies(ref, source, send, recv, at):
        def direct(d, n):
            return pltpu.make_async_remote_copy(
                source.at[at(0, n)], ref.at[me, at(0, n)], send.at[d, 0, n], recv.at[d, 0, n],
                device_id={"cols": ahead(d) * 2 + core}, device_id_type=MESH,
            )

        def relay(d, n):
            block = behind(d) * 2 + core
            return pltpu.make_async_remote_copy(
                source.at[at(0, n)] if d == 0 else ref.at[block, at(d, n)], ref.at[block, at(d, n)],
                send.at[d, 1, n], recv.at[d, 1, n],
                device_id={"cols": sibling}, device_id_type=MESH,
            )

        return direct, relay

    def group(d, n):
        return pl.ds(behind(d + n) * 2, 2)

    direct, relay = copies(all_ref, own_ref, a_send, a_recv, lambda d, n: pl.ds(n * size, size))
    far_panel, near_panel = copies(gram_ref, gram_ref.at[me], d_send, d_recv, group)

    def multiply(block, ch):
        at = pl.ds(ch * size, size)
        to = pl.ds(pl.multiple_of(block * width, width), width)
        product = dot(all_ref[block, at, :], own_ref[at, :], 0, 0)
        if ch == 0:
            part[to, :] = product
        else:
            part[to, :] += product

    def rows_of(g, r):
        return pl.ds(pl.multiple_of(behind(g) * (2 * width) + r * piece, piece), piece)

    def place(g):
        half = nr // 2
        at = pl.ds(pl.multiple_of(lax.rem(row, half) * piece, piece), piece)
        return gram_ref.at[me, behind(g) * 2 + row // half, at]

    def scatter(g, k):
        return pltpu.make_async_remote_copy(
            part.at[rows_of(g, peer(k))], land.at[g, k - 1],
            b_send.at[g, k - 1], b_recv.at[g, k - 1],
            device_id={"rows": peer(k)}, device_id_type=MESH,
        )

    def spread(g, k):
        return pltpu.make_async_remote_copy(
            place(g), place(g),
            c_send.at[g, k - 1], c_recv.at[g, k - 1],
            device_id={"rows": peer(k)}, device_id_type=MESH,
        )

    def send_group(g):
        for k in range(1, nr):
            start(scatter(g, k))

    def sum_group(g):
        total = part[rows_of(g, row), :]
        for k in range(1, nr):
            scatter(g, k).wait_recv()
            total += land[g, k - 1]
        place(g)[...] = total
        for k in range(1, nr):
            start(spread(g, k))

    def share_group(g):
        for k in range(1, nr):
            spread(g, k).wait_recv()
        for d in far:
            start(far_panel(d, g))
        start(near_panel(0, g))

    for ch in range(chunks):
        for d in far:
            start(direct(d, ch))
    for ch in range(chunks):
        start(relay(0, ch))
    all_ref[me] = own_ref[...]
    for ch in range(chunks):
        multiply(me, ch)
    for ch in range(chunks):
        relay(0, ch).wait_recv()
        multiply(sibling, ch)
    send_group(0)
    for ch in range(chunks + 1):
        for d in far:
            if ch < chunks:
                direct(d, ch).wait_recv()
                start(relay(d, ch))
                multiply(behind(d) * 2 + core, ch)
            if ch > 0:
                relay(d, ch - 1).wait_recv()
                multiply(behind(d) * 2 + 1 - core, ch - 1)
        if ch == chunks - 2:
            sum_group(0)
    for g in far:
        send_group(g)
    share_group(0)
    for g in far:
        sum_group(g)
    for g in far:
        share_group(g)
    for g in range(chips):
        for d in far:
            far_panel(d, g).wait_recv()
            start(near_panel(d, g))
    for g in range(chips):
        for d in range(chips):
            near_panel(d, g).wait_recv()
    rotate(nb, plan_ref, me, gram_ref, all_ref, out_ref)
    for copy in started:
        copy.wait_send()


CHUNKS = 4
LATE = 2


def tall(a, b):
    return lax.dot_general(
        cat([a[0], a[1], a[0]], 0), cat([b[0], b[0], b[1]], 0),
        (((0,), (0,)), ((), ())), preferred_element_type=jnp.float32,
    )


def kernel4(
    nr, plan_ref, own_ref, out_ref, all_ref, gram_ref, flat, cross, stage, early, near, land, high_ref, low_ref,
    down_ref, across_ref,
    masks_ref, local_sem, hop, *sems
):
    (swap_send, swap_recv, pair_send, pair_recv, relay_send, relay_recv, b_send, b_recv,
     c_send, c_recv, d_send, d_recv, g_send, g_recv, e_send, e_recv, f_send, f_recv) = sems
    me, row = lax.axis_index("cols"), lax.axis_index("rows")
    chip, core = me // 2, lax.rem(me, 2)
    sibling = chip * 2 + 1 - core
    far = (1 - chip) * 2 + core
    away = (1 - chip) * 2 + 1 - core
    rows, width = own_ref.shape
    half = rows // 2
    owners = nr // 2
    thick = width // nr
    owner = jnp.logical_and(row >= nr // 4, row < nr // 4 + owners)

    def peer(k):
        return lax.rem(row + k, nr)

    def there(d):
        return chip if d == 0 else 1 - chip

    def remote(source, target, send, recv, **device):
        return pltpu.make_async_remote_copy(
            source, target, send, recv, device_id=device, device_id_type=MESH
        )

    bits = [1 << n for n in range(nr.bit_length() - 1)]
    ways = [{"rows": jnp.bitwise_xor(row, bit)} for bit in bits[:-1]]
    ways += [{"cols": sibling}, {"cols": far}]
    first = ways + [{"rows": jnp.bitwise_xor(row, bits[-1])}]
    barrier = pltpu.get_barrier_semaphore()
    for way in first:
        pl.semaphore_signal(barrier, inc=1, device_id=way, device_id_type=MESH)
    plan_copy = pltpu.make_async_copy(plan_ref, masks_ref, local_sem.at[0])
    plan_copy.start()
    own_copy = pltpu.make_async_copy(own_ref, all_ref.at[me], local_sem.at[1])
    own_copy.start()
    own_copy.wait()
    pl.semaphore_wait(barrier, len(first))

    def tell(n):
        pl.semaphore_signal(hop.at[n], inc=1, device_id=ways[n], device_id_type=MESH)

    def hear(n):
        pl.semaphore_wait(hop.at[n], 1)

    started = []

    def start(copy):
        copy.start()
        started.append(copy)

    sizes = [half // CHUNKS] * CHUNKS + [half // LATE] * LATE
    offsets = [n * (half // CHUNKS) for n in range(CHUNKS)] + [n * (half // LATE) for n in range(LATE)]

    def span(side, n):
        at = side * half + offsets[n]
        return pl.ds(pl.multiple_of(at, 8), sizes[n])

    def swap(n):
        at = span(1 - chip if n < CHUNKS else chip, n)
        return remote(
            all_ref.at[me, at], all_ref.at[me, at], swap_send.at[n], swap_recv.at[n], cols=far
        )

    def relay(n):
        at = span(chip if n < CHUNKS else 1 - chip, n)
        return remote(
            all_ref.at[far, at], all_ref.at[far, at], relay_send.at[n], relay_recv.at[n],
            cols=sibling,
        )

    def pair(n):
        at = pl.ds(n * half, half)
        return remote(
            all_ref.at[me, at], all_ref.at[me, at], pair_send.at[n], pair_recv.at[n], cols=sibling
        )

    def scatter(o):
        return remote(
            stage.at[target(o) - nr // 4], early.at[row], b_send.at[o], b_recv.at[row],
            rows=target(o),
        )

    def scatter_all(act):
        for o in range(owners):

            @pl.when(target(o) != row)
            def _():
                act(scatter(o))

    def arrive_early(r):
        return remote(stage.at[0], early.at[r], b_send.at[0], b_recv.at[r], cols=sibling)

    def spread(k):
        at = near.at[me, row - nr // 4]
        return remote(at, at, c_send.at[k - 1], c_recv.at[row - nr // 4], rows=peer(k))

    def arrive_near(o):
        at = near.at[me, o]
        return remote(at, at, c_send.at[0], c_recv.at[o], cols=sibling)

    def forward(o):
        at = near.at[me, o]
        return remote(at, at, g_send.at[o], g_recv.at[o], cols=far)

    def share(n):
        at = near.at[me if n == 0 else far]
        return remote(at, at, d_send.at[n], d_recv.at[n], cols=sibling)

    def target(o):
        upper = (row < nr // 2) == (o < owners // 2)
        return jnp.where(upper, nr // 2, nr // 4) + lax.rem(o + row, owners // 2)

    def piece(x, r):
        index = x * owners + r - nr // 4
        return pl.ds(pl.multiple_of(index * thick, thick), thick)

    def side(b):
        return jnp.where(chip == 0, core, b)

    def slot(b):
        return jnp.where(chip == 0, b, core)

    def scatter_cross(b, d, o):
        return remote(
            cross.at[b, piece(there(d), target(o))], land.at[slot(b), chip, row],
            e_send.at[b, d, o], e_recv.at[slot(b), chip, row],
            cols=there(d) * 2 + side(b), rows=target(o),
        )

    def scatter_near(act):
        for o in range(owners):
            for b in range(2):
                same = jnp.logical_and(side(b) == core, target(o) == row)

                @pl.when(jnp.logical_not(same))
                def _():
                    act(scatter_cross(b, 0, o))

    def arrive_cross(i, x, r):
        return remote(
            cross.at[i, pl.ds(0, thick)], land.at[i, x, r],
            e_send.at[i, 0, 0], e_recv.at[i, x, r], cols=sibling,
        )

    def spread_cross(d, k):
        at = gram_ref.at[2 + core, pl.ds(0, 2), piece(chip, row)]
        return remote(
            at, at, f_send.at[d, k], f_recv.at[chip, row - nr // 4],
            cols=there(d) * 2 + core, rows=peer(k),
        )

    def arrive_spread(x, o):
        at = gram_ref.at[2 + core, pl.ds(0, 2), piece(x, nr // 4 + o)]
        return remote(at, at, f_send.at[0, 0], f_recv.at[x, o], cols=sibling)

    def pass_cross(x):
        at = gram_ref.at[2 + core, pl.ds(0, 2), pl.ds(x * (width // 2), width // 2)]
        return remote(at, at, d_send.at[2 + x], d_recv.at[2 + x], cols=sibling)

    tell(0)
    for n in range(CHUNKS):
        start(swap(n))
    for n in range(2):
        start(pair(n))

    step = rows // 4
    total = None
    for n in range(4):
        x = split(all_ref[me, pl.ds(n * step, step)])
        product = tall(x, x)
        total = product if total is None else total + product
    flat[0] = total
    inner = len(bits) - 1
    for n in range(inner):
        hear(n)
        tell(n + 1)
    total = None
    for n in range(4):
        if n % 2 == 0:
            pair(n // 2).wait_recv()
        at = pl.ds(n * step, step)
        product = tall(split(all_ref[chip * 2, at]), split(all_ref[chip * 2 + 1, at]))
        total = product if total is None else total + product
    flat[1] = total
    for o in range(owners):
        stage[o, : 2 * thick] = flat[0, 2 * thick * o : 2 * thick * (o + 1)]
        at = pl.multiple_of(core * (width // 2) + o * thick, thick)
        stage[o, 2 * thick :] = flat[1, pl.ds(at, thick)]
    scatter_all(lambda copy: copy.start())
    hear(inner)
    tell(inner + 1)
    hear(inner + 1)

    totals = [None, None]

    def keep(block, at):
        high_ref[block, at], low_ref[block, at] = split(all_ref[block, at])

    for n in range(CHUNKS):
        swap(n).wait_recv()
        at = span(chip, n)
        for b in range(2):
            left = all_ref[jnp.where(chip == 0, b, far), at]
            right = all_ref[jnp.where(chip == 0, far, 2 + b), at]
            product = tall(split(left), split(right))
            totals[b] = product if n == 0 else totals[b] + product
    for b in range(2):
        cross[b] = totals[b]
    for o in range(owners):
        for b in range(2):
            start(scatter_cross(b, 1, o))
    scatter_near(lambda copy: copy.start())
    for n in range(CHUNKS, CHUNKS + LATE):
        start(swap(n))

    order = sorted(range(nr), key=lambda k: abs(2 * k - nr - 1))

    @pl.when(owner)
    def _():
        early[row] = stage[row - nr // 4]
        for r in range(nr):

            @pl.when(row != r)
            def _():
                arrive_early(r).wait_recv()

        near[me, row - nr // 4] = sum((early[r] for r in range(1, nr)), early[0])
        for k in order:
            if k:
                spread(k).start()

    for n in range(CHUNKS):
        start(relay(n))
    for block in (me, sibling):
        keep(block, pl.ds(0, rows))
    for n in range(CHUNKS):
        keep(far, span(chip, n))

    @pl.when(owner)
    def _():
        for b in range(2):

            @pl.when(side(b) == core)
            def _():
                land[slot(b), chip, row] = cross[b, piece(chip, row)]

        for i in range(2):
            sums = None
            for x in range(2):
                for r in range(nr):
                    same = jnp.logical_and(row == r, chip == x)
                    if x == 1:
                        same = jnp.logical_and(same, core == i)

                    @pl.when(jnp.logical_not(same))
                    def _():
                        arrive_cross(i, x, r).wait_recv()

            for x in range(2):
                for r in range(nr):
                    sums = land[i, x, r] if sums is None else sums + land[i, x, r]
            gram_ref[2 + core, i, piece(chip, row)] = sums
        for d in (1, 0):
            for k in order:
                if d or k:
                    spread_cross(d, k).start()

    for o in range(owners):

        @pl.when(row != nr // 4 + o)
        def _():
            arrive_near(o).wait_recv()

        start(forward(o))
    start(share(0))

    for n in range(CHUNKS, CHUNKS + LATE):
        swap(n).wait_recv()
        start(relay(n))
    for o in range(owners):
        forward(o).wait_recv()
    for copy in started:
        copy.wait_send()
    scatter_near(lambda copy: copy.wait_send())
    scatter_all(lambda copy: copy.wait_send())

    @pl.when(owner)
    def _():
        for k in range(1, nr):
            spread(k).wait_send()

    plan_copy.wait()
    share(1).start()
    for n in range(CHUNKS, CHUNKS + LATE):
        keep(far, span(1 - chip, n))
    for n in range(CHUNKS + LATE):
        relay(n).wait_recv()
        keep(away, span(chip if n < CHUNKS else 1 - chip, n))
    for d in range(2):
        for o in range(owners):
            if d == 0:

                @pl.when(row != nr // 4 + o)
                def _():
                    arrive_spread(chip, o).wait_recv()

            else:
                arrive_spread(1 - chip, o).wait_recv()
        pass_cross(there(d)).start()
    @pl.when(owner)
    def _():
        for k in range(nr):
            for d in range(2):
                if d or k:
                    spread_cross(d, k).wait_send()

    for n in range(2):
        share(n).wait_recv()
    share(1).wait_send()
    for block in range(4):
        square = near[block, :, : 2 * thick].reshape(width, width)
        gram_ref[block, block] = square
        square = jnp.where(eyes(width), square, 0.0)
        down = inverse(jnp.sum(square, axis=1, keepdims=True))
        down_ref[block] = jnp.broadcast_to(down, (width, width))
        across = inverse(jnp.sum(square, axis=0, keepdims=True))
        across_ref[block] = jnp.broadcast_to(across, (8, width))
    for c in range(2):
        both = [near[2 * c + i, :, 2 * thick :].reshape(width // 2, width) for i in range(2)]
        both = cat(both, 0)
        gram_ref[2 * c + 1, 2 * c] = both
        gram_ref[2 * c, 2 * c + 1] = both.T

    for i in range(2):
        gram_ref[i, 2 + core] = gram_ref[2 + core, i].T
    for x in range(2):
        pass_cross(x).wait_recv()
    for i in range(2):
        gram_ref[i, 3 - core] = gram_ref[3 - core, i].T

    rotate4(masks_ref, me, gram_ref, down_ref, across_ref, high_ref, low_ref, out_ref)
    for x in range(2):
        pass_cross(x).wait_send()


def local4(nr, snapshots, plan):
    rows, width = snapshots.shape
    owners, thick = nr // 2, width // nr
    dma = pltpu.SemaphoreType.DMA
    return pl.pallas_call(
        functools.partial(kernel4, nr),
        out_shape=jax.ShapeDtypeStruct((rows, width), jnp.float32),
        in_specs=[HBM, HBM],
        out_specs=VMEM,
        scratch_shapes=[
            pltpu.VMEM((4, rows, width), jnp.float32),
            pltpu.VMEM((4, 4, width, width), jnp.float32),
            pltpu.VMEM((2, width, width), jnp.float32),
            pltpu.VMEM((2, width, width), jnp.float32),
            pltpu.VMEM((owners, 3 * thick, width), jnp.float32),
            pltpu.VMEM((nr, 3 * thick, width), jnp.float32),
            pltpu.VMEM((4, owners, 3 * thick, width), jnp.float32),
            pltpu.VMEM((2, 2, nr, thick, width), jnp.float32),
            pltpu.VMEM((4, rows, width), jnp.bfloat16), pltpu.VMEM((4, rows, width), jnp.bfloat16),
            pltpu.VMEM((4, width, width), jnp.float32), pltpu.VMEM((4, 8, width), jnp.float32),
            pltpu.SMEM(plan.shape, jnp.int32), dma((2,)),
            pltpu.SemaphoreType.REGULAR((nr.bit_length(),)),
            dma((CHUNKS + LATE,)), dma((CHUNKS + LATE,)),
            dma((2,)), dma((2,)),
            dma((CHUNKS + LATE,)), dma((CHUNKS + LATE,)),
            dma((owners,)), dma((nr,)),
            dma((nr - 1,)), dma((owners,)),
            dma((4,)), dma((4,)), dma((owners,)), dma((owners,)),
            dma((2, 2, nr // 2)), dma((2, 2, nr)),
            dma((2, nr)), dma((2, nr // 2)),
        ],
        compiler_params=pltpu.CompilerParams(
            collective_id=0, has_side_effects=True, vmem_limit_bytes=53 * 2**20
        ),
    )(plan, snapshots)


def local(nb, nr, snapshots, plan):
    rows, width = snapshots.shape
    chips = nb // 2
    dma = pltpu.SemaphoreType.DMA
    return pl.pallas_call(
        functools.partial(kernel, nb, nr),
        out_shape=jax.ShapeDtypeStruct((rows, width), jnp.float32),
        in_specs=[SMEM, VMEM],
        out_specs=VMEM,
        scratch_shapes=[
            pltpu.VMEM((nb, rows, width), jnp.float32),
            pltpu.VMEM((nb, nb, width, width), jnp.float32),
            pltpu.VMEM((nb * width, width), jnp.float32),
            pltpu.VMEM((chips, nr - 1, 2 * width // nr, width), jnp.float32),
            dma((chips, 2, 4)), dma((chips, 2, 4)),
            dma((chips, nr - 1)), dma((chips, nr - 1)),
            dma((chips, nr - 1)), dma((chips, nr - 1)),
            dma((chips, 2, chips)), dma((chips, 2, chips)),
        ],
        compiler_params=pltpu.CompilerParams(
            collective_id=0, has_side_effects=True, vmem_limit_bytes=48 * 2**20
        ),
    )(plan, snapshots)


def solution(mesh):
    nb, nr = mesh.shape["cols"], mesh.shape["rows"]
    four = nb == 4 and nr >= 4 and nr & (nr - 1) == 0
    body = functools.partial(local4, nr) if four else functools.partial(local, nb, nr)
    return jax.shard_map(
        body,
        mesh=mesh,
        in_specs=(P("rows", "cols"), P()),
        out_specs=P("rows", "cols"),
        check_vma=False,
    )
```

```python
import functools

import jax
import jax.numpy as jnp
from jax import lax
from jax.experimental import pallas as pl
from jax.experimental.pallas import tpu as pltpu
from jax.sharding import PartitionSpec as P

NSI = 5
EPS = 1e-6
VMEM = pl.BlockSpec(memory_space=pltpu.VMEM)
MESH = pl.DeviceIdType.MESH
SMEM = pl.BlockSpec(memory_space=pltpu.SMEM)
HBM = pl.BlockSpec(memory_space=pltpu.HBM)


def split(x):
    high = x.astype(jnp.bfloat16)
    return high, (x - high.astype(jnp.float32)).astype(jnp.bfloat16)


def dots(a, b, ca=1, cb=0):
    def one(x, y):
        return lax.dot_general(
            x, y, (((ca,), (cb,)), ((), ())), preferred_element_type=jnp.float32
        )

    return one(a[0], b[0]) + (one(a[0], b[1]) + one(a[1], b[0]))


def dot(a, b, ca=1, cb=0):
    return dots(split(a), split(b), ca, cb)


def columns(gens):
    width = gens[0].shape[0]
    row = lax.broadcasted_iota(jnp.int32, (width, width), 0)
    col = lax.broadcasted_iota(jnp.int32, (width, width), 1)
    eye = jnp.where(row == col, 1.0, 0.0).astype(jnp.float32)
    parts = [split(g) for g in gens]
    zs = [0.5 * (eye + dots(p, p, 1, 1)) for p in parts]
    qs = None
    for index in range(NSI):
        ts = [1.5 * eye - 0.5 * z for z in zs]
        tsp = [split(t) for t in ts]
        if qs is None:
            qs = [t * (0.5**0.5) for t in ts]
        else:
            qs = [dots(split(q), t) for q, t in zip(qs, tsp)]
        if index < NSI - 1:
            squares = [dots(t, t) for t in tsp]
            zs = [dot(z, s) for z, s in zip(zs, squares)]
    return [(q, dots(p, split(q), 0, 0)) for q, p in zip(qs, parts)]


def generator(cross, own, other, sign):
    width = cross.shape[0]
    row = lax.broadcasted_iota(jnp.int32, (width, width), 0)
    col = lax.broadcasted_iota(jnp.int32, (width, width), 1)
    diag = row == col
    dc = jnp.sum(jnp.where(diag, own, 0.0), axis=1, keepdims=True)
    dp = jnp.sum(jnp.where(diag, other, 0.0), axis=0, keepdims=True)
    dc = jnp.maximum(dc, 0.0) + EPS
    dp = jnp.maximum(dp, 0.0) + EPS
    cross = cross * (lax.rsqrt(dc) * lax.rsqrt(dp))
    total = jnp.sum(jnp.sum(cross * cross, axis=1, keepdims=True), axis=0, keepdims=True)
    return cross * (sign * lax.rsqrt(1.0 + total))


def rotate(nb, plan_ref, label, gram_ref, all_ref, out_ref):
    width = out_ref.shape[1]
    masks = [plan_ref[s] for s in range(3)]
    labels = []
    for slot in range(8):
        block = label
        for bit in range(3):
            if slot >> bit & 1:
                block = jnp.bitwise_xor(block, masks[bit])
        labels.append(block)

    def sign(i, j):
        return jnp.where(labels[i] < labels[j], 1.0, -1.0).astype(jnp.float32)

    loaded = {}

    def gram(i, j):
        if (i, j) not in loaded:
            loaded[i, j] = gram_ref[labels[j], labels[i]]
        return loaded[i, j]

    def stack(parts, axis):
        return jnp.concatenate(parts, axis=axis)

    outs = (0, 2, 4, 6)
    gens = [generator(gram(i, i + 1), gram(i, i), gram(i + 1, i + 1), sign(i, i + 1)) for i in outs]
    first = columns(gens)
    col = {i: split(stack(c, 0)) for i, c in zip(outs, first)}
    after = {}
    for i in outs:
        for j in outs:
            if j < i:
                continue
            wide = stack(
                [stack([gram(i + p, j), gram(i + p, j + 1)], 1) for p in (0, 1)], 0
            )
            half = dots(split(wide), col[j])
            after[i, j] = dots(col[i], split(half), 0, 0)

    gens = [generator(after[i, i + 2], after[i, i], after[i + 2, i + 2], sign(i, i + 2)) for i in (0, 4)]
    second = columns(gens)
    c0, c4 = [split(stack(c, 0)) for c in second]

    def block(i, j):
        return stack(
            [
                stack([after[i, j], after[i, j + 2]], 1),
                stack([after[i + 2, j] if i + 2 <= j else after[j, i + 2].T, after[i + 2, j + 2]], 1),
            ],
            0,
        )

    def update(ci, mat, cj):
        return dots(ci, split(dots(split(mat), cj)), 0, 0)

    g00 = update(c0, block(0, 0), c0)
    g04 = update(c0, block(0, 4), c4)
    g44 = update(c4, block(4, 4), c4)
    gens = [generator(g04, g00, g44, sign(0, 4))]
    (a, b), = columns(gens)
    top = dots(c0, split(a))
    bottom = dots(c4, split(b))
    weight = {0: top[:width], 2: top[width:], 4: bottom[:width], 6: bottom[width:]}
    coef = {}
    for i in outs:
        both = dots(col[i], split(weight[i]))
        coef[i], coef[i + 1] = both[:width], both[width:]
    coefs = [split(coef[k]) for k in range(8)]
    rows = out_ref.shape[0]
    tile = min(rows, 256)

    for at in range(0, rows, tile):
        total = jnp.zeros((tile, width), jnp.float32)
        for k in range(len(coefs)):
            total += dots(split(all_ref[labels[k], at : at + tile]), coefs[k])
        out_ref[at : at + tile, :] = total


def cat(parts, axis):
    return jnp.concatenate(parts, axis=axis)


def one(a, b, cb=0):
    return lax.dot_general(
        a, b, (((1,), (cb,)), ((), ())), preferred_element_type=jnp.float32
    )


def wide(a, b, cb=0):
    return one(cat([a[0], a[1], a[0]], 1), cat([b[0], b[0], b[1]], cb), cb)


def eyes(width):
    row = lax.broadcasted_iota(jnp.int32, (width, width), 0)
    col = lax.broadcasted_iota(jnp.int32, (width, width), 1)
    return row == col


def squares_of(turn, line):
    return jnp.sum(turn * line, axis=1, keepdims=True)


def strength(cross, sign):
    total = jnp.sum(jnp.sum(cross * cross, axis=0, keepdims=True), axis=1, keepdims=True)
    return sign * lax.rsqrt(1.0 + total)


def inverse(square):
    return lax.rsqrt(jnp.maximum(square, 0.0) + EPS)


def normal(cross, own, other, sign):
    dp = jnp.sum(jnp.where(eyes(cross.shape[0]), other, 0.0), axis=0, keepdims=True)
    cross = cross * (inverse(own) * inverse(dp))
    return cross, strength(cross, sign)


def rows_of_rotations(pairs, thin=False):
    width = pairs[0][0].shape[0]
    eye = jnp.where(eyes(width), 1.0, 0.0).astype(jnp.float32)
    parts = [split(c) for c, _ in pairs]
    squares = [wide(p, p, 1) for p in parts]
    es = [0.5 * eye - (0.5 * a * a) * s for (_, a), s in zip(pairs, squares)]
    gs = [a * c for c, a in pairs]
    ep = [split(e) for e in es]
    boths = [
        wide(p, p if thin and n % 2 else [cat([x, y], 1) for x, y in zip(p, split(g))])
        for n, (p, g) in enumerate(zip(ep, gs))
    ]
    ys = [
        (0.5**0.5)
        * (eye + 0.5 * e if thin and n % 2 else cat([eye + 0.5 * e, g + 0.5 * b[:, width:]], 1))
        for n, (e, g, b) in enumerate(zip(es, gs, boths))
    ]
    fs = [b[:, :width] for b in boths]
    es = [0.75 * f + 0.25 * wide(split(f), p) for f, p in zip(fs, ep)]
    ep = [split(e) for e in es]
    boths = [wide(p, [cat([x, z], 1) for x, z in zip(p, split(y))]) for p, y in zip(ep, ys)]
    ys = [y + 0.5 * b[:, width:] for y, b in zip(ys, boths)]
    fs = [b[:, :width] for b in boths]
    es = [0.75 * f + 0.25 * one(f.astype(jnp.bfloat16), p[0]) for f, p in zip(fs, ep)]
    ep = [split(e) for e in es]
    fs = [one(p[0], p[0]) for p in ep]
    ys = [y + 0.5 * wide(p, split(y)) for y, p in zip(ys, ep)]
    es = [0.75 * f + 0.25 * one(f.astype(jnp.bfloat16), p[0]) for f, p in zip(fs, ep)]
    eh = [e.astype(jnp.bfloat16) for e in es]
    fs = [one(h, h) for h in eh]
    ys = [y + 0.5 * one(h, y.astype(jnp.bfloat16)) for y, h in zip(ys, eh)]
    last = [
        (0.5 * (0.75 * f + 0.25 * one(f.astype(jnp.bfloat16), h))).astype(jnp.bfloat16)
        for f, h in zip(fs, eh)
    ]
    return ys, last


def finish(x, last):
    return x + one(last, x.astype(jnp.bfloat16))


def rotate4(plan_ref, label, gram_ref, down_ref, across_ref, high_ref, low_ref, out_ref):
    width = out_ref.shape[1]
    masks = [plan_ref[s] for s in range(2)]
    labels = [label, jnp.bitwise_xor(label, masks[0]), jnp.bitwise_xor(label, masks[1])]
    labels.append(jnp.bitwise_xor(labels[1], masks[1]))

    def sign(i, j):
        return jnp.where(labels[i] < labels[j], 1.0, -1.0).astype(jnp.float32)

    def grid(blocks):
        return cat([cat(line, 1) for line in blocks], 0)

    first = [[gram_ref[labels[j], labels[i]] for j in range(4)] for i in range(4)]
    pairs = []
    for i in range(4):
        scale = down_ref[labels[i]] * across_ref[labels[i ^ 1], :1]
        pairs.append(first[i][i ^ 1] * scale)
    sizes = [strength(pairs[i], sign(i, i ^ 1)) for i in (0, 2)]
    pairs = list(zip(pairs, (sizes[0], -sizes[0], sizes[1], -sizes[1])))
    ys, last = rows_of_rotations(pairs, True)
    ys = [cat([-ys[i - 1][:, width:].T, y], 1) if i % 2 else y for i, y in enumerate(ys)]
    turned = []
    lines = []
    norms = []
    for p in range(2):
        slab = split(grid([first[2 * p][2 * p :], first[2 * p + 1][2 * p :]]))
        top = wide(split(cat(ys[2 * p : 2 * p + 2], 0)), slab)
        top = cat([finish(top[:width], last[2 * p]), finish(top[width:], last[2 * p + 1])], 0)
        lines.append(split(top))
        turn = cat([finish(ys[2 * p + c], last[2 * p + c]) for c in (0, 1)], 0)
        turned.append(split(turn))
        sums = squares_of(turn, top[:, : 2 * width])
        norms += [sums[:width], sums[width:]]
    after = [[None] * 4 for _ in range(4)]
    for p in range(2):
        for q in range(p, 2):
            cut = slice(2 * (q - p) * width, 2 * (q - p + 1) * width)
            block = wide([x[:, cut] for x in lines[p]], turned[q], 1)
            for i in range(2):
                for j in range(2):
                    at = slice(i * width, (i + 1) * width), slice(j * width, (j + 1) * width)
                    after[2 * p + i][2 * q + j] = block[at]
    for i, j in ((2, 0), (2, 1), (3, 1)):
        after[i][j] = after[j][i].T
    own, far = (0, 2), (3, 1)
    pairs = [normal(after[i][j], norms[i], norms[j], sign(i, j)) for i, j in (own, far)]
    ys, last = rows_of_rotations(pairs)
    slab = split(grid([[after[i][j] for j in own + far] for i in own]))
    line0 = finish(wide(split(ys[0]), slab), last[0])
    slab = split(grid([[after[i][j] for j in far] for i in far]))
    line3 = finish(wide(split(ys[1]), slab), last[1])
    ys = [finish(y, e) for y, e in zip(ys, last)]
    c0, c3 = [split(y) for y in ys]
    g03 = wide(split(line0[:, 2 * width :]), c3, 1)
    g00 = squares_of(ys[0], line0[:, : 2 * width])
    g33 = squares_of(ys[1], line3)
    ys, last = rows_of_rotations([normal(g03, g00, g33, sign(0, 3))])

    def row(slot):
        at = slice(slot % 2 * width, (slot % 2 + 1) * width)
        return [x[at] for x in turned[slot // 2]]

    def piece(c, half, slot):
        return wide([x[:, half * width : (half + 1) * width] for x in c], row(slot))

    mixed = split(
        grid([[piece(c0, 0, 0), piece(c0, 1, 2)], [piece(c3, 1, 1), piece(c3, 0, 3)]])
    )
    coef = split(finish(wide(split(ys[0]), mixed), last[0]))
    rows = out_ref.shape[0]
    tile = min(rows, 512)
    for at in range(0, rows, tile):
        line = [
            cat([ref[labels[k], at : at + tile] for k in range(4)], 1) for ref in (high_ref, low_ref)
        ]
        both = one(line[0], cat(coef, 0), 1)
        out_ref[at : at + tile, :] = both[:, :width] + (both[:, width:] + one(line[1], coef[0], 1))


def kernel(nb, nr, plan_ref, own_ref, out_ref, all_ref, gram_ref, part, land, *sems):
    a_send, a_recv, b_send, b_recv, c_send, c_recv, d_send, d_recv = sems
    me, row = lax.axis_index("cols"), lax.axis_index("rows")
    chips = nb // 2
    chip, core = me // 2, lax.rem(me, 2)
    sibling = chip * 2 + (1 - core)
    rows, width = own_ref.shape
    piece = 2 * width // nr
    far = range(1, chips)
    chunks = a_send.shape[2]
    size = rows // chunks

    def ahead(d):
        return lax.rem(chip + d, chips)

    def behind(d):
        return lax.rem(chip + 2 * chips - d, chips)

    def peer(k):
        return lax.rem(row + k, nr)

    barrier = pltpu.get_barrier_semaphore()
    targets = [{"cols": sibling}] + [{"cols": ahead(d) * 2 + core} for d in far]
    targets += [{"rows": peer(k)} for k in range(1, nr)]
    for target in targets:
        pl.semaphore_signal(barrier, inc=1, device_id=target, device_id_type=MESH)
    pl.semaphore_wait(barrier, len(targets))

    started = []

    def start(copy):
        copy.start()
        started.append(copy)

    def copies(ref, source, send, recv, at):
        def direct(d, n):
            return pltpu.make_async_remote_copy(
                source.at[at(0, n)], ref.at[me, at(0, n)], send.at[d, 0, n], recv.at[d, 0, n],
                device_id={"cols": ahead(d) * 2 + core}, device_id_type=MESH,
            )

        def relay(d, n):
            block = behind(d) * 2 + core
            return pltpu.make_async_remote_copy(
                source.at[at(0, n)] if d == 0 else ref.at[block, at(d, n)], ref.at[block, at(d, n)],
                send.at[d, 1, n], recv.at[d, 1, n],
                device_id={"cols": sibling}, device_id_type=MESH,
            )

        return direct, relay

    def group(d, n):
        return pl.ds(behind(d + n) * 2, 2)

    direct, relay = copies(all_ref, own_ref, a_send, a_recv, lambda d, n: pl.ds(n * size, size))
    far_panel, near_panel = copies(gram_ref, gram_ref.at[me], d_send, d_recv, group)

    def multiply(block, ch):
        at = pl.ds(ch * size, size)
        to = pl.ds(pl.multiple_of(block * width, width), width)
        product = dot(all_ref[block, at, :], own_ref[at, :], 0, 0)
        if ch == 0:
            part[to, :] = product
        else:
            part[to, :] += product

    def rows_of(g, r):
        return pl.ds(pl.multiple_of(behind(g) * (2 * width) + r * piece, piece), piece)

    def place(g):
        half = nr // 2
        at = pl.ds(pl.multiple_of(lax.rem(row, half) * piece, piece), piece)
        return gram_ref.at[me, behind(g) * 2 + row // half, at]

    def scatter(g, k):
        return pltpu.make_async_remote_copy(
            part.at[rows_of(g, peer(k))], land.at[g, k - 1],
            b_send.at[g, k - 1], b_recv.at[g, k - 1],
            device_id={"rows": peer(k)}, device_id_type=MESH,
        )

    def spread(g, k):
        return pltpu.make_async_remote_copy(
            place(g), place(g),
            c_send.at[g, k - 1], c_recv.at[g, k - 1],
            device_id={"rows": peer(k)}, device_id_type=MESH,
        )

    def send_group(g):
        for k in range(1, nr):
            start(scatter(g, k))

    def sum_group(g):
        total = part[rows_of(g, row), :]
        for k in range(1, nr):
            scatter(g, k).wait_recv()
            total += land[g, k - 1]
        place(g)[...] = total
        for k in range(1, nr):
            start(spread(g, k))

    def share_group(g):
        for k in range(1, nr):
            spread(g, k).wait_recv()
        for d in far:
            start(far_panel(d, g))
        start(near_panel(0, g))

    for ch in range(chunks):
        for d in far:
            start(direct(d, ch))
    for ch in range(chunks):
        start(relay(0, ch))
    all_ref[me] = own_ref[...]
    for ch in range(chunks):
        multiply(me, ch)
    for ch in range(chunks):
        relay(0, ch).wait_recv()
        multiply(sibling, ch)
    send_group(0)
    for ch in range(chunks + 1):
        for d in far:
            if ch < chunks:
                direct(d, ch).wait_recv()
                start(relay(d, ch))
                multiply(behind(d) * 2 + core, ch)
            if ch > 0:
                relay(d, ch - 1).wait_recv()
                multiply(behind(d) * 2 + 1 - core, ch - 1)
        if ch == chunks - 2:
            sum_group(0)
    for g in far:
        send_group(g)
    share_group(0)
    for g in far:
        sum_group(g)
    for g in far:
        share_group(g)
    for g in range(chips):
        for d in far:
            far_panel(d, g).wait_recv()
            start(near_panel(d, g))
    for g in range(chips):
        for d in range(chips):
            near_panel(d, g).wait_recv()
    rotate(nb, plan_ref, me, gram_ref, all_ref, out_ref)
    for copy in started:
        copy.wait_send()


CHUNKS = 4
LATE = 1


def tall(a, b):
    return lax.dot_general(
        cat([a[0], a[1], a[0]], 0), cat([b[0], b[0], b[1]], 0),
        (((0,), (0,)), ((), ())), preferred_element_type=jnp.float32,
    )


def kernel4(
    nr, plan_ref, own_ref, out_ref, all_ref, gram_ref, flat, cross, stage, early, near, land, high_ref, low_ref,
    down_ref, across_ref,
    masks_ref, local_sem, hop, *sems
):
    (swap_send, swap_recv, pair_send, pair_recv, relay_send, relay_recv, b_send, b_recv,
     c_send, c_recv, d_send, d_recv, g_send, g_recv, e_send, e_recv, f_send, f_recv) = sems
    me, row = lax.axis_index("cols"), lax.axis_index("rows")
    chip, core = me // 2, lax.rem(me, 2)
    sibling = chip * 2 + 1 - core
    far = (1 - chip) * 2 + core
    away = (1 - chip) * 2 + 1 - core
    rows, width = own_ref.shape
    half = rows // 2
    owners = nr // 2
    thick = width // nr
    owner = jnp.logical_and(row >= nr // 4, row < nr // 4 + owners)

    def peer(k):
        return lax.rem(row + k, nr)

    def there(d):
        return chip if d == 0 else 1 - chip

    def remote(source, target, send, recv, **device):
        return pltpu.make_async_remote_copy(
            source, target, send, recv, device_id=device, device_id_type=MESH
        )

    bits = [1 << n for n in range(nr.bit_length() - 1)]
    ways = [{"rows": jnp.bitwise_xor(row, bit)} for bit in bits[:-1]]
    ways += [{"cols": sibling}, {"cols": far}]
    first = ways + [{"rows": jnp.bitwise_xor(row, bits[-1])}]
    barrier = pltpu.get_barrier_semaphore()
    plan_copy = pltpu.make_async_copy(plan_ref, masks_ref, local_sem.at[0])
    plan_copy.start()
    own_copy = pltpu.make_async_copy(own_ref, all_ref.at[me], local_sem.at[1])
    own_copy.start()
    for way in first:
        pl.semaphore_signal(barrier, inc=1, device_id=way, device_id_type=MESH)
    own_copy.wait()
    pl.semaphore_wait(barrier, len(first))

    def tell(n):
        pl.semaphore_signal(hop.at[n], inc=1, device_id=ways[n], device_id_type=MESH)

    def hear(n):
        pl.semaphore_wait(hop.at[n], 1)

    started = []

    def start(copy):
        copy.start()
        started.append(copy)

    sizes = [half // CHUNKS] * CHUNKS + [half // LATE] * LATE
    offsets = [n * (half // CHUNKS) for n in range(CHUNKS)] + [n * (half // LATE) for n in range(LATE)]

    def span(side, n):
        at = side * half + offsets[n]
        return pl.ds(pl.multiple_of(at, 8), sizes[n])

    def swap(n):
        at = span(1 - chip if n < CHUNKS else chip, n)
        return remote(
            all_ref.at[me, at], all_ref.at[me, at], swap_send.at[n], swap_recv.at[n], cols=far
        )

    def relay(n):
        at = span(chip if n < CHUNKS else 1 - chip, n)
        return remote(
            all_ref.at[far, at], all_ref.at[far, at], relay_send.at[n], relay_recv.at[n],
            cols=sibling,
        )

    def pair(n):
        at = pl.ds(n * half, half)
        return remote(
            all_ref.at[me, at], all_ref.at[me, at], pair_send.at[n], pair_recv.at[n], cols=sibling
        )

    def scatter(o):
        return remote(
            stage.at[target(o) - nr // 4], early.at[row], b_send.at[o], b_recv.at[row],
            rows=target(o),
        )

    def scatter_all(act):
        for o in range(owners):

            @pl.when(target(o) != row)
            def _():
                act(scatter(o))

    def arrive_early(r):
        return remote(stage.at[0], early.at[r], b_send.at[0], b_recv.at[r], cols=sibling)

    def spread(k):
        at = near.at[me, row - nr // 4]
        return remote(at, at, c_send.at[k - 1], c_recv.at[row - nr // 4], rows=peer(k))

    def arrive_near(o):
        at = near.at[me, o]
        return remote(at, at, c_send.at[0], c_recv.at[o], cols=sibling)

    def forward(o):
        at = near.at[me, o]
        return remote(at, at, g_send.at[o], g_recv.at[o], cols=far)

    def share(n):
        at = near.at[me if n == 0 else far]
        return remote(at, at, d_send.at[n], d_recv.at[n], cols=sibling)

    def target(o):
        upper = (row < nr // 2) == (o < owners // 2)
        return jnp.where(upper, nr // 2, nr // 4) + lax.rem(o + row, owners // 2)

    def piece(x, r):
        index = x * owners + r - nr // 4
        return pl.ds(pl.multiple_of(index * thick, thick), thick)

    def side(b):
        return jnp.where(chip == 0, core, b)

    def slot(b):
        return jnp.where(chip == 0, b, core)

    def scatter_cross(b, d, o):
        return remote(
            cross.at[b, piece(there(d), target(o))], land.at[slot(b), chip, row],
            e_send.at[b, d, o], e_recv.at[slot(b), chip, row],
            cols=there(d) * 2 + side(b), rows=target(o),
        )

    def scatter_near(act):
        for o in range(owners):
            for b in range(2):
                same = jnp.logical_and(side(b) == core, target(o) == row)

                @pl.when(jnp.logical_not(same))
                def _():
                    act(scatter_cross(b, 0, o))

    def arrive_cross(i, x, r):
        return remote(
            cross.at[i, pl.ds(0, thick)], land.at[i, x, r],
            e_send.at[i, 0, 0], e_recv.at[i, x, r], cols=sibling,
        )

    def spread_cross(d, k):
        at = gram_ref.at[2 + core, pl.ds(0, 2), piece(chip, row)]
        return remote(
            at, at, f_send.at[d, k], f_recv.at[chip, row - nr // 4],
            cols=there(d) * 2 + core, rows=peer(k),
        )

    def arrive_spread(x, o):
        at = gram_ref.at[2 + core, pl.ds(0, 2), piece(x, nr // 4 + o)]
        return remote(at, at, f_send.at[0, 0], f_recv.at[x, o], cols=sibling)

    def pass_cross(x):
        at = gram_ref.at[2 + core, pl.ds(0, 2), pl.ds(x * (width // 2), width // 2)]
        return remote(at, at, d_send.at[2 + x], d_recv.at[2 + x], cols=sibling)

    tell(0)
    for n in range(CHUNKS):
        start(swap(n))
    for n in range(2):
        start(pair(n))

    step = rows // 4
    total = None
    for n in range(4):
        x = split(all_ref[me, pl.ds(n * step, step)])
        product = tall(x, x)
        total = product if total is None else total + product
    flat[0] = total
    inner = len(bits) - 1
    for n in range(inner):
        hear(n)
        tell(n + 1)
    total = None
    for n in range(4):
        if n % 2 == 0:
            pair(n // 2).wait_recv()
        at = pl.ds(n * step, step)
        product = tall(split(all_ref[chip * 2, at]), split(all_ref[chip * 2 + 1, at]))
        total = product if total is None else total + product
    flat[1] = total
    for o in range(owners):
        stage[o, : 2 * thick] = flat[0, 2 * thick * o : 2 * thick * (o + 1)]
        at = pl.multiple_of(core * (width // 2) + o * thick, thick)
        stage[o, 2 * thick :] = flat[1, pl.ds(at, thick)]
    scatter_all(lambda copy: copy.start())
    hear(inner)
    tell(inner + 1)
    hear(inner + 1)

    totals = [None, None]

    def keep(block, at):
        high_ref[block, at], low_ref[block, at] = split(all_ref[block, at])

    for n in range(CHUNKS):
        swap(n).wait_recv()
        at = span(chip, n)
        for b in range(2):
            left = all_ref[jnp.where(chip == 0, b, far), at]
            right = all_ref[jnp.where(chip == 0, far, 2 + b), at]
            product = tall(split(left), split(right))
            totals[b] = product if n == 0 else totals[b] + product
    for b in range(2):
        cross[b] = totals[b]
    for o in range(owners):
        for b in range(2):
            start(scatter_cross(b, 1, o))
    scatter_near(lambda copy: copy.start())
    for n in range(CHUNKS, CHUNKS + LATE):
        start(swap(n))

    order = sorted(range(nr), key=lambda k: abs(2 * k - nr - 1))

    @pl.when(owner)
    def _():
        early[row] = stage[row - nr // 4]
        for r in range(nr):

            @pl.when(row != r)
            def _():
                arrive_early(r).wait_recv()

        near[me, row - nr // 4] = sum((early[r] for r in range(1, nr)), early[0])
        for k in order:
            if k:
                spread(k).start()

    for n in range(CHUNKS):
        start(relay(n))
    for block in (me, sibling):
        keep(block, pl.ds(0, rows))
    for n in range(CHUNKS):
        keep(far, span(chip, n))

    @pl.when(owner)
    def _():
        for b in range(2):

            @pl.when(side(b) == core)
            def _():
                land[slot(b), chip, row] = cross[b, piece(chip, row)]

        for i in range(2):
            sums = None
            for x in range(2):
                for r in range(nr):
                    same = jnp.logical_and(row == r, chip == x)
                    if x == 1:
                        same = jnp.logical_and(same, core == i)

                    @pl.when(jnp.logical_not(same))
                    def _():
                        arrive_cross(i, x, r).wait_recv()

            for x in range(2):
                for r in range(nr):
                    sums = land[i, x, r] if sums is None else sums + land[i, x, r]
            gram_ref[2 + core, i, piece(chip, row)] = sums
        for d in (1, 0):
            for k in order:
                if d or k:
                    spread_cross(d, k).start()

    for o in range(owners):

        @pl.when(row != nr // 4 + o)
        def _():
            arrive_near(o).wait_recv()

        start(forward(o))
    start(share(0))

    for n in range(CHUNKS, CHUNKS + LATE):
        swap(n).wait_recv()
        start(relay(n))
    for o in range(owners):
        forward(o).wait_recv()
    for copy in started:
        copy.wait_send()
    scatter_near(lambda copy: copy.wait_send())
    scatter_all(lambda copy: copy.wait_send())

    @pl.when(owner)
    def _():
        for k in range(1, nr):
            spread(k).wait_send()

    plan_copy.wait()
    share(1).start()
    for n in range(CHUNKS, CHUNKS + LATE):
        keep(far, span(1 - chip, n))
    for n in range(CHUNKS + LATE):
        relay(n).wait_recv()
        keep(away, span(chip if n < CHUNKS else 1 - chip, n))
    for d in range(2):
        for o in range(owners):
            if d == 0:

                @pl.when(row != nr // 4 + o)
                def _():
                    arrive_spread(chip, o).wait_recv()

            else:
                arrive_spread(1 - chip, o).wait_recv()
        pass_cross(there(d)).start()
    @pl.when(owner)
    def _():
        for k in range(nr):
            for d in range(2):
                if d or k:
                    spread_cross(d, k).wait_send()

    for n in range(2):
        share(n).wait_recv()
    share(1).wait_send()
    for block in range(4):
        square = near[block, :, : 2 * thick].reshape(width, width)
        gram_ref[block, block] = square
        square = jnp.where(eyes(width), square, 0.0)
        down = inverse(jnp.sum(square, axis=1, keepdims=True))
        down_ref[block] = jnp.broadcast_to(down, (width, width))
        across = inverse(jnp.sum(square, axis=0, keepdims=True))
        across_ref[block] = jnp.broadcast_to(across, (8, width))
    for c in range(2):
        both = [near[2 * c + i, :, 2 * thick :].reshape(width // 2, width) for i in range(2)]
        both = cat(both, 0)
        gram_ref[2 * c + 1, 2 * c] = both
        gram_ref[2 * c, 2 * c + 1] = both.T

    for i in range(2):
        gram_ref[i, 2 + core] = gram_ref[2 + core, i].T
    for x in range(2):
        pass_cross(x).wait_recv()
    for i in range(2):
        gram_ref[i, 3 - core] = gram_ref[3 - core, i].T

    rotate4(masks_ref, me, gram_ref, down_ref, across_ref, high_ref, low_ref, out_ref)
    for x in range(2):
        pass_cross(x).wait_send()


def local4(nr, snapshots, plan):
    rows, width = snapshots.shape
    owners, thick = nr // 2, width // nr
    dma = pltpu.SemaphoreType.DMA
    return pl.pallas_call(
        functools.partial(kernel4, nr),
        out_shape=jax.ShapeDtypeStruct((rows, width), jnp.float32),
        in_specs=[HBM, HBM],
        out_specs=VMEM,
        scratch_shapes=[
            pltpu.VMEM((4, rows, width), jnp.float32),
            pltpu.VMEM((4, 4, width, width), jnp.float32),
            pltpu.VMEM((2, width, width), jnp.float32),
            pltpu.VMEM((2, width, width), jnp.float32),
            pltpu.VMEM((owners, 3 * thick, width), jnp.float32),
            pltpu.VMEM((nr, 3 * thick, width), jnp.float32),
            pltpu.VMEM((4, owners, 3 * thick, width), jnp.float32),
            pltpu.VMEM((2, 2, nr, thick, width), jnp.float32),
            pltpu.VMEM((4, rows, width), jnp.bfloat16), pltpu.VMEM((4, rows, width), jnp.bfloat16),
            pltpu.VMEM((4, width, width), jnp.float32), pltpu.VMEM((4, 8, width), jnp.float32),
            pltpu.SMEM(plan.shape, jnp.int32), dma((2,)),
            pltpu.SemaphoreType.REGULAR((nr.bit_length(),)),
            dma((CHUNKS + LATE,)), dma((CHUNKS + LATE,)),
            dma((2,)), dma((2,)),
            dma((CHUNKS + LATE,)), dma((CHUNKS + LATE,)),
            dma((owners,)), dma((nr,)),
            dma((nr - 1,)), dma((owners,)),
            dma((4,)), dma((4,)), dma((owners,)), dma((owners,)),
            dma((2, 2, nr // 2)), dma((2, 2, nr)),
            dma((2, nr)), dma((2, nr // 2)),
        ],
        compiler_params=pltpu.CompilerParams(
            collective_id=0, has_side_effects=True, vmem_limit_bytes=53 * 2**20
        ),
    )(plan, snapshots)


def local(nb, nr, snapshots, plan):
    rows, width = snapshots.shape
    chips = nb // 2
    dma = pltpu.SemaphoreType.DMA
    return pl.pallas_call(
        functools.partial(kernel, nb, nr),
        out_shape=jax.ShapeDtypeStruct((rows, width), jnp.float32),
        in_specs=[SMEM, VMEM],
        out_specs=VMEM,
        scratch_shapes=[
            pltpu.VMEM((nb, rows, width), jnp.float32),
            pltpu.VMEM((nb, nb, width, width), jnp.float32),
            pltpu.VMEM((nb * width, width), jnp.float32),
            pltpu.VMEM((chips, nr - 1, 2 * width // nr, width), jnp.float32),
            dma((chips, 2, 4)), dma((chips, 2, 4)),
            dma((chips, nr - 1)), dma((chips, nr - 1)),
            dma((chips, nr - 1)), dma((chips, nr - 1)),
            dma((chips, 2, chips)), dma((chips, 2, chips)),
        ],
        compiler_params=pltpu.CompilerParams(
            collective_id=0, has_side_effects=True, vmem_limit_bytes=48 * 2**20
        ),
    )(plan, snapshots)


def solution(mesh):
    nb, nr = mesh.shape["cols"], mesh.shape["rows"]
    four = nb == 4 and nr >= 4 and nr & (nr - 1) == 0
    body = functools.partial(local4, nr) if four else functools.partial(local, nb, nr)
    return jax.shard_map(
        body,
        mesh=mesh,
        in_specs=(P("rows", "cols"), P()),
        out_specs=P("rows", "cols"),
        check_vma=False,
    )
```
